32 devices in a mesh: dp: 8 (over y, x, core), seq: 4 (over z).
Axes of the slice: x: 2, y: 2, z: 4, core: 2. Of those that a mesh axis runs over, the one named last changes fastest.
Arguments:
- inputs: bfloat16 [16384, 1024], P(('dp', 'seq')), may hold values from -6 to 6
- cotangent: bfloat16 [16384, 1024], P(('dp', 'seq')), may hold values from -6 to 6
- target_slot: int32 [16384], P(('dp', 'seq')), may hold values from 0 to 767, as said below
- anchor_slot: int32 [16384], P(('dp', 'seq')), may hold values from 0 to 767, as said below
- sequence_start: int32 [16384], P(('dp', 'seq')), may hold values from 0 to 2047, as said below
- attention_in: float32 [1024, 3072], P(('dp', 'seq')), may hold values from -0.09375 to 0.09375
- attention_out: float32 [1024, 1024], P(('dp', 'seq')), may hold values from -1.5 to 1.5
- gate_up: float32 [1024, 5632], P(('dp', 'seq')), may hold values from -0.09375 to 0.09375
- feed_down: float32 [2816, 1024], P(('dp', 'seq')), may hold values from -0.109375 to 0.109375
- norm_gains: float32 [2, 1024], P(None, ('dp', 'seq')), may hold values from 0.5 to 8
- first_in: float32 [1024, 3072], P(('dp', 'seq')), may hold values from -0.00048828125 to 0.00048828125
- first_out: float32 [1024, 1024], P(('dp', 'seq')), may hold values from -4.5776367e-05 to 4.5776367e-05
- first_gate: float32 [1024, 5632], P(('dp', 'seq')), may hold values from -0.00048828125 to 0.00048828125
- first_down: float32 [2816, 1024], P(('dp', 'seq')), may hold values from -0.00048828125 to 0.00048828125
- first_gains: float32 [2, 1024], P(None, ('dp', 'seq')), may hold values from -0.00048828125 to 0.00048828125
- second_in: float32 [1024, 3072], P(('dp', 'seq')), may hold values from 4.094308e-09 to 1.6346096e-08
- second_out: float32 [1024, 1024], P(('dp', 'seq')), may hold values from 4.094308e-11 to 1.6346097e-10
- second_gate: float32 [1024, 5632], P(('dp', 'seq')), may hold values from 4.094308e-09 to 1.6346096e-08
- second_down: float32 [2816, 1024], P(('dp', 'seq')), may hold values from 4.094308e-09 to 1.6346096e-08
- second_gains: float32 [2, 1024], P(None, ('dp', 'seq')), may hold values from 4.094308e-09 to 1.6346096e-08
Outputs:
- outputs: bfloat16 [16384, 1024], P(('dp', 'seq'))
- input_gradient: bfloat16 [16384, 1024], P(('dp', 'seq'))
- gradient_norm: float32 [], replicated
- updated_first_in: float32 [1024, 3072], P(('dp', 'seq'))
- updated_second_in: float32 [1024, 3072], P(('dp', 'seq'))
- updated_attention_in: float32 [1024, 3072], P(('dp', 'seq'))
- updated_first_out: float32 [1024, 1024], P(('dp', 'seq'))
- updated_second_out: float32 [1024, 1024], P(('dp', 'seq'))
- updated_attention_out: float32 [1024, 1024], P(('dp', 'seq'))
- updated_first_gate: float32 [1024, 5632], P(('dp', 'seq'))
- updated_second_gate: float32 [1024, 5632], P(('dp', 'seq'))
- updated_gate_up: float32 [1024, 5632], P(('dp', 'seq'))
- updated_first_down: float32 [2816, 1024], P(('dp', 'seq'))
- updated_second_down: float32 [2816, 1024], P(('dp', 'seq'))
- updated_feed_down: float32 [2816, 1024], P(('dp', 'seq'))
- updated_first_gains: float32 [2, 1024], P(None, ('dp', 'seq'))
- updated_second_gains: float32 [2, 1024], P(None, ('dp', 'seq'))
- updated_norm_gains: float32 [2, 1024], P(None, ('dp', 'seq'))
The draws below stay inside these ranges and needn't reach their ends.
Inputs may be any that keep to these rules, and one draw needn't show every extreme that they name: `target_slot`: A device at seq index s sends its 512 rows to the owners of seq index s: value g * 96 + q is slot q of its block for dp index g. Values on one device are distinct and the used slots of a block are its first ones. Every owner receives 512 rows in all, and in every draw some device fills all 96 slots of some block. `anchor_slot`: value j * 96 + q: the row arrives from the device at dp index j of the same seq index, from slot q of its block for this owner; it matches target_slot, and each value stands once on a device. `sequence_start`: rows of one dp index form a group of 2048 rows in seq order; the value is the group position of the first row of the row's sequence, never above the row's own position and never falling within a group. A group holds three runs: a leading and a trailing one of 1 to 511 rows each (parts of sequences cut at the group's ends), and between them one whole sequence that begins on the first device of seq and ends on the last.
All inputs are finite; a program needn't handle non-finite values.
Results may differ from the reference program's by a relative error of at most 0.02.
Values may be sent and summed in bfloat16 or wider, within the bound.
No kernel may reach another device: no remote copies, remote signals or barrier semaphores. Data moves between devices by JAX's collectives and lax.ppermute only.
A program may use at most 256 MiB of HBM per device.

```python
import math
import jax
import jax.numpy as jnp
from jax import lax

D = 1024
HEAD = 64
FF = 2816
TOK_DEV = 512
BLOCK = 512
STEP = 10
OWNERS = 8
SPANS = 4
CAP = 96
GROUP = 2048
TOKENS = 16384
PARAMS = 12847104


def shuffle_rows(key, count, rows):

    def single_order(single):
        return jax.random.permutation(single, rows)
    return jax.vmap(single_order)(jax.random.split(key, count))


def spread_rows(counts, rows, capacity):
    running = jnp.cumsum(counts, axis=1)
    before = running - counts
    position = jnp.arange(rows, dtype=jnp.int32)
    partner = jnp.sum((running[:, None, :] <= position[None, :, None]).astype(jnp.int32), axis=2)
    offset = position[None, :] - jnp.take_along_axis(before, partner, axis=1)
    return partner * capacity + offset


def place_rows(values, orders):
    count = values.shape[0]
    return jnp.zeros_like(values).at[jnp.arange(count)[:, None], orders].set(values)


def routing_tables(key):
    owners = OWNERS
    rows = TOK_DEV
    per_owner = rows // owners
    margin = per_owner // 2
    capacity = per_owner + margin

    def span_tables(span_key):
        split_keys = jax.random.split(span_key, 4)
        order = jax.random.permutation(split_keys[0], owners)
        place = jnp.zeros((owners,), jnp.int32).at[order].set(jnp.arange(owners, dtype=jnp.int32))
        shifts = jax.random.randint(split_keys[1], (owners // 2, owners // 2), 0, margin + 1)
        shifts = shifts.at[0, 0].set(margin)
        pair_row = place[:, None] // 2
        pair_col = place[None, :] // 2
        parity = jnp.where(place[:, None] % 2 == place[None, :] % 2, 1, -1)
        counts = per_owner + parity * shifts[pair_row, pair_col]
        senders = place_rows(spread_rows(counts, rows, capacity), shuffle_rows(split_keys[2], owners, rows))
        receivers = place_rows(spread_rows(jnp.transpose(counts), rows, capacity), shuffle_rows(split_keys[3], owners, rows))
        return (senders, receivers)
    senders, receivers = jax.vmap(span_tables)(jax.random.split(key, SPANS))
    target = jnp.transpose(senders, (1, 0, 2)).reshape(-1).astype(jnp.int32)
    anchor = jnp.transpose(receivers, (1, 0, 2)).reshape(-1).astype(jnp.int32)
    return (target, anchor)


def draw_target_slot(key, part):
    return routing_tables(key)[0]


def draw_anchor_slot(key, part):
    return routing_tables(key)[1]


def draw_sequence_start(key, part):
    key = jax.random.fold_in(key, 7)
    first_key, second_key = jax.random.split(key)
    group = TOK_DEV * SPANS
    leading = jax.random.randint(first_key, (OWNERS,), 1, TOK_DEV)
    trailing = jax.random.randint(second_key, (OWNERS,), 1, TOK_DEV)
    position = jnp.arange(group, dtype=jnp.int32)[None, :]
    last_start = group - trailing[:, None]
    starts = jnp.where(position < leading[:, None], 0, jnp.where(position < last_start, leading[:, None], last_start))
    return starts.reshape(-1).astype(jnp.int32)


def draw_norm_gains(key, part):
    key = jax.random.fold_in(key, 11)
    rising = 2.0
    column = jnp.arange(D, dtype=jnp.int32)
    device = column // (D // (OWNERS * SPANS))
    owner_part = (device // SPANS).astype(jnp.float32) / (OWNERS - 1)
    span_part = (device % SPANS).astype(jnp.float32) / (SPANS - 1)
    base = jnp.sqrt((1.0 + rising * owner_part) * (1.0 + rising * span_part))
    noise = jax.random.uniform(key, (2, D), jnp.float32, 0.8, 1.2)
    return (base[None, :] * noise).astype(jnp.float32)


def steps_of(stream_key, shape, cuts, low, largest):
    factor_of, own = 1.0, jax.random.fold_in(stream_key, 6)
    for dim, shards_of in cuts:
        heights = jnp.exp(jax.random.uniform(jax.random.fold_in(own, dim), (shards_of,), jnp.float32, low / len(cuts), largest / len(cuts)))
        factor_of = factor_of * jnp.repeat(heights, shape[dim] // shards_of).reshape([-1 if axis == dim else 1 for axis in range(len(shape))])
    return factor_of


def gaussian(stream_key, extent, scale, reach, shards=(), kind=jnp.bfloat16):
    values = scale * jax.random.normal(stream_key, extent, jnp.float32)
    if shards:
        values = values * steps_of(stream_key, extent, shards, -0.22, 0.18)
    return jnp.clip(values, -reach, reach).astype(kind)


def setup_inputs(seed: int = 0) -> dict:
    arg_keys = jax.random.split(jax.random.key(seed), 21)
    return {
        "inputs": gaussian(arg_keys[0], (TOKENS, D), 1.0, 6.0, ((0, 32),)),
        "cotangent": gaussian(arg_keys[1], (TOKENS, D), 1.0, 6.0, ((0, 32),)),
        "target_slot": draw_target_slot(jax.random.fold_in(arg_keys[20], 71), 0),
        "anchor_slot": draw_anchor_slot(jax.random.fold_in(arg_keys[20], 71), 0),
        "sequence_start": draw_sequence_start(jax.random.fold_in(arg_keys[20], 71), 0),
        "attention_in": gaussian(arg_keys[5], (D, 3 * D), (4 * D) ** -0.5, 0.09375, ((0, 32),), jnp.float32),
        "attention_out": gaussian(arg_keys[6], (D, D), 16 ** -0.5, 1.5, ((0, 32),), jnp.float32),
        "gate_up": gaussian(arg_keys[7], (D, 2 * FF), (4 * D) ** -0.5, 0.09375, ((0, 32),), jnp.float32),
        "feed_down": gaussian(arg_keys[8], (FF, D), FF ** -0.5, 0.109375, ((0, 32),), jnp.float32),
        "norm_gains": draw_norm_gains(jax.random.fold_in(arg_keys[20], 71), 0),
        "first_in": gaussian(arg_keys[10], (D, 3 * D), (0.111 / PARAMS ** 0.5), 0.00048828125, ((0, 32),), jnp.float32),
        "first_out": gaussian(arg_keys[11], (D, D), (0.0111 / PARAMS ** 0.5), 4.57763671875e-05, ((0, 32),), jnp.float32),
        "first_gate": gaussian(arg_keys[12], (D, 2 * FF), (0.111 / PARAMS ** 0.5), 0.00048828125, ((0, 32),), jnp.float32),
        "first_down": gaussian(arg_keys[13], (FF, D), (0.111 / PARAMS ** 0.5), 0.00048828125, ((0, 32),), jnp.float32),
        "first_gains": gaussian(arg_keys[14], (2, D), (0.111 / PARAMS ** 0.5), 0.00048828125, ((1, 32),), jnp.float32),
        "second_in": jnp.clip(jnp.exp(math.log(1.6346096032293644e-08) - 1.3843914 * jax.random.uniform(arg_keys[15], (D, 3 * D), jnp.float32) ** steps_of(arg_keys[15], (D, 3 * D), ((0, 32),), -0.2, 0.2)), 4.094308003743663e-09, 1.6346096032293644e-08),
        "second_out": jnp.clip(jnp.exp(math.log(1.634609669842746e-10) - 1.3843914 * jax.random.uniform(arg_keys[16], (D, D), jnp.float32) ** steps_of(arg_keys[16], (D, D), ((0, 32),), -0.2, 0.2)), 4.094307878843573e-11, 1.634609669842746e-10),
        "second_gate": jnp.clip(jnp.exp(math.log(1.6346096032293644e-08) - 1.3843914 * jax.random.uniform(arg_keys[17], (D, 2 * FF), jnp.float32) ** steps_of(arg_keys[17], (D, 2 * FF), ((0, 32),), -0.2, 0.2)), 4.094308003743663e-09, 1.6346096032293644e-08),
        "second_down": jnp.clip(jnp.exp(math.log(1.6346096032293644e-08) - 1.3843914 * jax.random.uniform(arg_keys[18], (FF, D), jnp.float32) ** steps_of(arg_keys[18], (FF, D), ((0, 32),), -0.2, 0.2)), 4.094308003743663e-09, 1.6346096032293644e-08),
        "second_gains": jnp.clip(jnp.exp(math.log(1.6346096032293644e-08) - 1.3843914 * jax.random.uniform(arg_keys[19], (2, D), jnp.float32) ** steps_of(arg_keys[19], (2, D), ((1, 32),), -0.2, 0.2)), 4.094308003743663e-09, 1.6346096032293644e-08),
    }


HIGHEST = lax.Precision.HIGHEST
EPSILON = 1e-05
THETA = 500000.0
NEGATIVE = -1e+30
BETA_FIRST = 0.9
BETA_SECOND = 0.95
ADAM_EPSILON = 1e-08
DECAY = 0.1
CLIP = 1.0

@jax.custom_vjp
def low(v):
    return lax.optimization_barrier(v.astype(jnp.bfloat16)).astype(jnp.float32)

@jax.custom_vjp
def low_back(v):
    return v

def low_keep(v):
    return (low(v), None)

def low_pass(kept, grad):
    return (grad,)

def back_keep(v):
    return (v, None)

def back_low(kept, grad):
    return (low(grad),)
low.defvjp(low_keep, low_pass)
low_back.defvjp(back_keep, back_low)

def norm_rows(values, gain_row):
    inverse = lax.rsqrt(lax.optimization_barrier(jnp.mean(values * values, axis=1, keepdims=True)) + EPSILON)
    return values * inverse * gain_row[None, :]

def rope_tables(positions):
    half_size = HEAD // 2
    frequency = jnp.power(THETA, -2.0 * jnp.arange(half_size, dtype=jnp.float32) / HEAD)
    angles = positions[:, None] * frequency[None, :]
    cosine_table = jnp.cos(angles)
    sine_table = jnp.sin(angles)
    return (jnp.concatenate([cosine_table, cosine_table], axis=1), jnp.concatenate([-sine_table, sine_table], axis=1))

def rotate(values, cosine_table, sine_table):
    half_size = values.shape[-1] // 2
    swapped = jnp.concatenate([values[..., half_size:], values[..., :half_size]], axis=-1)
    return values * cosine_table[:, None, :] + swapped * sine_table[:, None, :]

def attend_group(parts):
    queries, key_rows, value_rows, starts = parts
    key_index = jnp.arange(GROUP, dtype=jnp.int32)

    def score_block(block_index):
        offset = block_index * BLOCK
        query_block = lax.dynamic_slice_in_dim(queries, offset, BLOCK, 0)
        start_block = lax.dynamic_slice_in_dim(starts, offset, BLOCK, 0)
        query_index = offset + jnp.arange(BLOCK, dtype=jnp.int32)
        scores = low_back(0.125 * jnp.einsum('qhd,khd->hqk', query_block, key_rows, precision=HIGHEST))
        visible = (key_index[None, :] <= query_index[:, None]) & (key_index[None, :] >= start_block[:, None])
        scores = jnp.where(visible[None], scores, NEGATIVE)
        shifted = jnp.exp(scores - lax.optimization_barrier(jnp.max(scores, axis=2, keepdims=True)))
        shares = shifted / lax.optimization_barrier(jnp.sum(shifted, axis=2, keepdims=True))
        return jnp.einsum('hqk,khd->qhd', low(shares), value_rows, precision=HIGHEST)
    blocks = lax.map(jax.checkpoint(score_block), jnp.arange(GROUP // BLOCK, dtype=jnp.int32))
    return blocks.reshape(GROUP, queries.shape[1], queries.shape[2])

def layer(values, weight_in, weight_out, weight_gate, weight_down, gains, starts):
    width = values.shape[1]
    heads = width // HEAD
    weight_in = low(weight_in)
    weight_out = low(weight_out)
    weight_gate = low(weight_gate)
    weight_down = low(weight_down)
    gains = low(gains)
    normed_one = low(norm_rows(values, gains[0]))
    mixed = low_back(jnp.dot(normed_one, weight_in, precision=HIGHEST))
    positions = (jnp.arange(GROUP, dtype=jnp.int32)[None, :] - starts).reshape(-1).astype(jnp.float32)
    cosine_table, sine_table = rope_tables(positions)
    queries = low(rotate(mixed[:, :width].reshape(-1, heads, HEAD), cosine_table, sine_table))
    key_rows = low(rotate(mixed[:, width:2 * width].reshape(-1, heads, HEAD), cosine_table, sine_table))
    value_rows = low(mixed[:, 2 * width:].reshape(-1, heads, HEAD))
    grouped = (queries.reshape(OWNERS, GROUP, heads, HEAD), key_rows.reshape(OWNERS, GROUP, heads, HEAD), value_rows.reshape(OWNERS, GROUP, heads, HEAD), starts)
    attended = lax.map(attend_group, grouped).reshape(-1, width)
    attended = low_back(low(attended))
    branch = low_back(jnp.dot(attended, weight_out, precision=HIGHEST))
    middle = values + branch
    normed_two = low(norm_rows(middle, gains[1]))
    gate_values = low_back(jnp.dot(normed_two, weight_gate, precision=HIGHEST))
    hidden_width = weight_down.shape[0]
    gate_part = gate_values[:, :hidden_width]
    hidden = low(gate_part * jax.nn.sigmoid(gate_part) * gate_values[:, hidden_width:])
    return middle + jnp.dot(hidden, weight_down, precision=HIGHEST)

def balanced_order(target_slot, anchor_slot):
    target = target_slot.reshape(OWNERS, SPANS, TOK_DEV)
    anchor = anchor_slot.reshape(OWNERS, SPANS, TOK_DEV)
    sender = jnp.broadcast_to(jnp.arange(OWNERS, dtype=jnp.int32)[:, None, None], target.shape)
    span_index = jnp.broadcast_to(jnp.arange(SPANS, dtype=jnp.int32)[None, :, None], target.shape)
    local_row = jnp.broadcast_to(jnp.arange(TOK_DEV, dtype=jnp.int32)[None, None, :], target.shape)
    table = jnp.zeros((OWNERS, SPANS, OWNERS * CAP), jnp.int32).at[sender, span_index, target].set(local_row)
    source = anchor // CAP
    place = anchor % CAP
    found = table[source, span_index, sender * CAP + place]
    return ((source * SPANS + span_index) * TOK_DEV + found).reshape(-1).astype(jnp.int32)

def adamw(weight, gradient, first, second, rate, factor):
    clipped = gradient * factor
    first_new = BETA_FIRST * first + (1.0 - BETA_FIRST) * clipped
    second_new = BETA_SECOND * second + (1.0 - BETA_SECOND) * clipped * clipped
    corrected_first = first_new / (1.0 - BETA_FIRST ** STEP)
    corrected_second = second_new / (1.0 - BETA_SECOND ** STEP)
    weight_new = weight - rate * (corrected_first / (jnp.sqrt(corrected_second) + ADAM_EPSILON) + DECAY * weight)
    return (first_new, second_new, weight_new)

def reference(inputs, cotangent, target_slot, anchor_slot, sequence_start, attention_in, attention_out, gate_up, feed_down, norm_gains, first_in, first_out, first_gate, first_down, first_gains, second_in, second_out, second_gate, second_down, second_gains):
    order = balanced_order(target_slot, anchor_slot)
    balanced_in = jnp.take(inputs, order, axis=0).astype(jnp.float32)
    balanced_upstream = jnp.take(cotangent, order, axis=0).astype(jnp.float32)
    starts = sequence_start.reshape(OWNERS, GROUP)

    def forward(values, weight_in, weight_out, weight_gate, weight_down, gains):
        return layer(values, weight_in, weight_out, weight_gate, weight_down, gains, starts)
    result, pullback = jax.vjp(forward, balanced_in, attention_in, attention_out, gate_up, feed_down, norm_gains)
    input_grad, in_grad, out_grad, gate_grad, down_grad, gains_grad = pullback(balanced_upstream)
    outputs = jnp.zeros(inputs.shape, jnp.bfloat16).at[order].set(result.astype(jnp.bfloat16))
    input_gradient = jnp.zeros(inputs.shape, jnp.bfloat16).at[order].set(input_grad.astype(jnp.bfloat16))
    total = jnp.sum(in_grad * in_grad) + jnp.sum(out_grad * out_grad) + jnp.sum(gate_grad * gate_grad) + jnp.sum(down_grad * down_grad) + jnp.sum(gains_grad * gains_grad)
    gradient_norm = jnp.sqrt(total)
    factor = CLIP / jnp.maximum(gradient_norm, CLIP)
    first_a, second_a, weight_a = adamw(attention_in, in_grad, first_in, second_in, D ** (-0.5), factor)
    first_b, second_b, weight_b = adamw(attention_out, out_grad, first_out, second_out, 0.5, factor)
    first_c, second_c, weight_c = adamw(gate_up, gate_grad, first_gate, second_gate, D ** (-0.5), factor)
    first_d, second_d, weight_d = adamw(feed_down, down_grad, first_down, second_down, 2.0 * FF ** (-0.5), factor)
    first_e, second_e, weight_e = adamw(norm_gains, gains_grad, first_gains, second_gains, 1.5, factor)
    return (outputs, input_gradient, gradient_norm, first_a, second_a, weight_a, first_b, second_b, weight_b, first_c, second_c, weight_c, first_d, second_d, weight_d, first_e, second_e, weight_e)
```

```python
import functools

import jax
import jax.numpy as jnp
from jax import lax
from jax.experimental import pallas as pl
from jax.experimental.pallas import tpu as pltpu
from jax.sharding import Mesh
from jax.sharding import PartitionSpec as P

D = 1024
HEAD = 64
FF = 2816
STEP = 10
LANES = 128
TILE = 512

EPSILON = 1e-05
THETA = 500000.0
NEGATIVE = -1e30
BETA_FIRST = 0.9
BETA_SECOND = 0.95
ADAM_EPSILON = 1e-08
DECAY = 0.1
CLIP = 1.0
SCALE = 0.125
VMEM = 56 * 1024 * 1024
F32 = jnp.float32
BF16 = jnp.bfloat16
ROWS = ("chip", "core", "seq")


def norm_rows(values, gain_row):
    inverse = lax.rsqrt(jnp.mean(values * values, axis=1, keepdims=True) + EPSILON)
    normal = values * inverse
    return (normal * gain_row[None, :], normal, inverse)


def norm_back(upstream, normal, inverse, gain_row):
    gain_grad = jnp.sum(upstream * normal, axis=0)
    scaled = upstream * gain_row[None, :]
    return (
        inverse * (scaled - normal * jnp.mean(scaled * normal, axis=1, keepdims=True)),
        gain_grad,
    )


def rope_tables(positions):
    half_size = HEAD // 2
    frequency = jnp.power(THETA, -2.0 * jnp.arange(half_size, dtype=F32) / HEAD)
    angles = positions[:, None] * frequency[None, :]
    cosine = jnp.cos(angles)
    sine = jnp.sin(angles)
    return (
        jnp.concatenate([cosine] * 4, axis=1),
        jnp.concatenate([-sine, sine, -sine, sine], axis=1),
    )


def swap_halves(values):
    lane = lax.broadcasted_iota(jnp.int32, values.shape, 1)
    left = pltpu.roll(values, LANES - HEAD // 2, 1)
    right = pltpu.roll(values, HEAD // 2, 1)
    return jnp.where(lane % HEAD < HEAD // 2, left, right)


def contract_last(left, right):
    return lax.dot_general(left, right, (((1,), (1,)), ((), ())), preferred_element_type=F32)


def project_kernel(heads_width, spans, x_ref, gain_ref, w_ref, cos_ref, sin_ref, out_ref, h_ref):
    step = pl.program_id(0)

    @pl.when(step == 0)
    def _():
        x = x_ref[...].astype(F32)
        inverse = lax.rsqrt(jnp.mean(x * x, axis=1, keepdims=True) + EPSILON)
        h_ref[...] = (x * inverse * gain_ref[...]).astype(BF16)

    acc = jnp.dot(h_ref[...], w_ref[...], preferred_element_type=F32)

    @pl.when(step < 2 * spans)
    def _():
        for c in range(heads_width // LANES):
            part = acc[:, c * LANES : (c + 1) * LANES]
            turned = part * cos_ref[...] + swap_halves(part) * sin_ref[...]
            out_ref[0, :, c * LANES : (c + 1) * LANES] = turned.astype(BF16)

    @pl.when(step >= 2 * spans)
    def _():
        out_ref[0] = acc.astype(BF16)


def project(x, gain_row, weight, cosine, sine, spans):
    rows, width = x.shape
    hw = width // spans
    return pl.pallas_call(
        functools.partial(project_kernel, hw, spans),
        grid=(3 * spans,),
        in_specs=[
            pl.BlockSpec((rows, width), lambda t: (0, 0)),
            pl.BlockSpec((1, width), lambda t: (0, 0)),
            pl.BlockSpec((width, hw), lambda t: (0, t)),
            pl.BlockSpec((rows, LANES), lambda t: (0, 0)),
            pl.BlockSpec((rows, LANES), lambda t: (0, 0)),
        ],
        out_specs=[
            pl.BlockSpec((1, rows, hw), lambda t: (t % spans, 0, t // spans)),
            pl.BlockSpec((rows, width), lambda t: (0, 0)),
        ],
        out_shape=[
            jax.ShapeDtypeStruct((spans, rows, 3 * hw), BF16),
            jax.ShapeDtypeStruct((rows, width), BF16),
        ],
        compiler_params=pltpu.CompilerParams(vmem_limit_bytes=VMEM),
        cost_estimate=pl.CostEstimate(
            flops=2 * rows * width * 3 * width, bytes_accessed=12 * width * width, transcendentals=0
        ),
        name="project",
    )(x, gain_row, weight, cosine, sine)


def attend_kernel(block, start_ref, q_ref, k_ref, v_ref, low_ref, out_ref, log_ref):
    i = pl.program_id(1)
    lane = lax.broadcasted_iota(jnp.int32, (block, LANES), 1)
    first = lane < HEAD
    q_pair = q_ref[...] * SCALE
    query = i * block + lax.broadcasted_iota(jnp.int32, (block, block), 0)
    key = lax.broadcasted_iota(jnp.int32, (block, block), 1)
    starts = start_ref[...]
    parts = []
    for head in range(2):
        mine = first if head == 0 else jnp.logical_not(first)
        q = jnp.where(mine, q_pair, jnp.zeros_like(q_pair))

        def scores(j, diagonal, q=q):
            k = k_ref[pl.ds(pl.multiple_of(j * block, block), block), :]
            s = contract_last(q, k)
            seen = key + j * block >= starts
            if diagonal:
                seen = seen & (key + j * block <= query)
            return jnp.where(seen, s, NEGATIVE)

        def weigh(j, p):
            v = v_ref[pl.ds(pl.multiple_of(j * block, block), block), :]
            return jnp.dot(p.astype(BF16), v, preferred_element_type=F32)

        s = scores(i, True)
        top = jnp.max(s, axis=1, keepdims=True)
        p = jnp.exp(s - top)
        carry = (top, jnp.sum(p, axis=1, keepdims=True), weigh(i, p))

        def visit(j, carry):
            top, total, acc = carry
            s = scores(j, False)
            new = jnp.maximum(top, jnp.max(s, axis=1, keepdims=True))
            factor = jnp.exp(top - new)
            p = jnp.exp(s - new)
            return (
                new,
                total * factor + jnp.sum(p, axis=1, keepdims=True),
                acc * factor + weigh(j, p),
            )

        top, total, acc = lax.fori_loop(0, i, visit, carry)
        parts.append((acc / total, top + jnp.log(total)))
    out = jnp.where(first, parts[0][0], parts[1][0])
    out_ref[...] = out
    low_ref[...] = out.astype(BF16)
    logs = jnp.where(first, parts[0][1], parts[1][1]).T
    log_ref[0, 0:1, :] = logs[0:1]
    log_ref[0, 1:2, :] = logs[HEAD : HEAD + 1]


def attend(qkv, starts):
    group, width = qkv.shape
    hw = width // 3
    pairs = hw // LANES
    block = TILE
    return pl.pallas_call(
        functools.partial(attend_kernel, block),
        grid=(pairs, group // block),
        in_specs=[
            pl.BlockSpec((block, 1), lambda p, i: (i, 0)),
            pl.BlockSpec((block, LANES), lambda p, i: (i, p)),
            pl.BlockSpec((group, LANES), lambda p, i: (0, pairs + p)),
            pl.BlockSpec((group, LANES), lambda p, i: (0, 2 * pairs + p)),
        ],
        out_specs=[
            pl.BlockSpec((block, LANES), lambda p, i: (i, p)),
            pl.BlockSpec((block, LANES), lambda p, i: (i, p)),
            pl.BlockSpec((1, 8, block), lambda p, i: (p, 0, i)),
        ],
        out_shape=[
            jax.ShapeDtypeStruct((group, hw), BF16),
            jax.ShapeDtypeStruct((group, hw), F32),
            jax.ShapeDtypeStruct((pairs, 8, group), F32),
        ],
        compiler_params=pltpu.CompilerParams(vmem_limit_bytes=VMEM),
        cost_estimate=pl.CostEstimate(
            flops=4 * group * group * hw, bytes_accessed=8 * group * width, transcendentals=0
        ),
        name="attend",
    )(starts.reshape(group, 1), qkv, qkv, qkv)


def attend_back_kernel(
    block,
    start_ref,
    q_ref,
    k_ref,
    v_ref,
    do_ref,
    out_ref,
    log_ref,
    cos_ref,
    sin_ref,
    dq_ref,
    dk_ref,
    dv_ref,
    delta_ref,
    turned_ref,
):
    j = pl.program_id(1)
    blocks = pl.num_programs(1)
    lane = lax.broadcasted_iota(jnp.int32, (block, LANES), 1)
    first = lane < HEAD

    @pl.when(j == 0)
    def _():
        def prepare(i, carry):
            at = pl.ds(pl.multiple_of(i * block, block), block)
            product = (do_ref[at, :].astype(F32) * out_ref[at, :]).T
            delta_ref[0:1, at] = jnp.sum(product[:HEAD], axis=0, keepdims=True)
            delta_ref[1:2, at] = jnp.sum(product[HEAD:], axis=0, keepdims=True)
            return carry

        lax.fori_loop(0, blocks, prepare, 0)
        turned_ref[...] = jnp.zeros_like(turned_ref)

    here = pl.ds(pl.multiple_of(j * block, block), block)
    k_pair = k_ref[here, :]
    v_pair = v_ref[here, :]
    k_turned = k_pair.astype(F32).T.astype(BF16)
    key = j * block + lax.broadcasted_iota(jnp.int32, (block, block), 0)
    query = lax.broadcasted_iota(jnp.int32, (block, block), 1)

    def visit(i, carry, diagonal):
        dk, dv = carry
        at = pl.ds(pl.multiple_of(i * block, block), block)
        q_pair = q_ref[at, :] * SCALE
        do_pair = do_ref[at, :]
        seen = key >= start_ref[:, at]
        if diagonal:
            seen = seen & (key <= query + i * block)
        for head in range(2):
            mine = first if head == 0 else jnp.logical_not(first)
            q = jnp.where(mine, q_pair, jnp.zeros_like(q_pair))
            do = jnp.where(mine, do_pair, jnp.zeros_like(do_pair))
            s = jnp.where(seen, contract_last(k_pair, q), NEGATIVE)
            p = jnp.exp(s - log_ref[0, head : head + 1, at])
            dp = contract_last(v_pair, do)
            ds = (p * (dp - delta_ref[head : head + 1, at])).astype(BF16)
            dv = dv + jnp.dot(p.astype(BF16), do, preferred_element_type=F32)
            dk = dk + jnp.dot(ds, q, preferred_element_type=F32)
            lines = slice(head * HEAD, (head + 1) * HEAD)
            turned_ref[lines, at] += jnp.dot(k_turned[lines], ds, preferred_element_type=F32)
        return (dk, dv)

    zero = jnp.zeros((block, LANES), F32)
    carry = visit(j, (zero, zero), True)
    dk, dv = lax.fori_loop(j + 1, blocks, lambda i, c: visit(i, c, False), carry)

    def turn_back(values, at):
        return values * cos_ref[at, :] + swap_halves(values * sin_ref[at, :])

    dk_ref[0] = turn_back(dk, here).astype(BF16)
    dv_ref[0] = dv.astype(BF16)

    @pl.when(j == blocks - 1)
    def _():
        def finish(i, carry):
            at = pl.ds(pl.multiple_of(i * block, block), block)
            dq_ref[0, at, :] = turn_back(turned_ref[:, at].T * SCALE, at).astype(BF16)
            return carry

        lax.fori_loop(0, blocks, finish, 0)


def attend_back(qkv, starts, do, out, logs, cosine, sine):
    group, width = qkv.shape
    hw = width // 3
    pairs = hw // LANES
    block = TILE
    whole = lambda p, j: (0, 0)
    return pl.pallas_call(
        functools.partial(attend_back_kernel, block),
        grid=(pairs, group // block),
        in_specs=[
            pl.BlockSpec((1, group), whole),
            pl.BlockSpec((group, LANES), lambda p, j: (0, p)),
            pl.BlockSpec((group, LANES), lambda p, j: (0, pairs + p)),
            pl.BlockSpec((group, LANES), lambda p, j: (0, 2 * pairs + p)),
            pl.BlockSpec((group, LANES), lambda p, j: (0, p)),
            pl.BlockSpec((group, LANES), lambda p, j: (0, p)),
            pl.BlockSpec((1, 8, group), lambda p, j: (p, 0, 0)),
            pl.BlockSpec((group, LANES), whole),
            pl.BlockSpec((group, LANES), whole),
        ],
        out_specs=[
            pl.BlockSpec((1, group, LANES), lambda p, j: (0, 0, p)),
            pl.BlockSpec((1, block, LANES), lambda p, j: (0, j, p)),
            pl.BlockSpec((1, block, LANES), lambda p, j: (0, j, p)),
        ],
        out_shape=[jax.ShapeDtypeStruct((1, group, hw), BF16)] * 3,
        scratch_shapes=[pltpu.VMEM((8, group), F32), pltpu.VMEM((LANES, group), F32)],
        compiler_params=pltpu.CompilerParams(vmem_limit_bytes=VMEM),
        cost_estimate=pl.CostEstimate(
            flops=10 * group * group * hw, bytes_accessed=12 * group * width, transcendentals=0
        ),
        name="attend_back",
    )(starts.reshape(1, group), qkv, qkv, qkv, do, out, logs, cosine, sine)


def adamw(weight, gradient, first, second, rate, factor):
    clipped = gradient * factor
    first_new = BETA_FIRST * first + (1.0 - BETA_FIRST) * clipped
    second_new = BETA_SECOND * second + (1.0 - BETA_SECOND) * clipped * clipped
    corrected_first = first_new / (1.0 - BETA_FIRST**STEP)
    corrected_second = second_new / (1.0 - BETA_SECOND**STEP)
    weight_new = weight - rate * (
        corrected_first / (jnp.sqrt(corrected_second) + ADAM_EPSILON) + DECAY * weight
    )
    return (first_new, second_new, weight_new)


def swap_core(values):
    return lax.ppermute(values, "core", [(0, 1), (1, 0)])


def gather_weight(shard):
    chips = lax.axis_size("chip")
    width = shard.shape[1]
    mine = lax.all_gather(shard.astype(BF16), ("chip", "seq"), axis=0, tiled=True)
    other = swap_core(mine)
    mine = mine.reshape(chips, 1, -1, width)
    other = other.reshape(chips, 1, -1, width)
    own = lax.axis_index("core") == 0
    both = jnp.where(
        own,
        jnp.concatenate([mine, other], axis=1),
        jnp.concatenate([other, mine], axis=1),
    )
    return both.reshape(-1, width)


def scatter_sum(gradient):
    chips = lax.axis_size("chip")
    rows, width = gradient.shape
    parts = gradient.reshape(chips, 2, -1, width)
    own = lax.axis_index("core") == 0
    mine = jnp.where(own, parts[:, 0], parts[:, 1])
    other = jnp.where(own, parts[:, 1], parts[:, 0]).astype(BF16)
    both = (mine + swap_core(other).astype(F32)).astype(BF16).reshape(-1, width)
    line = lax.psum_scatter(both, "chip", scatter_dimension=0, tiled=True)
    return lax.psum_scatter(line, "seq", scatter_dimension=0, tiled=True).astype(F32)


def sum_everywhere(values):
    for axis in ROWS:
        count = lax.axis_size(axis)
        step = 1
        while step < count:
            values = values + lax.ppermute(values, axis, [(i, i ^ step) for i in range(count)])
            step *= 2
    return values


def place(index, values, slots):
    chosen = lax.broadcasted_iota(jnp.int32, (slots, index.shape[0]), 0) == index[None, :]
    return jnp.dot(chosen.astype(BF16), values, preferred_element_type=F32).astype(BF16)


def pick(index, values):
    slots = values.shape[0]
    chosen = lax.broadcasted_iota(jnp.int32, (index.shape[0], slots), 1) == index[:, None]
    return jnp.dot(chosen.astype(BF16), values, preferred_element_type=F32).astype(BF16)


def per_device(
    inputs,
    cotangent,
    target_slot,
    anchor_slot,
    sequence_start,
    attention_in,
    attention_out,
    gate_up,
    feed_down,
    norm_gains,
    first_in,
    first_out,
    first_gate,
    first_down,
    first_gains,
    second_in,
    second_out,
    second_gate,
    second_down,
    second_gains,
):
    owners = lax.axis_size("chip") * lax.axis_size("core")
    spans = lax.axis_size("seq")
    rows, width = inputs.shape
    per_owner = rows // owners
    capacity = per_owner + per_owner // 2
    slots = owners * capacity
    group = rows * spans
    hw = width // spans
    first_row = lax.axis_index("seq") * rows

    def exchange(values):
        return lax.all_to_all(values, ("chip", "core"), split_axis=0, concat_axis=0, tiled=True)

    def across(values):
        return lax.all_to_all(values, "seq", split_axis=0, concat_axis=0, tiled=True)

    balanced_in = pick(anchor_slot, exchange(place(target_slot, inputs, slots)))
    upstream = pick(anchor_slot, exchange(place(target_slot, cotangent, slots)))
    gain_rows = lax.all_gather(norm_gains.astype(BF16), ROWS, axis=1, tiled=True).astype(F32)
    starts = lax.all_gather(sequence_start, "seq", axis=0, tiled=True)
    weight_in = gather_weight(attention_in)
    weight_out = gather_weight(attention_out)
    weight_gate = gather_weight(gate_up)
    weight_down = gather_weight(feed_down)

    local = first_row + jnp.arange(rows, dtype=jnp.int32) - sequence_start
    cosine, sine = rope_tables(local.astype(F32))
    cosine_all, sine_all = rope_tables((jnp.arange(group, dtype=jnp.int32) - starts).astype(F32))

    residual = balanced_in.astype(F32)
    cut, normed_one = project(balanced_in, gain_rows[0:1], weight_in, cosine, sine, spans)
    qkv = across(cut).reshape(group, 3 * hw)
    attended_cut, attended, logs = attend(qkv, starts)

    def whole_rows(values):
        return jnp.transpose(across(values.reshape(spans, rows, hw)), (1, 0, 2)).reshape(rows, width)

    attended_low = whole_rows(attended_cut)
    middle = residual + jnp.dot(attended_low, weight_out, preferred_element_type=F32)
    normed_two, normal_two, inverse_two = norm_rows(middle, gain_rows[1])
    normed_two = normed_two.astype(BF16)
    gate_values = jnp.dot(normed_two, weight_gate, preferred_element_type=F32)
    hidden_width = weight_down.shape[0]
    gate_part = gate_values[:, :hidden_width]
    up_part = gate_values[:, hidden_width:]
    sigmoid_gate = jax.nn.sigmoid(gate_part)
    activated = gate_part * sigmoid_gate
    hidden = (activated * up_part).astype(BF16)
    result = middle + jnp.dot(hidden, weight_down, preferred_element_type=F32)
    result_low = result.astype(BF16)
    down_grad = jnp.dot(hidden.T, upstream, preferred_element_type=F32)
    hidden_grad = jnp.dot(upstream, weight_down.T, preferred_element_type=F32)
    gate_grad = hidden_grad * up_part * sigmoid_gate * (1.0 + gate_part * (1.0 - sigmoid_gate))
    up_grad = hidden_grad * activated
    mixed_two_grad = jnp.concatenate([gate_grad, up_grad], axis=1).astype(BF16)
    gate_weight_grad = jnp.dot(normed_two.T, mixed_two_grad, preferred_element_type=F32)
    normed_two_grad = jnp.dot(mixed_two_grad, weight_gate.T, preferred_element_type=F32)
    middle_norm_grad, gain_two_grad = norm_back(
        normed_two_grad, normal_two, inverse_two, gain_rows[1]
    )
    middle_grad = upstream.astype(F32) + middle_norm_grad
    branch_grad = middle_grad.astype(BF16)
    out_weight_grad = jnp.dot(attended_low.T, branch_grad, preferred_element_type=F32)
    grad_heads = jnp.dot(branch_grad, weight_out.T, preferred_element_type=F32).astype(BF16)
    grad_cut = across(jnp.transpose(grad_heads.reshape(rows, spans, hw), (1, 0, 2)))
    grads = attend_back(
        qkv, starts, grad_cut.reshape(group, hw), attended, logs, cosine_all, sine_all
    )
    mixed_grad = jnp.concatenate([whole_rows(grad) for grad in grads], axis=1)
    in_weight_grad = jnp.dot(normed_one.T, mixed_grad, preferred_element_type=F32)
    normed_one_grad = jnp.dot(mixed_grad, weight_in.T, preferred_element_type=F32)
    _, normal_one, inverse_one = norm_rows(residual, gain_rows[0])
    residual_norm_grad, gain_one_grad = norm_back(
        normed_one_grad, normal_one, inverse_one, gain_rows[0]
    )
    input_low = (middle_grad + residual_norm_grad).astype(BF16)
    outputs = pick(target_slot, exchange(place(anchor_slot, result_low, slots)))
    input_gradient = pick(target_slot, exchange(place(anchor_slot, input_low, slots)))

    down_shard = scatter_sum(down_grad)
    gate_shard = scatter_sum(gate_weight_grad)
    out_shard = scatter_sum(out_weight_grad)
    in_shard = scatter_sum(in_weight_grad)
    gains_total = sum_everywhere(jnp.stack([gain_one_grad, gain_two_grad]))
    columns = norm_gains.shape[1]
    device = (lax.axis_index("chip") * 2 + lax.axis_index("core")) * spans + lax.axis_index("seq")
    gain_shard = lax.dynamic_slice_in_dim(gains_total, device * columns, columns, 1)
    local_total = (
        jnp.sum(in_shard * in_shard)
        + jnp.sum(out_shard * out_shard)
        + jnp.sum(gate_shard * gate_shard)
        + jnp.sum(down_shard * down_shard)
        + jnp.sum(gain_shard * gain_shard)
    )
    total = sum_everywhere(jnp.broadcast_to(local_total, (8, LANES)))[0, 0]
    gradient_norm = jnp.sqrt(total)
    factor = CLIP / jnp.maximum(gradient_norm, CLIP)
    updates = []
    for weight, gradient, first, second, rate in (
        (attention_in, in_shard, first_in, second_in, D ** (-0.5)),
        (attention_out, out_shard, first_out, second_out, 0.5),
        (gate_up, gate_shard, first_gate, second_gate, D ** (-0.5)),
        (feed_down, down_shard, first_down, second_down, 2.0 * FF ** (-0.5)),
        (norm_gains, gain_shard, first_gains, second_gains, 1.5),
    ):
        updates.extend(adamw(weight, gradient, first, second, rate, factor))
    return (outputs, input_gradient, gradient_norm, *updates)


def solution(mesh):
    owners, spans = mesh.shape["dp"], mesh.shape["seq"]
    parts = Mesh(mesh.devices.reshape(owners // 2, 2, spans), ROWS)
    rows = P(ROWS, None)
    columns = P(None, ROWS)
    line = P(ROWS)
    in_specs = (rows, rows, line, line, line) + ((rows,) * 4 + (columns,)) * 3
    out_specs = (rows, rows, P()) + (rows,) * 12 + (columns,) * 3
    return jax.shard_map(
        per_device, mesh=parts, in_specs=in_specs, out_specs=out_specs, check_vma=False
    )
```

```python
import functools

import jax
import jax.numpy as jnp
from jax import lax
from jax.experimental import pallas as pl
from jax.experimental.pallas import tpu as pltpu
from jax.sharding import Mesh
from jax.sharding import PartitionSpec as P

D = 1024
HEAD = 64
FF = 2816
STEP = 10
LANES = 128

EPSILON = 1e-05
THETA = 500000.0
NEGATIVE = -1e30
BETA_FIRST = 0.9
BETA_SECOND = 0.95
ADAM_EPSILON = 1e-08
DECAY = 0.1
CLIP = 1.0
SCALE = 0.125
VMEM = 56 * 1024 * 1024
F32 = jnp.float32
BF16 = jnp.bfloat16
ROWS = ("chip", "core", "seq")


def norm_rows(values, gain_row):
    inverse = lax.rsqrt(jnp.mean(values * values, axis=1, keepdims=True) + EPSILON)
    normal = values * inverse
    return (normal * gain_row[None, :], normal, inverse)


def norm_back(upstream, normal, inverse, gain_row):
    gain_grad = jnp.sum(upstream * normal, axis=0)
    scaled = upstream * gain_row[None, :]
    return (
        inverse * (scaled - normal * jnp.mean(scaled * normal, axis=1, keepdims=True)),
        gain_grad,
    )


def rope_tables(positions):
    half_size = HEAD // 2
    frequency = jnp.power(THETA, -2.0 * jnp.arange(half_size, dtype=F32) / HEAD)
    angles = positions[:, None] * frequency[None, :]
    cosine = jnp.cos(angles)
    sine = jnp.sin(angles)
    return (
        jnp.concatenate([cosine] * 4, axis=1),
        jnp.concatenate([-sine, sine, -sine, sine], axis=1),
    )


def swap_halves(values):
    lane = lax.broadcasted_iota(jnp.int32, values.shape, 1)
    left = pltpu.roll(values, LANES - HEAD // 2, 1)
    right = pltpu.roll(values, HEAD // 2, 1)
    return jnp.where(lane % HEAD < HEAD // 2, left, right)


def contract_last(left, right):
    return lax.dot_general(left, right, (((1,), (1,)), ((), ())), preferred_element_type=F32)


def params():
    return pltpu.CompilerParams(vmem_limit_bytes=VMEM)


def turned(values):
    return values.astype(F32).T.astype(BF16)


def rows_at(index, count):
    return pl.ds(pl.multiple_of(index * count, count), count)


def project_kernel(spans, half, place_ref, x_ref, gain_ref, wa_ref, wb_ref, cos_ref, sin_ref, h_ref, *outs):
    step = pl.program_id(0)
    hw = wa_ref.shape[1]

    @pl.when(step == 0)
    def _():
        x = x_ref[...].astype(F32)
        inverse = lax.rsqrt(jnp.mean(x * x, axis=1, keepdims=True) + EPSILON)
        h_ref[...] = (x * inverse * gain_ref[...]).astype(BF16)

    def work(w_ref, rotated):
        acc = jnp.dot(h_ref[...], w_ref[...], preferred_element_type=F32)
        if rotated:
            pieces = []
            for c in range(hw // LANES):
                part = acc[:, c * LANES : (c + 1) * LANES]
                pieces.append(part * cos_ref[...] + swap_halves(part) * sin_ref[...])
            acc = jnp.concatenate(pieces, axis=1)
        low = acc.astype(BF16)
        for k in range(spans):

            @pl.when((step % spans) ^ place_ref[0] == k)
            def _(k=k):
                for pair in range(hw // LANES):
                    outs[pair * spans + k][...] = low[:, pair * LANES : (pair + 1) * LANES]

    turning = step < 2 * spans
    pl.when(step < half)(lambda: work(wa_ref, True))
    pl.when((step >= half) & turning)(lambda: work(wb_ref, True))
    pl.when(jnp.logical_not(turning))(lambda: work(wb_ref, False))


def project(spot, x, gain_row, weights, cosine, sine, spans):
    rows, width = x.shape
    hw = width // spans
    half = 3 * spans // 2
    fixed = lambda t, p: (0, 0)
    return pl.pallas_call(
        functools.partial(project_kernel, spans, half),
        grid_spec=pltpu.PrefetchScalarGridSpec(
            num_scalar_prefetch=1,
            grid=(3 * spans,),
            in_specs=[
                pl.BlockSpec((rows, width), fixed),
                pl.BlockSpec((1, width), fixed),
                pl.BlockSpec((width, hw), lambda t, p: (0, jnp.minimum(t, half - 1))),
                pl.BlockSpec((width, hw), lambda t, p: (0, jnp.maximum(t - half, 0))),
                pl.BlockSpec((rows, LANES), fixed),
                pl.BlockSpec((rows, LANES), fixed),
            ],
            out_specs=[pl.BlockSpec((rows, width), fixed)]
            + [pl.BlockSpec((rows, LANES), lambda t, p: (0, t // spans))] * (width // LANES),
        ),
        out_shape=[jax.ShapeDtypeStruct((rows, width), BF16)]
        + [jax.ShapeDtypeStruct((rows, 3 * LANES), BF16)] * (width // LANES),
        compiler_params=params(),
        cost_estimate=pl.CostEstimate(
            flops=17250000000, bytes_accessed=0, transcendentals=0
        ),
        name="project",
    )(spot, x, gain_row, *weights, cosine, sine)


def attend_kernel(spans, place_ref, start_ref, *refs):
    pieces, refs = refs[: 3 * spans], refs[3 * spans :]
    lows, (out_ref, log_ref, q_scr, k_scr, v_scr) = refs[:spans], refs[spans:]
    block = q_scr.shape[0] // spans
    here = place_ref[0]
    relative = pl.program_id(0)
    i = relative ^ here
    lane = lax.broadcasted_iota(jnp.int32, (block, LANES), 1)
    first = lane < HEAD

    @pl.when(relative == 0)
    def _():
        for k in range(spans):
            at = rows_at(here ^ k, block)
            q_scr[k * block : (k + 1) * block, :] = pieces[k][...]
            k_scr[at, :] = pieces[spans + k][...]
            v_scr[:, at] = turned(pieces[2 * spans + k][...])

    q_pair = q_scr[rows_at(relative, block), :] * SCALE
    key = lax.broadcasted_iota(jnp.int32, (block, block), 0)
    query = lax.broadcasted_iota(jnp.int32, (block, block), 1)
    starts = start_ref[:, rows_at(i, block)]
    heads = []
    for head in range(2):
        mine = first if head == 0 else jnp.logical_not(first)
        heads.append(jnp.where(mine, q_pair, jnp.zeros_like(q_pair)))

    def visit(j, carry, diagonal):
        at = rows_at(j, block)
        k = k_scr[at, :]
        seen = key + j * block >= starts
        if diagonal:
            seen = seen & (key <= query)
        result = []
        for head in range(2):
            s = jnp.where(seen, contract_last(k, heads[head]), NEGATIVE)
            lines = slice(head * HEAD, (head + 1) * HEAD)
            new = jnp.max(s, axis=0, keepdims=True)
            if not diagonal:
                top, total, acc = carry[head]
                new = jnp.maximum(top, new)
            p = jnp.exp(s - new)
            added = jnp.sum(p, axis=0, keepdims=True)
            weighed = jnp.dot(v_scr[lines, at], p.astype(BF16), preferred_element_type=F32)
            if not diagonal:
                factor = jnp.exp(top - new)
                added = added + total * factor
                weighed = weighed + acc * factor
            result.append((new, added, weighed))
        return tuple(result)

    carry = visit(i, None, True)
    carry = lax.fori_loop(0, i, lambda j, c: visit(j, c, False), carry)
    parts = []
    for head in range(2):
        top, total, acc = carry[head]
        parts.append(acc / total)
        log_ref[head : head + 1, :] = top + jnp.log(total)
    out = jnp.concatenate(parts, axis=0).T
    out_ref[0] = out
    low = out.astype(BF16)
    for k in range(spans):

        @pl.when(relative == k)
        def _(k=k):
            lows[k][...] = low


def piece_specs(rows, spans):
    return [
        pl.BlockSpec((rows, LANES), functools.partial(lambda part, i, s: (0, part), part))
        for part in range(3)
        for _ in range(spans)
    ]


def attend(spot, qkv, starts):
    spans = len(qkv)
    rows = qkv[0].shape[0]
    group = rows * spans
    return pl.pallas_call(
        functools.partial(attend_kernel, spans),
        grid_spec=pltpu.PrefetchScalarGridSpec(
            num_scalar_prefetch=1,
            grid=(spans,),
            in_specs=[pl.BlockSpec((1, group), lambda i, s: (0, 0))] + piece_specs(rows, spans),
            out_specs=[pl.BlockSpec((rows, LANES), lambda i, s: (0, 0))] * spans
            + [
                pl.BlockSpec((1, rows, LANES), lambda i, s: (i, 0, 0)),
                pl.BlockSpec((8, rows), lambda i, s: (0, i ^ s[0])),
            ],
            scratch_shapes=[
                pltpu.VMEM((group, LANES), BF16),
                pltpu.VMEM((group, LANES), BF16),
                pltpu.VMEM((LANES, group), BF16),
            ],
        ),
        out_shape=[jax.ShapeDtypeStruct((rows, LANES), BF16)] * spans
        + [
            jax.ShapeDtypeStruct((spans, rows, LANES), F32),
            jax.ShapeDtypeStruct((8, group), F32),
        ],
        compiler_params=params(),
        cost_estimate=pl.CostEstimate(
            flops=18400000000, bytes_accessed=0, transcendentals=0
        ),
        name="attend",
    )(spot, starts.reshape(1, group), *(list(qkv) * 3))


def attend_back_kernel(spans, place_ref, start_ref, *refs):
    pieces, refs = refs[: 3 * spans], refs[3 * spans :]
    grads, refs = refs[:spans], refs[spans:]
    (out_ref, log_ref, cos_ref, sin_ref), refs = refs[:4], refs[4:]
    outs, refs = refs[:spans], refs[spans:]
    q_scr, k_scr, v_scr, do_scr, dq_scr, dk_scr, dv_scr, delta_ref, turned_ref = refs
    block = q_scr.shape[0] // spans
    here = place_ref[0]
    j = pl.program_id(0)
    lane = lax.broadcasted_iota(jnp.int32, (block, LANES), 1)
    first = lane < HEAD

    @pl.when(j == 0)
    def _():
        for k in range(spans):
            at = rows_at(here ^ k, block)
            q_scr[at, :] = pieces[k][...]
            k_scr[at, :] = pieces[spans + k][...]
            v_scr[at, :] = pieces[2 * spans + k][...]
            do = grads[k][...]
            do_scr[at, :] = do
            product = (do.astype(F32) * out_ref[k]).T
            delta_ref[0:1, at] = jnp.sum(product[:HEAD], axis=0, keepdims=True)
            delta_ref[1:2, at] = jnp.sum(product[HEAD:], axis=0, keepdims=True)
        turned_ref[...] = jnp.zeros_like(turned_ref)

    now = rows_at(j, block)
    k_pair = k_scr[now, :]
    v_pair = v_scr[now, :]
    k_turned = turned(k_pair)
    key = j * block + lax.broadcasted_iota(jnp.int32, (block, block), 0)
    query = lax.broadcasted_iota(jnp.int32, (block, block), 1)

    def visit(i, carry, diagonal):
        dk, dv = carry
        at = rows_at(i, block)
        q_pair = q_scr[at, :] * SCALE
        do_pair = do_scr[at, :]
        seen = key >= start_ref[:, at]
        if diagonal:
            seen = seen & (key <= query + i * block)
        for head in range(2):
            mine = first if head == 0 else jnp.logical_not(first)
            q = jnp.where(mine, q_pair, jnp.zeros_like(q_pair))
            do = jnp.where(mine, do_pair, jnp.zeros_like(do_pair))
            s = jnp.where(seen, contract_last(k_pair, q), NEGATIVE)
            p = jnp.exp(s - log_ref[head : head + 1, at])
            dp = contract_last(v_pair, do)
            ds = (p * (dp - delta_ref[head : head + 1, at])).astype(BF16)
            dv = dv + jnp.dot(p.astype(BF16), do, preferred_element_type=F32)
            dk = dk + jnp.dot(ds, q, preferred_element_type=F32)
            lines = slice(head * HEAD, (head + 1) * HEAD)
            turned_ref[lines, at] += jnp.dot(k_turned[lines], ds, preferred_element_type=F32)
        return (dk, dv)

    zero = jnp.zeros((block, LANES), F32)
    carry = visit(j, (zero, zero), True)
    dk, dv = lax.fori_loop(j + 1, spans, lambda i, c: visit(i, c, False), carry)

    def turn_back(values, at):
        return values * cos_ref[at, :] + swap_halves(values * sin_ref[at, :])

    dk_scr[now, :] = turn_back(dk, now).astype(BF16)
    dv_scr[now, :] = dv.astype(BF16)

    @pl.when(j == spans - 1)
    def _():
        def finish(i, carry):
            at = rows_at(i, block)
            dq_scr[at, :] = turn_back(turned_ref[:, at].T * SCALE, at).astype(BF16)
            return carry

        lax.fori_loop(0, spans, finish, 0)
        for k in range(spans):
            at = rows_at(here ^ k, block)
            for part, scr in enumerate((dq_scr, dk_scr, dv_scr)):
                outs[k][:, part * LANES : (part + 1) * LANES] = scr[at, :]


def attend_back(spot, qkv, starts, grads, out, logs, cosine, sine):
    spans = len(qkv)
    rows = qkv[0].shape[0]
    group = rows * spans
    whole = lambda j, s: (0, 0)
    low = pltpu.VMEM((group, LANES), BF16)
    return pl.pallas_call(
        functools.partial(attend_back_kernel, spans),
        grid_spec=pltpu.PrefetchScalarGridSpec(
            num_scalar_prefetch=1,
            grid=(spans,),
            in_specs=[pl.BlockSpec((1, group), whole)]
            + piece_specs(rows, spans)
            + [pl.BlockSpec((rows, LANES), whole)] * spans
            + [
                pl.BlockSpec((spans, rows, LANES), lambda j, s: (0, 0, 0)),
                pl.BlockSpec((8, group), whole),
                pl.BlockSpec((group, LANES), whole),
                pl.BlockSpec((group, LANES), whole),
            ],
            out_specs=[pl.BlockSpec((rows, 3 * LANES), whole)] * spans,
            scratch_shapes=[low] * 7 + [pltpu.VMEM((8, group), F32), pltpu.VMEM((LANES, group), F32)],
        ),
        out_shape=[jax.ShapeDtypeStruct((rows, 3 * LANES), BF16)] * spans,
        compiler_params=params(),
        cost_estimate=pl.CostEstimate(
            flops=27600000000, bytes_accessed=0, transcendentals=0
        ),
        name="attend_back",
    )(spot, starts.reshape(1, group), *(list(qkv) * 3), *grads, out, logs, cosine, sine)


def core_split(values, block, own):
    width = values.shape[1]
    sides = []
    for core in range(2):
        blocks = [values[:, b * block : (b + 1) * block] for b in range(core, width // block, 2)]
        sides.append(jnp.concatenate(blocks, axis=1))
    return (jnp.where(own == 0, sides[0], sides[1]), jnp.where(own == 0, sides[1], sides[0]))


def core_merge(mine, other, block, own):
    sides = (jnp.where(own == 0, mine, other), jnp.where(own == 0, other, mine))
    blocks = mine.shape[1] // block
    return jnp.concatenate(
        [side[:, b * block : (b + 1) * block] for b in range(blocks) for side in sides], axis=1
    )


def middle_kernel(spans, block, place_ref, x_ref, dy_ref, gain_ref, om_ref, oo_ref, *refs):
    heads = x_ref.shape[1] // LANES
    attended, refs = refs[:heads], refs[heads:]
    (gm_ref, um_ref, go_ref, uo_ref, da_ref, db_ref), refs = refs[:6], refs[6:]
    (y_ref, dx_ref, branch_ref, ow_ref, ox_ref, gain_grad_ref), refs = refs[:6], refs[6:]
    (gk_ref, uk_ref, gs_ref, us_ref, ga_ref, gb_ref), refs = refs[:6], refs[6:]
    grads, refs = refs[:heads], refs[heads:]
    hm_scr, ho_scr, kept_scr, sent_scr, x2_scr, y_scr, dm_scr, do_scr, wide_scr = refs
    step, steps = pl.program_id(0), pl.num_programs(0)
    half = x_ref.shape[1] // 2
    here, core = place_ref[0], place_ref[1]

    def pieces_at(pieces):
        for index, piece in enumerate(pieces):
            pair, k = index // spans, index % spans
            yield rows_at((here ^ k) * (heads // spans) + pair, LANES), piece

    def normal():
        x2 = x2_scr[...]
        inverse = lax.rsqrt(jnp.mean(x2 * x2, axis=1, keepdims=True) + EPSILON)
        return (x2 * inverse, inverse)

    @pl.when(step == 0)
    def _():
        for at, piece in pieces_at(attended):
            wide_scr[:, at] = piece[...]
        mine, other = core_split(wide_scr[...], block, core)
        ow_ref[...] = mine
        ox_ref[...] = other
        x2_scr[...] = (
            x_ref[...].astype(F32)
            + jnp.dot(mine, om_ref[...], preferred_element_type=F32)
            + jnp.dot(other, oo_ref[...], preferred_element_type=F32)
        )
        h = (normal()[0] * gain_ref[...]).astype(BF16).astype(F32)
        mine, other = core_split(h, block, core)
        hm_scr[...] = mine.astype(BF16)
        ho_scr[...] = other.astype(BF16)
        kept_scr[...] = mine.T.astype(BF16)
        sent_scr[...] = other.T.astype(BF16)
        y_scr[...] = jnp.zeros_like(y_scr)
        dm_scr[...] = jnp.zeros_like(dm_scr)
        do_scr[...] = jnp.zeros_like(do_scr)

    hm, ho, dy = hm_scr[...], ho_scr[...], dy_ref[...]
    gm, um, go, uo = gm_ref[...], um_ref[...], go_ref[...], uo_ref[...]
    gate = jnp.dot(hm, gm, preferred_element_type=F32) + jnp.dot(ho, go, preferred_element_type=F32)
    up = jnp.dot(hm, um, preferred_element_type=F32) + jnp.dot(ho, uo, preferred_element_type=F32)
    share = jax.nn.sigmoid(gate)
    active = gate * share
    hidden_full = active * up
    hidden = hidden_full.astype(BF16)
    down = jnp.concatenate([da_ref[...], db_ref[...]], axis=1)
    y_scr[...] += jnp.dot(hidden, down, preferred_element_type=F32)
    dhid = contract_last(dy, down)
    dgate = (dhid * up * share * (1.0 + gate * (1.0 - share))).astype(BF16)
    dup = (dhid * active).astype(BF16)
    dm_scr[...] += contract_last(dgate, gm) + contract_last(dup, um)
    do_scr[...] += contract_last(dgate, go) + contract_last(dup, uo)
    kept, sent = kept_scr[...], sent_scr[...]
    gs_ref[...] = jnp.dot(sent, dgate, preferred_element_type=F32).astype(BF16)
    us_ref[...] = jnp.dot(sent, dup, preferred_element_type=F32).astype(BF16)
    gk_ref[...] = jnp.dot(kept, dgate, preferred_element_type=F32).astype(BF16)
    uk_ref[...] = jnp.dot(kept, dup, preferred_element_type=F32).astype(BF16)
    hidden_turned = hidden_full.T.astype(BF16)
    ga_ref[...] = jnp.dot(hidden_turned, dy[:, :half], preferred_element_type=F32).astype(BF16)
    gb_ref[...] = jnp.dot(hidden_turned, dy[:, half:], preferred_element_type=F32).astype(BF16)

    @pl.when(step == steps - 1)
    def _():
        y_ref[...] = (x2_scr[...] + y_scr[...]).astype(BF16)
        norm, inverse = normal()
        dh = core_merge(dm_scr[...], do_scr[...], block, core)
        gain_grad_ref[...] = jnp.sum(dh * norm, axis=0, keepdims=True)
        scaled = dh * gain_ref[...]
        inner = jnp.mean(scaled * norm, axis=1, keepdims=True)
        dx = dy_ref[...].astype(F32) + inverse * (scaled - norm * inner)
        dx_ref[...] = dx
        branch = dx.astype(BF16)
        branch_ref[...] = branch
        mine = contract_last(branch, om_ref[...]).astype(BF16)
        other = contract_last(branch, oo_ref[...]).astype(BF16)
        wide_scr[...] = core_merge(mine, other, block, core)
        for at, piece in pieces_at(grads):
            piece[...] = wide_scr[:, at]


def middle(spot, owners, spans, x, dy, gain_row, weight_out, attended, weight_gate, weight_down):
    rows, width = x.shape
    hidden = weight_gate[0].shape[1]
    heads, half, tile = width // LANES, width // 2, 2 * LANES
    tiles = hidden // tile
    fixed = lambda t, s: (0, 0)
    full = pl.BlockSpec((rows, width), fixed)
    side = pl.BlockSpec((rows, half), fixed)
    across = lambda t, s: (0, t)
    along = lambda t, s: (t, 0)
    shape = jax.ShapeDtypeStruct
    return pl.pallas_call(
        functools.partial(middle_kernel, spans, width // owners),
        grid_spec=pltpu.PrefetchScalarGridSpec(
            num_scalar_prefetch=1,
            grid=(tiles,),
            in_specs=[full, full, pl.BlockSpec((1, width), fixed)]
            + [pl.BlockSpec((half, width), fixed)] * 2
            + [pl.BlockSpec((rows, LANES), fixed)] * heads
            + [pl.BlockSpec((half, tile), across)] * 4
            + [pl.BlockSpec((tile, half), along)] * 2,
            out_specs=[full] * 3
            + [side] * 2
            + [pl.BlockSpec((1, width), fixed)]
            + [pl.BlockSpec((half, tile), across)] * 4
            + [pl.BlockSpec((tile, half), along)] * 2
            + [pl.BlockSpec((rows, LANES), fixed)] * heads,
            scratch_shapes=[
                pltpu.VMEM((rows, half), BF16),
                pltpu.VMEM((rows, half), BF16),
                pltpu.VMEM((half, rows), BF16),
                pltpu.VMEM((half, rows), BF16),
                pltpu.VMEM((rows, width), F32),
                pltpu.VMEM((rows, width), F32),
                pltpu.VMEM((rows, half), F32),
                pltpu.VMEM((rows, half), F32),
                pltpu.VMEM((rows, width), BF16),
            ],
        ),
        out_shape=[
            shape((rows, width), BF16),
            shape((rows, width), F32),
            shape((rows, width), BF16),
            shape((rows, half), BF16),
            shape((rows, half), BF16),
            shape((1, width), F32),
        ]
        + [shape((half, hidden), BF16)] * 4
        + [shape((hidden, half), BF16)] * 2
        + [shape((rows, LANES), BF16)] * heads,
        compiler_params=params(),
        cost_estimate=pl.CostEstimate(
            flops=55200000000, bytes_accessed=0, transcendentals=0
        ),
        name="middle",
    )(
        spot,
        x,
        dy,
        gain_row,
        *weight_out,
        *attended,
        *weight_gate,
        *weight_down,
    )


def last_kernel(spans, half, block, place_ref, x_ref, dx2_ref, gain_ref, h_ref, wa_ref, wb_ref, *refs):
    heads = x_ref.shape[1] // LANES
    pieces, refs = refs[:heads], refs[heads:]
    sa_ref, sb_ref, ka_ref, kb_ref, dx_ref, gain_grad_ref, d_scr, kept_scr, sent_scr, dh_scr = refs
    step = pl.program_id(0)

    @pl.when(step == 0)
    def _():
        kept, sent = core_split(h_ref[...].astype(F32), block, place_ref[1])
        kept_scr[...] = kept.T.astype(BF16)
        sent_scr[...] = sent.T.astype(BF16)
        dh_scr[...] = jnp.zeros_like(dh_scr)

    for k in range(spans):

        @pl.when((step % spans) ^ place_ref[0] == k)
        def _(k=k):
            for pair in range(heads // spans):
                d_scr[:, pair * LANES : (pair + 1) * LANES] = pieces[pair * spans + k][...]

    def work(w_ref, s_ref, k_ref):
        d = d_scr[...]
        s_ref[...] = jnp.dot(sent_scr[...], d, preferred_element_type=F32).astype(BF16)
        k_ref[...] = jnp.dot(kept_scr[...], d, preferred_element_type=F32).astype(BF16)
        dh_scr[...] += contract_last(d, w_ref[...])

    pl.when(step < half)(lambda: work(wa_ref, sa_ref, ka_ref))
    pl.when(step >= half)(lambda: work(wb_ref, sb_ref, kb_ref))

    @pl.when(step == pl.num_programs(0) - 1)
    def _():
        x = x_ref[...].astype(F32)
        inverse = lax.rsqrt(jnp.mean(x * x, axis=1, keepdims=True) + EPSILON)
        norm = x * inverse
        dh = dh_scr[...]
        gain_grad_ref[...] = jnp.sum(dh * norm, axis=0, keepdims=True)
        scaled = dh * gain_ref[...]
        inner = jnp.mean(scaled * norm, axis=1, keepdims=True)
        dx_ref[...] = (dx2_ref[...] + inverse * (scaled - norm * inner)).astype(BF16)


def last(spot, owners, spans, x, dx2, gain_row, normed, weights, pieces):
    rows, width = x.shape
    hw = width // spans
    half = 3 * spans // 2
    low = lambda t, s: (0, jnp.minimum(t, half - 1))
    high = lambda t, s: (0, jnp.maximum(t - half, 0))
    fixed = lambda t, s: (0, 0)
    full = pl.BlockSpec((rows, width), fixed)
    row = pl.BlockSpec((1, width), fixed)
    shape = jax.ShapeDtypeStruct
    return pl.pallas_call(
        functools.partial(last_kernel, spans, half, width // owners),
        grid_spec=pltpu.PrefetchScalarGridSpec(
            num_scalar_prefetch=1,
            grid=(3 * spans,),
            in_specs=[full, full, row, full]
            + [pl.BlockSpec((width, hw), low), pl.BlockSpec((width, hw), high)]
            + [pl.BlockSpec((rows, LANES), lambda t, s: (0, t // spans))] * len(pieces),
            out_specs=[
                pl.BlockSpec((width // 2, hw), low),
                pl.BlockSpec((width // 2, hw), high),
                pl.BlockSpec((width // 2, hw), low),
                pl.BlockSpec((width // 2, hw), high),
                full,
                row,
            ],
            scratch_shapes=[
                pltpu.VMEM((rows, hw), BF16),
                pltpu.VMEM((width // 2, rows), BF16),
                pltpu.VMEM((width // 2, rows), BF16),
                pltpu.VMEM((rows, width), F32),
            ],
        ),
        out_shape=[shape((width // 2, 3 * width // 2), BF16)] * 4
        + [shape((rows, width), BF16), shape((1, width), F32)],
        compiler_params=params(),
        cost_estimate=pl.CostEstimate(
            flops=21850000000, bytes_accessed=0, transcendentals=0
        ),
        name="last",
    )(spot, x, dx2, gain_row, normed, *weights, *pieces)


def adamw(weight, gradient, first, second, rate, factor):
    clipped = gradient * factor
    first_new = BETA_FIRST * first + (1.0 - BETA_FIRST) * clipped
    second_new = BETA_SECOND * second + (1.0 - BETA_SECOND) * clipped * clipped
    corrected_first = first_new / (1.0 - BETA_FIRST**STEP)
    corrected_second = second_new / (1.0 - BETA_SECOND**STEP)
    weight_new = weight - rate * (
        corrected_first / (jnp.sqrt(corrected_second) + ADAM_EPSILON) + DECAY * weight
    )
    return (first_new, second_new, weight_new)


def swap(values, axis, step):
    count = lax.axis_size(axis)
    return lax.ppermute(values, axis, [(i, i ^ step) for i in range(count)])


def paired():
    return lax.axis_size("seq") == 4


def group_place():
    if paired():
        return 2 * lax.axis_index("core") + lax.axis_index("seq") % 2
    return lax.axis_index("seq")


def group_swap(values, step):
    if not paired():
        return swap(values, "seq", step)
    spans = lax.axis_size("seq")
    pairs = [
        (c * spans + z, (c ^ (step >> 1)) * spans + (z ^ (step & 1)))
        for c in range(2)
        for z in range(spans)
    ]
    return lax.ppermute(values, ("core", "seq"), pairs)


def regroup(values):
    if not paired():
        return values
    spans = lax.axis_size("seq")
    pairs = [
        (c * spans + z, (z // 2) * spans + 2 * c + z % 2) for c in range(2) for z in range(spans)
    ]
    return lax.ppermute(values, ("core", "seq"), pairs)


def trade(pieces):
    return [pieces[0]] + [group_swap(pieces[k], k) for k in range(1, len(pieces))]


def bit_of(axis, step):
    return lax.axis_index(axis) & step


def ordered(own_bit, mine, other, at):
    return jnp.where(own_bit == 0, jnp.stack([mine, other], at), jnp.stack([other, mine], at))


def in_order(pieces, here):
    count = len(pieces)
    bits = count.bit_length() - 1
    stack = jnp.stack(pieces).reshape((2,) * bits + pieces[0].shape)
    for at in range(bits):
        flipped = jnp.flip(stack, axis=at)
        stack = jnp.where((here >> (bits - 1 - at)) & 1 == 1, flipped, stack)
    return stack.reshape((count,) + pieces[0].shape)


def chip_bits():
    count = lax.axis_size("chip")
    bits = [b for b in range(count.bit_length() - 1)]
    return bits, bits[::-1]


def halves_of(values):
    middle = values.shape[-1] // 2
    return (values[..., :middle], values[..., middle:])


def spread(values, axes):
    count = 1
    for axis in axes:
        count *= lax.axis_size(axis)
    copies = jnp.broadcast_to(values[None], (count,) + values.shape)
    return lax.all_to_all(copies, axes, split_axis=0, concat_axis=0, tiled=True)


def gather_line(shard, *gates):
    spans = lax.axis_size("seq")
    pieces = [shard] + [swap(shard, "seq", k) for k in range(1, spans)]
    pieces = after(pieces, gates)
    return in_order(pieces, lax.axis_index("seq")).reshape(-1, shard.shape[1])


def after(values, *tokens):
    return lax.optimization_barrier((values, tokens))[0]


def gather_chips(block, gate=None):
    parts, orders = halves_of(block), chip_bits()
    for at_step in range(len(orders[0])):
        if gate is not None and at_step == len(orders[0]) - 1:
            parts = after(parts, gate)
        others = [swap(half, "chip", 1 << order[at_step]) for half, order in zip(parts, orders)]
        parts = [
            ordered(
                bit_of("chip", 1 << order[at_step]),
                half,
                other,
                sum(1 for d in order[:at_step] if d > order[at_step]),
            )
            for half, other, order in zip(parts, others, orders)
        ]
    return [half.reshape(-1, half.shape[-1]) for half in parts]


def core_order(mine, other):
    chips, width = lax.axis_size("chip"), mine.shape[1]
    mine, other = mine.reshape(chips, -1, width), other.reshape(chips, -1, width)
    return ordered(lax.axis_index("core"), mine, other, 1).reshape(-1, width)


def core_sum(kept, sent, *gates):
    came = after([swap(other, "core", 1) for other in sent], gates)
    parts = [
        (mine.astype(F32) + other.astype(F32)).astype(BF16) for mine, other in zip(kept, came)
    ]
    return jnp.concatenate(parts, axis=-1)


def chips_scatter(values):
    return lax.psum_scatter(values, "chip", scatter_dimension=0, tiled=True)


def line_scatter(values):
    return lax.psum_scatter(values, "seq", scatter_dimension=0, tiled=True).astype(F32)


def direct_sum(values, axis):
    count, here = lax.axis_size(axis), lax.axis_index(axis)
    total = lax.dynamic_index_in_dim(values, here, 0, keepdims=False).astype(F32)
    for k in range(1, count):
        piece = lax.dynamic_index_in_dim(values, here ^ k, 0, keepdims=False)
        total = total + swap(piece, axis, k).astype(F32)
    return total


def line_sum(values):
    spans = lax.axis_size("seq")
    return direct_sum(values.reshape(spans, -1, values.shape[-1]), "seq")


def chips_sum(values):
    chips = lax.axis_size("chip")
    return direct_sum(values.reshape(chips, -1, values.shape[-1]), "chip").astype(BF16)


def outer(left, right):
    return lax.dot_general(left, right, (((0,), (0,)), ((), ())), preferred_element_type=F32)


def row_parts(gradient):
    width = gradient.shape[1]
    chips = lax.axis_size("chip")
    parts = gradient.reshape(chips, 2, -1, width)
    own = lax.axis_index("core") == 0
    kept = jnp.where(own, parts[:, 0], parts[:, 1]).reshape(-1, width)
    sent = jnp.where(own, parts[:, 1], parts[:, 0]).reshape(-1, width)
    return (kept, sent)


def place(index, values, slots):
    chosen = lax.broadcasted_iota(jnp.int32, (slots, index.shape[0]), 0) == index[None, :]
    return jnp.dot(chosen.astype(BF16), values, preferred_element_type=F32).astype(BF16)


def pick(index, values):
    slots = values.shape[0]
    chosen = lax.broadcasted_iota(jnp.int32, (index.shape[0], slots), 1) == index[:, None]
    return jnp.dot(chosen.astype(BF16), values, preferred_element_type=F32).astype(BF16)


def per_device(
    inputs,
    cotangent,
    target_slot,
    anchor_slot,
    sequence_start,
    attention_in,
    attention_out,
    gate_up,
    feed_down,
    norm_gains,
    first_in,
    first_out,
    first_gate,
    first_down,
    first_gains,
    second_in,
    second_out,
    second_gate,
    second_down,
    second_gains,
):
    owners = lax.axis_size("chip") * lax.axis_size("core")
    spans = lax.axis_size("seq")
    rows, width = inputs.shape
    per_owner = rows // owners
    capacity = per_owner + per_owner // 2
    slots = owners * capacity
    group = rows * spans
    here = group_place()
    device = (lax.axis_index("chip") * 2 + lax.axis_index("core")) * spans + lax.axis_index("seq")
    spot = jnp.stack([here, lax.axis_index("core")]).astype(jnp.int32)

    def exchange(values):
        return lax.all_to_all(values, ("chip", "core"), split_axis=0, concat_axis=0, tiled=True)

    pairs = width // spans // LANES

    def by_pair(pieces):
        return [pieces[p * spans : (p + 1) * spans] for p in range(pairs)]

    def joined(lists):
        return [piece for pieces in lists for piece in pieces]

    columns = norm_gains.shape[1]
    own_gains = jnp.pad(norm_gains.astype(BF16).reshape(1, -1), ((0, 7), (0, width - 2 * columns)))
    placed = jnp.concatenate(
        [
            place(target_slot, inputs, slots).reshape(owners, capacity, width),
            jnp.broadcast_to(own_gains[None], (owners, 8, width)),
        ],
        axis=1,
    )
    arrived = exchange(placed)
    gains_line = arrived[:, capacity, : 2 * columns]
    arrived = arrived[:, :capacity].reshape(slots, width)
    own_starts = regroup(sequence_start.reshape(1, rows))
    line_in = gather_line(attention_in.astype(BF16), placed)
    picked = pick(anchor_slot, arrived)
    balanced_in = regroup(picked)
    low = after((attention_out.astype(BF16), feed_down.astype(BF16)), line_in)
    line_out, line_down = [gather_line(shard) for shard in low]
    side_in = gather_chips(line_in, gate=(picked, line_out, line_down))
    weight_in = [core_order(half, swap(half, "core", 1)) for half in side_in]
    line_gate = gather_line(after(gate_up.astype(BF16), picked))
    late = after(cotangent, picked)
    arrived_late = exchange(place(target_slot, late, slots))
    gains_line = gains_line.astype(F32)
    gain_pieces = [gains_line] + [swap(gains_line, "seq", k) for k in range(1, spans)]
    gain_rows = in_order(gain_pieces, lax.axis_index("seq")).reshape(spans, owners, 2, columns)
    gain_rows = jnp.transpose(gain_rows, (2, 1, 0, 3)).reshape(2, width)

    own_starts = after(own_starts, line_in)
    pieces = [own_starts] + [group_swap(own_starts, k) for k in range(1, spans)]
    starts = in_order(pieces, here).reshape(group)
    cosine_all, sine_all = rope_tables((jnp.arange(group, dtype=jnp.int32) - starts).astype(F32))
    cosine = lax.dynamic_slice_in_dim(cosine_all, here * rows, rows, 0)
    sine = lax.dynamic_slice_in_dim(sine_all, here * rows, rows, 0)

    balanced_in = after(balanced_in, line_gate)
    normed_one, *cut = project(spot, balanced_in, gain_rows[0:1], weight_in, cosine, sine, spans)
    qkv = [trade(pieces) for pieces in by_pair(cut)]
    upstream = pick(anchor_slot, after(arrived_late, normed_one))
    side_gate = gather_chips(line_gate)
    qkv[-1] = after(qkv[-1], upstream)
    upstream = regroup(upstream)
    forward = [attend(spot, pieces, starts) for pieces in qkv]
    line_out, line_down = after((line_out, line_down), normed_one)
    side_out = gather_chips(line_out)
    side_down = gather_chips(line_down)
    side_gate, side_out, side_down = after((side_gate, side_out, side_down), forward[0])
    side_out = jnp.concatenate(side_out, axis=-1)
    weight_out = (side_out, swap(side_out, "core", 1))
    weight_down = [core_order(half, swap(half, "core", 1)) for half in side_down]
    weight_gate = side_gate + [swap(half, "core", 1) for half in side_gate]
    (
        result_low,
        middle_grad,
        branch_grad,
        attended_mine,
        attended_other,
        gain_two_grad,
        *rest,
    ) = middle(
        spot,
        owners,
        spans,
        balanced_in,
        upstream,
        gain_rows[1:2],
        weight_out,
        joined(trade(out[:spans]) for out in forward),
        weight_gate,
        weight_down,
    )
    gate_kept, gate_sent, down_grad, grad_cut = rest[:2], rest[2:4], rest[4:6], rest[6:]
    grad_heads = [trade(pieces) for pieces in by_pair(grad_cut)]
    grads = [attend_back(spot, qkv[0], starts, grad_heads[0], *forward[0][spans:], cosine_all, sine_all)]
    gate_both = core_sum(gate_kept, gate_sent, grads[0])
    down_both = core_sum(*zip(*(row_parts(half) for half in down_grad)), grads[0])
    result_slots = place(anchor_slot, after(regroup(result_low), grads[0]), slots)
    down_line = chips_scatter(down_both)
    gate_line = chips_scatter(gate_both)
    for p in range(1, pairs):
        do = after(grad_heads[p], gate_both, down_both, result_slots)
        grads.append(attend_back(spot, qkv[p], starts, do, *forward[p][spans:], cosine_all, sine_all))
    down_shard = line_scatter(after(down_line, grads[-1]))
    outputs = exchange(result_slots)
    middle_grad = after(middle_grad, outputs)
    sent_a, sent_b, kept_a, kept_b, input_low, gain_one_grad = last(
        spot,
        owners,
        spans,
        balanced_in,
        middle_grad,
        gain_rows[0:1],
        normed_one,
        weight_in,
        joined(trade(pieces) for pieces in grads),
    )
    outputs = pick(target_slot, after(outputs, input_low))
    gate_shard = line_scatter(after(gate_line, input_low))
    attended_mine, attended_other, branch_grad = after(
        (attended_mine, attended_other, branch_grad), input_low
    )
    out_both = core_sum(
        [outer(attended_mine, branch_grad).astype(BF16)],
        [outer(attended_other, branch_grad).astype(BF16)],
    )
    out_line = chips_sum(out_both)
    in_line = chips_sum(core_sum([kept_a, kept_b], [sent_a, sent_b]))
    out_shard = line_sum(out_line)
    in_shard = line_sum(in_line)
    input_low = regroup(input_low)
    input_gradient = pick(target_slot, exchange(place(anchor_slot, input_low, slots)))
    gain_one_grad, gain_two_grad = gain_one_grad.reshape(width), gain_two_grad.reshape(width)
    gain_parts = jnp.stack([gain_one_grad, gain_two_grad]).reshape(2, -1, columns)
    gain_parts = jnp.transpose(gain_parts, (1, 0, 2))
    gain_parts = lax.all_to_all(gain_parts, ROWS, split_axis=0, concat_axis=0, tiled=True)
    gain_shard = jnp.sum(gain_parts, axis=0)
    local_total = (
        jnp.sum(in_shard * in_shard)
        + jnp.sum(out_shard * out_shard)
        + jnp.sum(gate_shard * gate_shard)
        + jnp.sum(down_shard * down_shard)
        + jnp.sum(gain_shard * gain_shard)
    )
    total = jnp.sum(spread(jnp.broadcast_to(local_total, (8, LANES)), ROWS).reshape(-1, 8, LANES)[:, 0, 0])
    gradient_norm = jnp.sqrt(total)
    factor = CLIP / jnp.maximum(gradient_norm, CLIP)
    updates = []
    for weight, gradient, first, second, rate in (
        (attention_in, in_shard, first_in, second_in, D ** (-0.5)),
        (attention_out, out_shard, first_out, second_out, 0.5),
        (gate_up, gate_shard, first_gate, second_gate, D ** (-0.5)),
        (feed_down, down_shard, first_down, second_down, 2.0 * FF ** (-0.5)),
        (norm_gains, gain_shard, first_gains, second_gains, 1.5),
    ):
        updates.extend(adamw(weight, gradient, first, second, rate, factor))
    return (outputs, input_gradient, gradient_norm, *updates)


def solution(mesh):
    owners, spans = mesh.shape["dp"], mesh.shape["seq"]
    parts = Mesh(mesh.devices.reshape(owners // 2, 2, spans), ROWS)
    rows = P(ROWS, None)
    columns = P(None, ROWS)
    line = P(ROWS)
    in_specs = (rows, rows, line, line, line) + ((rows,) * 4 + (columns,)) * 3
    out_specs = (rows, rows, P()) + (rows,) * 12 + (columns,) * 3
    return jax.shard_map(
        per_device, mesh=parts, in_specs=in_specs, out_specs=out_specs, check_vma=False
    )
```

```python
import functools

import jax
import jax.numpy as jnp
from jax import lax
from jax.experimental import pallas as pl
from jax.experimental.pallas import tpu as pltpu
from jax.sharding import Mesh
from jax.sharding import PartitionSpec as P

D = 1024
HEAD = 64
FF = 2816
STEP = 10
LANES = 128

EPSILON = 1e-05
THETA = 500000.0
NEGATIVE = -1e30
BETA_FIRST = 0.9
BETA_SECOND = 0.95
ADAM_EPSILON = 1e-08
DECAY = 0.1
CLIP = 1.0
SCALE = 0.125
VMEM = 56 * 1024 * 1024
F32 = jnp.float32
BF16 = jnp.bfloat16
ROWS = ("chip", "core", "seq")


def norm_rows(values, gain_row):
    inverse = lax.rsqrt(jnp.mean(values * values, axis=1, keepdims=True) + EPSILON)
    normal = values * inverse
    return (normal * gain_row[None, :], normal, inverse)


def norm_back(upstream, normal, inverse, gain_row):
    gain_grad = jnp.sum(upstream * normal, axis=0)
    scaled = upstream * gain_row[None, :]
    return (
        inverse * (scaled - normal * jnp.mean(scaled * normal, axis=1, keepdims=True)),
        gain_grad,
    )


def rope_tables(positions):
    half_size = HEAD // 2
    frequency = jnp.power(THETA, -2.0 * jnp.arange(half_size, dtype=F32) / HEAD)
    angles = positions[:, None] * frequency[None, :]
    cosine = jnp.cos(angles)
    sine = jnp.sin(angles)
    return (
        jnp.concatenate([cosine] * 4, axis=1),
        jnp.concatenate([-sine, sine, -sine, sine], axis=1),
    )


def swap_halves(values):
    lane = lax.broadcasted_iota(jnp.int32, values.shape, 1)
    left = pltpu.roll(values, LANES - HEAD // 2, 1)
    right = pltpu.roll(values, HEAD // 2, 1)
    return jnp.where(lane % HEAD < HEAD // 2, left, right)


def contract_last(left, right):
    return lax.dot_general(left, right, (((1,), (1,)), ((), ())), preferred_element_type=F32)


def params():
    return pltpu.CompilerParams(vmem_limit_bytes=VMEM)


def turned(values):
    return values.astype(F32).T.astype(BF16)


def rows_at(index, count):
    return pl.ds(pl.multiple_of(index * count, count), count)


def project_kernel(spans, half, place_ref, x_ref, gain_ref, wa_ref, wb_ref, cos_ref, sin_ref, h_ref, *outs):
    step = pl.program_id(0)
    hw = wa_ref.shape[1]

    @pl.when(step == 0)
    def _():
        x = x_ref[...].astype(F32)
        inverse = lax.rsqrt(jnp.mean(x * x, axis=1, keepdims=True) + EPSILON)
        h_ref[...] = (x * inverse * gain_ref[...]).astype(BF16)

    def work(w_ref, rotated):
        acc = jnp.dot(h_ref[...], w_ref[...], preferred_element_type=F32)
        if rotated:
            pieces = []
            for c in range(hw // LANES):
                part = acc[:, c * LANES : (c + 1) * LANES]
                pieces.append(part * cos_ref[...] + swap_halves(part) * sin_ref[...])
            acc = jnp.concatenate(pieces, axis=1)
        low = acc.astype(BF16)
        for k in range(spans):

            @pl.when((step % spans) ^ place_ref[0] == k)
            def _(k=k):
                for pair in range(hw // LANES):
                    outs[pair * spans + k][...] = low[:, pair * LANES : (pair + 1) * LANES]

    turning = step < 2 * spans
    pl.when(step < half)(lambda: work(wa_ref, True))
    pl.when((step >= half) & turning)(lambda: work(wb_ref, True))
    pl.when(jnp.logical_not(turning))(lambda: work(wb_ref, False))


def project(spot, x, gain_row, weights, cosine, sine, spans):
    rows, width = x.shape
    hw = width // spans
    half = 3 * spans // 2
    fixed = lambda t, p: (0, 0)
    return pl.pallas_call(
        functools.partial(project_kernel, spans, half),
        grid_spec=pltpu.PrefetchScalarGridSpec(
            num_scalar_prefetch=1,
            grid=(3 * spans,),
            in_specs=[
                pl.BlockSpec((rows, width), fixed),
                pl.BlockSpec((1, width), fixed),
                pl.BlockSpec((width, hw), lambda t, p: (0, jnp.minimum(t, half - 1))),
                pl.BlockSpec((width, hw), lambda t, p: (0, jnp.maximum(t - half, 0))),
                pl.BlockSpec((rows, LANES), fixed),
                pl.BlockSpec((rows, LANES), fixed),
            ],
            out_specs=[pl.BlockSpec((rows, width), fixed)]
            + [pl.BlockSpec((rows, LANES), lambda t, p: (0, t // spans))] * (width // LANES),
        ),
        out_shape=[jax.ShapeDtypeStruct((rows, width), BF16)]
        + [jax.ShapeDtypeStruct((rows, 3 * LANES), BF16)] * (width // LANES),
        compiler_params=params(),
        cost_estimate=pl.CostEstimate(
            flops=17250000000, bytes_accessed=0, transcendentals=0
        ),
        name="project",
    )(spot, x, gain_row, *weights, cosine, sine)


def attend_kernel(spans, place_ref, start_ref, *refs):
    pieces, refs = refs[: 3 * spans], refs[3 * spans :]
    lows, (out_ref, log_ref, q_scr, k_scr, v_scr) = refs[:spans], refs[spans:]
    block = q_scr.shape[0] // spans
    here = place_ref[0]
    relative = pl.program_id(0)
    i = relative ^ here
    lane = lax.broadcasted_iota(jnp.int32, (block, LANES), 1)
    first = lane < HEAD

    @pl.when(relative == 0)
    def _():
        for k in range(spans):
            at = rows_at(here ^ k, block)
            q_scr[k * block : (k + 1) * block, :] = pieces[k][...]
            k_scr[at, :] = pieces[spans + k][...]
            v_scr[:, at] = turned(pieces[2 * spans + k][...])

    q_pair = q_scr[rows_at(relative, block), :] * SCALE
    key = lax.broadcasted_iota(jnp.int32, (block, block), 0)
    query = lax.broadcasted_iota(jnp.int32, (block, block), 1)
    starts = start_ref[:, rows_at(i, block)]
    heads = []
    for head in range(2):
        mine = first if head == 0 else jnp.logical_not(first)
        heads.append(jnp.where(mine, q_pair, jnp.zeros_like(q_pair)))

    def visit(j, carry, diagonal):
        at = rows_at(j, block)
        k = k_scr[at, :]
        seen = key + j * block >= starts
        if diagonal:
            seen = seen & (key <= query)
        result = []
        for head in range(2):
            s = jnp.where(seen, contract_last(k, heads[head]), NEGATIVE)
            lines = slice(head * HEAD, (head + 1) * HEAD)
            new = jnp.max(s, axis=0, keepdims=True)
            if not diagonal:
                top, total, acc = carry[head]
                new = jnp.maximum(top, new)
            p = jnp.exp(s - new)
            added = jnp.sum(p, axis=0, keepdims=True)
            weighed = jnp.dot(v_scr[lines, at], p.astype(BF16), preferred_element_type=F32)
            if not diagonal:
                factor = jnp.exp(top - new)
                added = added + total * factor
                weighed = weighed + acc * factor
            result.append((new, added, weighed))
        return tuple(result)

    carry = visit(i, None, True)
    carry = lax.fori_loop(0, i, lambda j, c: visit(j, c, False), carry)
    parts = []
    for head in range(2):
        top, total, acc = carry[head]
        parts.append(acc / total)
        log_ref[head : head + 1, :] = top + jnp.log(total)
    out = jnp.concatenate(parts, axis=0).T
    out_ref[0] = out
    low = out.astype(BF16)
    for k in range(spans):

        @pl.when(relative == k)
        def _(k=k):
            lows[k][...] = low


def piece_specs(rows, spans):
    return [
        pl.BlockSpec((rows, LANES), functools.partial(lambda part, i, s: (0, part), part))
        for part in range(3)
        for _ in range(spans)
    ]


def attend(spot, qkv, starts):
    spans = len(qkv)
    rows = qkv[0].shape[0]
    group = rows * spans
    return pl.pallas_call(
        functools.partial(attend_kernel, spans),
        grid_spec=pltpu.PrefetchScalarGridSpec(
            num_scalar_prefetch=1,
            grid=(spans,),
            in_specs=[pl.BlockSpec((1, group), lambda i, s: (0, 0))] + piece_specs(rows, spans),
            out_specs=[pl.BlockSpec((rows, LANES), lambda i, s: (0, 0))] * spans
            + [
                pl.BlockSpec((1, rows, LANES), lambda i, s: (i, 0, 0)),
                pl.BlockSpec((8, rows), lambda i, s: (0, i ^ s[0])),
            ],
            scratch_shapes=[
                pltpu.VMEM((group, LANES), BF16),
                pltpu.VMEM((group, LANES), BF16),
                pltpu.VMEM((LANES, group), BF16),
            ],
        ),
        out_shape=[jax.ShapeDtypeStruct((rows, LANES), BF16)] * spans
        + [
            jax.ShapeDtypeStruct((spans, rows, LANES), F32),
            jax.ShapeDtypeStruct((8, group), F32),
        ],
        compiler_params=params(),
        cost_estimate=pl.CostEstimate(
            flops=18400000000, bytes_accessed=0, transcendentals=0
        ),
        name="attend",
    )(spot, starts.reshape(1, group), *(list(qkv) * 3))


def attend_back_kernel(spans, place_ref, start_ref, *refs):
    pieces, refs = refs[: 3 * spans], refs[3 * spans :]
    grads, refs = refs[:spans], refs[spans:]
    (out_ref, log_ref, cos_ref, sin_ref), refs = refs[:4], refs[4:]
    outs, refs = refs[:spans], refs[spans:]
    q_scr, k_scr, v_scr, do_scr, dq_scr, dk_scr, dv_scr, delta_ref, turned_ref = refs
    block = q_scr.shape[0] // spans
    here = place_ref[0]
    j = pl.program_id(0)
    lane = lax.broadcasted_iota(jnp.int32, (block, LANES), 1)
    first = lane < HEAD

    @pl.when(j == 0)
    def _():
        for k in range(spans):
            at = rows_at(here ^ k, block)
            q_scr[at, :] = pieces[k][...]
            k_scr[at, :] = pieces[spans + k][...]
            v_scr[at, :] = pieces[2 * spans + k][...]
            do = grads[k][...]
            do_scr[at, :] = do
            product = (do.astype(F32) * out_ref[k]).T
            delta_ref[0:1, at] = jnp.sum(product[:HEAD], axis=0, keepdims=True)
            delta_ref[1:2, at] = jnp.sum(product[HEAD:], axis=0, keepdims=True)
        turned_ref[...] = jnp.zeros_like(turned_ref)

    now = rows_at(j, block)
    k_pair = k_scr[now, :]
    v_pair = v_scr[now, :]
    k_turned = turned(k_pair)
    key = j * block + lax.broadcasted_iota(jnp.int32, (block, block), 0)
    query = lax.broadcasted_iota(jnp.int32, (block, block), 1)

    def visit(i, carry, diagonal):
        dk, dv = carry
        at = rows_at(i, block)
        q_pair = q_scr[at, :] * SCALE
        do_pair = do_scr[at, :]
        seen = key >= start_ref[:, at]
        if diagonal:
            seen = seen & (key <= query + i * block)
        for head in range(2):
            mine = first if head == 0 else jnp.logical_not(first)
            q = jnp.where(mine, q_pair, jnp.zeros_like(q_pair))
            do = jnp.where(mine, do_pair, jnp.zeros_like(do_pair))
            s = jnp.where(seen, contract_last(k_pair, q), NEGATIVE)
            p = jnp.exp(s - log_ref[head : head + 1, at])
            dp = contract_last(v_pair, do)
            ds = (p * (dp - delta_ref[head : head + 1, at])).astype(BF16)
            dv = dv + jnp.dot(p.astype(BF16), do, preferred_element_type=F32)
            dk = dk + jnp.dot(ds, q, preferred_element_type=F32)
            lines = slice(head * HEAD, (head + 1) * HEAD)
            turned_ref[lines, at] += jnp.dot(k_turned[lines], ds, preferred_element_type=F32)
        return (dk, dv)

    zero = jnp.zeros((block, LANES), F32)
    carry = visit(j, (zero, zero), True)
    dk, dv = lax.fori_loop(j + 1, spans, lambda i, c: visit(i, c, False), carry)

    def turn_back(values, at):
        return values * cos_ref[at, :] + swap_halves(values * sin_ref[at, :])

    dk_scr[now, :] = turn_back(dk, now).astype(BF16)
    dv_scr[now, :] = dv.astype(BF16)

    @pl.when(j == spans - 1)
    def _():
        def finish(i, carry):
            at = rows_at(i, block)
            dq_scr[at, :] = turn_back(turned_ref[:, at].T * SCALE, at).astype(BF16)
            return carry

        lax.fori_loop(0, spans, finish, 0)
        for k in range(spans):
            at = rows_at(here ^ k, block)
            for part, scr in enumerate((dq_scr, dk_scr, dv_scr)):
                outs[k][:, part * LANES : (part + 1) * LANES] = scr[at, :]


def attend_back(spot, pair, qkv, starts, grads, out, logs, cosine, sine):
    spans = len(qkv)
    rows = qkv[0].shape[0]
    group = rows * spans
    whole = lambda j, s: (0, 0)
    low = pltpu.VMEM((group, LANES), BF16)
    return pl.pallas_call(
        functools.partial(attend_back_kernel, spans),
        grid_spec=pltpu.PrefetchScalarGridSpec(
            num_scalar_prefetch=1,
            grid=(spans,),
            in_specs=[pl.BlockSpec((1, group), whole)]
            + piece_specs(rows, spans)
            + [pl.BlockSpec((rows, LANES), lambda j, s: (0, pair))] * spans
            + [
                pl.BlockSpec((spans, rows, LANES), lambda j, s: (0, 0, 0)),
                pl.BlockSpec((8, group), whole),
                pl.BlockSpec((group, LANES), whole),
                pl.BlockSpec((group, LANES), whole),
            ],
            out_specs=[pl.BlockSpec((rows, 3 * LANES), whole)] * spans,
            scratch_shapes=[low] * 7 + [pltpu.VMEM((8, group), F32), pltpu.VMEM((LANES, group), F32)],
        ),
        out_shape=[jax.ShapeDtypeStruct((rows, 3 * LANES), BF16)] * spans,
        compiler_params=params(),
        cost_estimate=pl.CostEstimate(
            flops=27600000000, bytes_accessed=0, transcendentals=0
        ),
        name="attend_back",
    )(spot, starts.reshape(1, group), *(list(qkv) * 3), *grads, out, logs, cosine, sine)


def core_split(values, block, own):
    width = values.shape[1]
    sides = []
    for core in range(2):
        blocks = [values[:, b * block : (b + 1) * block] for b in range(core, width // block, 2)]
        sides.append(jnp.concatenate(blocks, axis=1))
    return (jnp.where(own == 0, sides[0], sides[1]), jnp.where(own == 0, sides[1], sides[0]))


def core_merge(mine, other, block, own):
    sides = (jnp.where(own == 0, mine, other), jnp.where(own == 0, other, mine))
    blocks = mine.shape[1] // block
    return jnp.concatenate(
        [side[:, b * block : (b + 1) * block] for b in range(blocks) for side in sides], axis=1
    )


def middle_kernel(spans, block, place_ref, x_ref, dy_ref, gain_ref, om_ref, oo_ref, *refs):
    heads = x_ref.shape[1] // LANES
    attended, refs = refs[:heads], refs[heads:]
    (gm_ref, um_ref, go_ref, uo_ref, da_ref, db_ref), refs = refs[:6], refs[6:]
    (y_ref, dx_ref, branch_ref, ow_ref, ox_ref, gain_grad_ref), refs = refs[:6], refs[6:]
    (gk_ref, uk_ref, gs_ref, us_ref, ga_ref, gb_ref), refs = refs[:6], refs[6:]
    grads, refs = refs[:spans], refs[spans:]
    hm_scr, ho_scr, kept_scr, sent_scr, x2_scr, y_scr, dm_scr, do_scr, wide_scr = refs
    step, steps = pl.program_id(0), pl.num_programs(0)
    half = x_ref.shape[1] // 2
    here, core = place_ref[0], place_ref[1]

    def pieces_at(pieces):
        for index, piece in enumerate(pieces):
            pair, k = index // spans, index % spans
            yield rows_at((here ^ k) * (heads // spans) + pair, LANES), piece

    hw = x_ref.shape[1] // spans

    def normal():
        x2 = x2_scr[...]
        inverse = lax.rsqrt(jnp.mean(x2 * x2, axis=1, keepdims=True) + EPSILON)
        return (x2 * inverse, inverse)

    @pl.when(step == 0)
    def _():
        for at, piece in pieces_at(attended):
            wide_scr[:, at] = piece[...]
        mine, other = core_split(wide_scr[...], block, core)
        ow_ref[...] = mine
        ox_ref[...] = other
        x2_scr[...] = (
            x_ref[...].astype(F32)
            + jnp.dot(mine, om_ref[...], preferred_element_type=F32)
            + jnp.dot(other, oo_ref[...], preferred_element_type=F32)
        )
        h = (normal()[0] * gain_ref[...]).astype(BF16).astype(F32)
        mine, other = core_split(h, block, core)
        hm_scr[...] = mine.astype(BF16)
        ho_scr[...] = other.astype(BF16)
        kept_scr[...] = mine.T.astype(BF16)
        sent_scr[...] = other.T.astype(BF16)
        y_scr[...] = jnp.zeros_like(y_scr)
        dm_scr[...] = jnp.zeros_like(dm_scr)
        do_scr[...] = jnp.zeros_like(do_scr)

    hm, ho, dy = hm_scr[...], ho_scr[...], dy_ref[...]
    gm, um, go, uo = gm_ref[...], um_ref[...], go_ref[...], uo_ref[...]
    gate = jnp.dot(hm, gm, preferred_element_type=F32) + jnp.dot(ho, go, preferred_element_type=F32)
    up = jnp.dot(hm, um, preferred_element_type=F32) + jnp.dot(ho, uo, preferred_element_type=F32)
    share = jax.nn.sigmoid(gate)
    active = gate * share
    hidden_full = active * up
    hidden = hidden_full.astype(BF16)
    down = jnp.concatenate([da_ref[...], db_ref[...]], axis=1)
    y_scr[...] += jnp.dot(hidden, down, preferred_element_type=F32)
    dhid = contract_last(dy, down)
    dgate = (dhid * up * share * (1.0 + gate * (1.0 - share))).astype(BF16)
    dup = (dhid * active).astype(BF16)
    dm_scr[...] += contract_last(dgate, gm) + contract_last(dup, um)
    do_scr[...] += contract_last(dgate, go) + contract_last(dup, uo)
    kept, sent = kept_scr[...], sent_scr[...]
    gs_ref[...] = jnp.dot(sent, dgate, preferred_element_type=F32).astype(BF16)
    us_ref[...] = jnp.dot(sent, dup, preferred_element_type=F32).astype(BF16)
    gk_ref[...] = jnp.dot(kept, dgate, preferred_element_type=F32).astype(BF16)
    uk_ref[...] = jnp.dot(kept, dup, preferred_element_type=F32).astype(BF16)
    hidden_turned = hidden_full.T.astype(BF16)
    ga_ref[...] = jnp.dot(hidden_turned, dy[:, :half], preferred_element_type=F32).astype(BF16)
    gb_ref[...] = jnp.dot(hidden_turned, dy[:, half:], preferred_element_type=F32).astype(BF16)

    @pl.when(step == steps - 1)
    def _():
        y_ref[...] = (x2_scr[...] + y_scr[...]).astype(BF16)
        norm, inverse = normal()
        dh = core_merge(dm_scr[...], do_scr[...], block, core)
        gain_grad_ref[...] = jnp.sum(dh * norm, axis=0, keepdims=True)
        scaled = dh * gain_ref[...]
        inner = jnp.mean(scaled * norm, axis=1, keepdims=True)
        dx = dy_ref[...].astype(F32) + inverse * (scaled - norm * inner)
        dx_ref[...] = dx
        branch = dx.astype(BF16)
        branch_ref[...] = branch
        mine = contract_last(branch, om_ref[...]).astype(BF16)
        other = contract_last(branch, oo_ref[...]).astype(BF16)
        wide_scr[...] = core_merge(mine, other, block, core)
        for k in range(spans):
            grads[k][...] = wide_scr[:, rows_at(here ^ k, hw)]


def middle(spot, owners, spans, x, dy, gain_row, weight_out, attended, weight_gate, weight_down):
    rows, width = x.shape
    hidden = weight_gate[0].shape[1]
    heads, half, tile = width // LANES, width // 2, 2 * LANES
    tiles = hidden // tile
    fixed = lambda t, s: (0, 0)
    full = pl.BlockSpec((rows, width), fixed)
    side = pl.BlockSpec((rows, half), fixed)
    across = lambda t, s: (0, t)
    along = lambda t, s: (t, 0)
    shape = jax.ShapeDtypeStruct
    return pl.pallas_call(
        functools.partial(middle_kernel, spans, width // owners),
        grid_spec=pltpu.PrefetchScalarGridSpec(
            num_scalar_prefetch=1,
            grid=(tiles,),
            in_specs=[full, full, pl.BlockSpec((1, width), fixed)]
            + [pl.BlockSpec((half, width), fixed)] * 2
            + [pl.BlockSpec((rows, LANES), fixed)] * heads
            + [pl.BlockSpec((half, tile), across)] * 4
            + [pl.BlockSpec((tile, half), along)] * 2,
            out_specs=[full] * 3
            + [side] * 2
            + [pl.BlockSpec((1, width), fixed)]
            + [pl.BlockSpec((half, tile), across)] * 4
            + [pl.BlockSpec((tile, half), along)] * 2
            + [pl.BlockSpec((rows, width // spans), fixed)] * spans,
            scratch_shapes=[
                pltpu.VMEM((rows, half), BF16),
                pltpu.VMEM((rows, half), BF16),
                pltpu.VMEM((half, rows), BF16),
                pltpu.VMEM((half, rows), BF16),
                pltpu.VMEM((rows, width), F32),
                pltpu.VMEM((rows, width), F32),
                pltpu.VMEM((rows, half), F32),
                pltpu.VMEM((rows, half), F32),
                pltpu.VMEM((rows, width), BF16),
            ],
        ),
        out_shape=[
            shape((rows, width), BF16),
            shape((rows, width), F32),
            shape((rows, width), BF16),
            shape((rows, half), BF16),
            shape((rows, half), BF16),
            shape((1, width), F32),
        ]
        + [shape((half, hidden), BF16)] * 4
        + [shape((hidden, half), BF16)] * 2
        + [shape((rows, width // spans), BF16)] * spans,
        compiler_params=params(),
        cost_estimate=pl.CostEstimate(
            flops=55200000000, bytes_accessed=0, transcendentals=0
        ),
        name="middle",
    )(
        spot,
        x,
        dy,
        gain_row,
        *weight_out,
        *attended,
        *weight_gate,
        *weight_down,
    )


def last_kernel(spans, half, block, place_ref, x_ref, dx2_ref, gain_ref, second_ref, h_ref, wa_ref, wb_ref, *refs):
    heads = x_ref.shape[1] // LANES
    pieces, refs = refs[:heads], refs[heads:]
    sa_ref, sb_ref, ka_ref, kb_ref, dx_ref, gk_ref, gs_ref, d_scr, kept_scr, sent_scr, dh_scr = refs
    step = pl.program_id(0)

    @pl.when(step == 0)
    def _():
        kept, sent = core_split(h_ref[...].astype(F32), block, place_ref[1])
        kept_scr[...] = kept.T.astype(BF16)
        sent_scr[...] = sent.T.astype(BF16)
        dh_scr[...] = jnp.zeros_like(dh_scr)

    for k in range(spans):

        @pl.when((step % spans) ^ place_ref[0] == k)
        def _(k=k):
            for pair in range(heads // spans):
                d_scr[:, pair * LANES : (pair + 1) * LANES] = pieces[pair * spans + k][...]

    def work(w_ref, s_ref, k_ref):
        d = d_scr[...]
        s_ref[...] = jnp.dot(sent_scr[...], d, preferred_element_type=F32).astype(BF16)
        k_ref[...] = jnp.dot(kept_scr[...], d, preferred_element_type=F32).astype(BF16)
        dh_scr[...] += contract_last(d, w_ref[...])

    pl.when(step < half)(lambda: work(wa_ref, sa_ref, ka_ref))
    pl.when(step >= half)(lambda: work(wb_ref, sb_ref, kb_ref))

    @pl.when(step == pl.num_programs(0) - 1)
    def _():
        x = x_ref[...].astype(F32)
        inverse = lax.rsqrt(jnp.mean(x * x, axis=1, keepdims=True) + EPSILON)
        norm = x * inverse
        dh = dh_scr[...]
        row = lax.broadcasted_iota(jnp.int32, (LANES, x.shape[1]), 0)
        gains = jnp.where(row == 0, jnp.sum(dh * norm, axis=0, keepdims=True), 0.0)
        gains = jnp.where(row == 1, second_ref[...], gains)
        kept, sent = core_split(gains, block, place_ref[1])
        gk_ref[...] = kept.T.astype(BF16)
        gs_ref[...] = sent.T.astype(BF16)
        scaled = dh * gain_ref[...]
        inner = jnp.mean(scaled * norm, axis=1, keepdims=True)
        dx_ref[...] = (dx2_ref[...] + inverse * (scaled - norm * inner)).astype(BF16)


def last(spot, owners, spans, x, dx2, gain_row, gain_two_grad, normed, weights, pieces):
    rows, width = x.shape
    hw = width // spans
    half = 3 * spans // 2
    low = lambda t, s: (0, jnp.minimum(t, half - 1))
    high = lambda t, s: (0, jnp.maximum(t - half, 0))
    fixed = lambda t, s: (0, 0)
    full = pl.BlockSpec((rows, width), fixed)
    row = pl.BlockSpec((1, width), fixed)
    shape = jax.ShapeDtypeStruct
    return pl.pallas_call(
        functools.partial(last_kernel, spans, half, width // owners),
        grid_spec=pltpu.PrefetchScalarGridSpec(
            num_scalar_prefetch=1,
            grid=(3 * spans,),
            in_specs=[full, full, row, row, full]
            + [pl.BlockSpec((width, hw), low), pl.BlockSpec((width, hw), high)]
            + [pl.BlockSpec((rows, LANES), lambda t, s: (0, t // spans))] * len(pieces),
            out_specs=[
                pl.BlockSpec((width // 2, hw), low),
                pl.BlockSpec((width // 2, hw), high),
                pl.BlockSpec((width // 2, hw), low),
                pl.BlockSpec((width // 2, hw), high),
                full,
                pl.BlockSpec((width // 2, LANES), fixed),
                pl.BlockSpec((width // 2, LANES), fixed),
            ],
            scratch_shapes=[
                pltpu.VMEM((rows, hw), BF16),
                pltpu.VMEM((width // 2, rows), BF16),
                pltpu.VMEM((width // 2, rows), BF16),
                pltpu.VMEM((rows, width), F32),
            ],
        ),
        out_shape=[shape((width // 2, 3 * width // 2), BF16)] * 4
        + [shape((rows, width), BF16)]
        + [shape((width // 2, LANES), BF16)] * 2,
        compiler_params=params(),
        cost_estimate=pl.CostEstimate(
            flops=21850000000, bytes_accessed=0, transcendentals=0
        ),
        name="last",
    )(spot, x, dx2, gain_row, gain_two_grad, normed, *weights, *pieces)


def adamw(weight, gradient, first, second, rate, factor):
    clipped = gradient * factor
    first_new = BETA_FIRST * first + (1.0 - BETA_FIRST) * clipped
    second_new = BETA_SECOND * second + (1.0 - BETA_SECOND) * clipped * clipped
    corrected_first = first_new / (1.0 - BETA_FIRST**STEP)
    corrected_second = second_new / (1.0 - BETA_SECOND**STEP)
    weight_new = weight - rate * (
        corrected_first / (jnp.sqrt(corrected_second) + ADAM_EPSILON) + DECAY * weight
    )
    return (first_new, second_new, weight_new)


def swap(values, axis, step):
    count = lax.axis_size(axis)
    return lax.ppermute(values, axis, [(i, i ^ step) for i in range(count)])


def paired():
    return lax.axis_size("seq") == 4


def group_place():
    if paired():
        return 2 * lax.axis_index("core") + lax.axis_index("seq") % 2
    return lax.axis_index("seq")


def group_swap(values, step):
    if not paired():
        return swap(values, "seq", step)
    spans = lax.axis_size("seq")
    pairs = [
        (c * spans + z, (c ^ (step >> 1)) * spans + (z ^ (step & 1)))
        for c in range(2)
        for z in range(spans)
    ]
    return lax.ppermute(values, ("core", "seq"), pairs)


def regroup(values, *gates):
    if not paired():
        return values
    spans = lax.axis_size("seq")
    pairs = [
        (c * spans + z, (z // 2) * spans + 2 * c + z % 2)
        for c in range(2)
        for z in range(spans)
        if c != z // 2
    ]
    stays = lax.axis_index("core") == lax.axis_index("seq") // 2
    came = after(lax.ppermute(values, ("core", "seq"), pairs), gates)
    return jnp.where(stays, values, came)


def trade(pieces, *gates):
    return [pieces[0], *after([group_swap(pieces[k], k) for k in range(1, len(pieces))], gates)]


def bit_of(axis, step):
    return lax.axis_index(axis) & step


def ordered(own_bit, mine, other, at):
    return jnp.where(own_bit == 0, jnp.stack([mine, other], at), jnp.stack([other, mine], at))


def in_order(pieces, here):
    count = len(pieces)
    bits = count.bit_length() - 1
    stack = jnp.stack(pieces).reshape((2,) * bits + pieces[0].shape)
    for at in range(bits):
        flipped = jnp.flip(stack, axis=at)
        stack = jnp.where((here >> (bits - 1 - at)) & 1 == 1, flipped, stack)
    return stack.reshape((count,) + pieces[0].shape)


def chip_bits():
    count = lax.axis_size("chip")
    bits = [b for b in range(count.bit_length() - 1)]
    return bits, bits[::-1]


def halves_of(values):
    middle = values.shape[-1] // 2
    return (values[..., :middle], values[..., middle:])


def spread(values, axes):
    count = 1
    for axis in axes:
        count *= lax.axis_size(axis)
    copies = jnp.broadcast_to(values[None], (count,) + values.shape)
    return lax.all_to_all(copies, axes, split_axis=0, concat_axis=0, tiled=True)


def gather_line(shard, *gates):
    spans = lax.axis_size("seq")
    pieces = [shard] + [swap(shard, "seq", k) for k in range(1, spans)]
    pieces = after(pieces, gates)
    return in_order(pieces, lax.axis_index("seq")).reshape(-1, shard.shape[1])


def after(values, *tokens):
    return lax.optimization_barrier((values, tokens))[0]


def gather_chips(block, gate=None, came=()):
    parts, orders = halves_of(block), chip_bits()
    for at_step in range(len(orders[0])):
        if gate is not None and at_step == len(orders[0]) - 1:
            parts = after(parts, gate)
        others = [swap(half, "chip", 1 << order[at_step]) for half, order in zip(parts, orders)]
        if at_step < len(came):
            others = after(others, came[at_step])
        parts = [
            ordered(
                bit_of("chip", 1 << order[at_step]),
                half,
                other,
                sum(1 for d in order[:at_step] if d > order[at_step]),
            )
            for half, other, order in zip(parts, others, orders)
        ]
    return [half.reshape(-1, half.shape[-1]) for half in parts]


def core_order(mine, other):
    chips, width = lax.axis_size("chip"), mine.shape[1]
    mine, other = mine.reshape(chips, -1, width), other.reshape(chips, -1, width)
    return ordered(lax.axis_index("core"), mine, other, 1).reshape(-1, width)


def core_sum(kept, sent, *gates):
    came = after([swap(other, "core", 1) for other in sent], gates)
    parts = [
        (mine.astype(F32) + other.astype(F32)).astype(BF16) for mine, other in zip(kept, came)
    ]
    return jnp.concatenate(parts, axis=-1)


def chips_scatter(values):
    return lax.psum_scatter(values, "chip", scatter_dimension=0, tiled=True)


def line_scatter(values):
    return lax.psum_scatter(values, "seq", scatter_dimension=0, tiled=True).astype(F32)


def direct_sum(values, axis, *gates):
    count, here = lax.axis_size(axis), lax.axis_index(axis)
    total = lax.dynamic_index_in_dim(values, here, 0, keepdims=False).astype(F32)
    pieces = [
        swap(lax.dynamic_index_in_dim(values, here ^ k, 0, keepdims=False), axis, k)
        for k in range(1, count)
    ]
    for piece in after(pieces, gates):
        total = total + piece.astype(F32)
    return total


def line_sum(values):
    spans = lax.axis_size("seq")
    return direct_sum(values.reshape(spans, -1, values.shape[-1]), "seq")


def chips_sum(values, *gates):
    chips = lax.axis_size("chip")
    return direct_sum(values.reshape(chips, -1, values.shape[-1]), "chip", *gates).astype(BF16)


def outer(left, right):
    return lax.dot_general(left, right, (((0,), (0,)), ((), ())), preferred_element_type=F32)


def row_parts(gradient):
    width = gradient.shape[1]
    chips = lax.axis_size("chip")
    parts = gradient.reshape(chips, 2, -1, width)
    own = lax.axis_index("core") == 0
    kept = jnp.where(own, parts[:, 0], parts[:, 1]).reshape(-1, width)
    sent = jnp.where(own, parts[:, 1], parts[:, 0]).reshape(-1, width)
    return (kept, sent)


def place(index, values, slots):
    chosen = lax.broadcasted_iota(jnp.int32, (slots, index.shape[0]), 0) == index[None, :]
    return jnp.dot(chosen.astype(BF16), values, preferred_element_type=F32).astype(BF16)


def pick(index, values):
    slots = values.shape[0]
    chosen = lax.broadcasted_iota(jnp.int32, (index.shape[0], slots), 1) == index[:, None]
    return jnp.dot(chosen.astype(BF16), values, preferred_element_type=F32).astype(BF16)


def per_device(
    inputs,
    cotangent,
    target_slot,
    anchor_slot,
    sequence_start,
    attention_in,
    attention_out,
    gate_up,
    feed_down,
    norm_gains,
    first_in,
    first_out,
    first_gate,
    first_down,
    first_gains,
    second_in,
    second_out,
    second_gate,
    second_down,
    second_gains,
):
    owners = lax.axis_size("chip") * lax.axis_size("core")
    spans = lax.axis_size("seq")
    rows, width = inputs.shape
    per_owner = rows // owners
    capacity = per_owner + per_owner // 2
    slots = owners * capacity
    group = rows * spans
    here = group_place()
    device = (lax.axis_index("chip") * 2 + lax.axis_index("core")) * spans + lax.axis_index("seq")
    spot = jnp.stack([here, lax.axis_index("core")]).astype(jnp.int32)

    def exchange(values):
        return lax.all_to_all(values, ("chip", "core"), split_axis=0, concat_axis=0, tiled=True)

    pairs = width // spans // LANES

    def by_pair(pieces):
        return [pieces[p * spans : (p + 1) * spans] for p in range(pairs)]

    def joined(lists):
        return [piece for pieces in lists for piece in pieces]

    columns = norm_gains.shape[1]
    own_gains = jnp.pad(norm_gains.astype(BF16).reshape(1, -1), ((0, 7), (0, width - 2 * columns)))
    placed = jnp.concatenate(
        [
            place(target_slot, inputs, slots).reshape(owners, capacity, width),
            jnp.broadcast_to(own_gains[None], (owners, 8, width)),
        ],
        axis=1,
    )
    arrived = exchange(placed)
    gains_line = arrived[:, capacity, : 2 * columns]
    arrived = arrived[:, :capacity].reshape(slots, width)
    line_in = gather_line(attention_in.astype(BF16), placed)
    picked = pick(anchor_slot, arrived)
    balanced_in = regroup(picked)
    line_gate = gather_line(gate_up.astype(BF16), picked)
    side_in = gather_chips(line_in, gate=picked)
    line_gate_late = after(line_gate, side_in, balanced_in)
    core_in = after(side_in, line_gate)
    own_starts = regroup(sequence_start.reshape(1, rows), side_in)
    straight = jnp.concatenate([attention_out.astype(BF16), feed_down.astype(BF16)], axis=0)
    side_rest = lax.all_gather(after(straight, side_in), ("chip", "seq"), axis=0, tiled=True)
    weight_in = [core_order(half, swap(half, "core", 1)) for half in core_in]
    gains_line = after(gains_line.astype(F32), side_in)
    gain_pieces = [gains_line] + [swap(gains_line, "seq", k) for k in range(1, spans)]
    gain_rows = in_order(gain_pieces, lax.axis_index("seq")).reshape(spans, owners, 2, columns)
    gain_rows = jnp.transpose(gain_rows, (2, 1, 0, 3)).reshape(2, width)

    own_starts = after(own_starts, balanced_in).reshape(rows)
    local = here * rows + jnp.arange(rows, dtype=jnp.int32) - own_starts
    cosine, sine = rope_tables(local.astype(F32))

    normed_one, *cut = project(spot, balanced_in, gain_rows[0:1], weight_in, cosine, sine, spans)
    cuts = by_pair(cut)
    qkv = [trade(cuts[0])]
    pieces = trade([own_starts.reshape(1, rows)] * spans, normed_one)
    starts = in_order(pieces, here).reshape(group)
    late = after(cotangent, normed_one)
    arrived_late = exchange(place(target_slot, late, slots))
    upstream = pick(anchor_slot, arrived_late)
    own_rows = attention_out.shape[0]

    def cut_rest(rest):
        rest = rest.reshape(-1, straight.shape[0], width)
        return [rest[:, :own_rows].reshape(-1, width), rest[:, own_rows:].reshape(-1, width)]

    forward = [attend(spot, after(qkv[0], upstream), starts)]
    upstream = regroup(upstream)
    positions = jnp.arange(group, dtype=jnp.int32) - after(starts, forward[0])
    cosine_all, sine_all = rope_tables(positions.astype(F32))
    side_rest = after(side_rest, forward[0])
    other_rest = swap(side_rest, "core", 1)
    side_rest = cut_rest(side_rest)
    for pieces in cuts[1:]:
        qkv.append(trade(pieces, forward[0]))
        forward.append(attend(spot, after(qkv[-1], upstream, side_rest), starts))
    side_gate = gather_chips(line_gate_late, came=(normed_one, forward[-1]))
    other_rest = cut_rest(after(other_rest, forward[-1]))
    weight_out = (side_rest[0], other_rest[0])
    weight_down = halves_of(core_order(side_rest[1], other_rest[1]))
    traded = [trade(out[:spans]) for out in forward]
    side_gate = after(side_gate, traded)
    weight_gate = side_gate + [swap(half, "core", 1) for half in side_gate]
    (
        result_low,
        middle_grad,
        branch_grad,
        attended_mine,
        attended_other,
        gain_two_grad,
        *rest,
    ) = middle(
        spot,
        owners,
        spans,
        balanced_in,
        upstream,
        gain_rows[1:2],
        weight_out,
        joined(traded),
        weight_gate,
        weight_down,
    )
    gate_kept, gate_sent, down_grad, grad_cut = rest[:2], rest[2:4], rest[4:6], rest[6:]
    grad_heads = trade(grad_cut)
    gate_both = core_sum(gate_kept, gate_sent, grad_heads)
    down_both = core_sum(*zip(*(row_parts(half) for half in down_grad)), grad_heads)
    grad_heads = after(grad_heads, gate_both, down_both)
    down_line = chips_scatter(down_both)
    gate_line = chips_scatter(gate_both)
    grads = [
        attend_back(spot, p, qkv[p], starts, grad_heads, *forward[p][spans:], cosine_all, sine_all)
        for p in range(pairs)
    ]
    result_slots = place(anchor_slot, after(regroup(result_low, grads[0]), grads[-1]), slots)
    outputs = exchange(result_slots)
    attended_mine, attended_other, branch_grad = after(
        (attended_mine, attended_other, branch_grad), grads[-1]
    )
    out_kept = outer(attended_mine, branch_grad).astype(BF16)
    out_sent = outer(attended_other, branch_grad).astype(BF16)
    middle_grad = after(middle_grad, result_slots, out_kept, out_sent, down_line)
    sent_a, sent_b, kept_a, kept_b, input_low, gains_kept, gains_sent = last(
        spot,
        owners,
        spans,
        balanced_in,
        middle_grad,
        gain_rows[0:1],
        gain_two_grad,
        normed_one,
        weight_in,
        joined(trade(pieces) for pieces in grads),
    )
    gate_shard = line_scatter(gate_line)
    down_shard = line_scatter(after(down_line, gate_shard))
    in_both = core_sum(
        [kept_a, kept_b, out_kept, gains_kept], [sent_a, sent_b, out_sent, gains_sent]
    )
    in_both = after(in_both, gate_line)
    in_line = chips_sum(in_both)
    outputs = pick(target_slot, after(outputs, in_both))
    shards = line_sum(in_line)
    in_shard, out_shard = shards[:, : 3 * width], shards[:, 3 * width : 4 * width]
    chosen = jnp.eye(2, LANES, dtype=F32)
    gain_shard = lax.dot_general(
        chosen,
        shards[:, 4 * width :],
        (((1,), (1,)), ((), ())),
        precision=lax.Precision.HIGHEST,
        preferred_element_type=F32,
    )
    returned = exchange(place(anchor_slot, regroup(input_low, in_both), slots))
    input_gradient = pick(target_slot, returned)
    local_total = (
        jnp.sum(in_shard * in_shard)
        + jnp.sum(out_shard * out_shard)
        + jnp.sum(gate_shard * gate_shard)
        + jnp.sum(down_shard * down_shard)
        + jnp.sum(gain_shard * gain_shard)
    )
    total = jnp.sum(spread(jnp.broadcast_to(local_total, (8, LANES)), ROWS).reshape(-1, 8, LANES)[:, 0, 0])
    gradient_norm = jnp.sqrt(total)
    factor = CLIP / jnp.maximum(gradient_norm, CLIP)
    updates = []
    for weight, gradient, first, second, rate in (
        (attention_in, in_shard, first_in, second_in, D ** (-0.5)),
        (attention_out, out_shard, first_out, second_out, 0.5),
        (gate_up, gate_shard, first_gate, second_gate, D ** (-0.5)),
        (feed_down, down_shard, first_down, second_down, 2.0 * FF ** (-0.5)),
        (norm_gains, gain_shard, first_gains, second_gains, 1.5),
    ):
        updates.extend(adamw(weight, gradient, first, second, rate, factor))
    return (outputs, input_gradient, gradient_norm, *updates)


def solution(mesh):
    owners, spans = mesh.shape["dp"], mesh.shape["seq"]
    parts = Mesh(mesh.devices.reshape(owners // 2, 2, spans), ROWS)
    rows = P(ROWS, None)
    columns = P(None, ROWS)
    line = P(ROWS)
    in_specs = (rows, rows, line, line, line) + ((rows,) * 4 + (columns,)) * 3
    out_specs = (rows, rows, P()) + (rows,) * 12 + (columns,) * 3
    return jax.shard_map(
        per_device, mesh=parts, in_specs=in_specs, out_specs=out_specs, check_vma=False
    )
```

```python
import functools

import jax
import jax.numpy as jnp
from jax import lax
from jax.experimental import pallas as pl
from jax.experimental.pallas import tpu as pltpu
from jax.sharding import Mesh
from jax.sharding import PartitionSpec as P

D = 1024
HEAD = 64
FF = 2816
STEP = 10
LANES = 128

EPSILON = 1e-05
THETA = 500000.0
NEGATIVE = -1e30
BETA_FIRST = 0.9
BETA_SECOND = 0.95
ADAM_EPSILON = 1e-08
DECAY = 0.1
CLIP = 1.0
SCALE = 0.125
VMEM = 56 * 1024 * 1024
F32 = jnp.float32
BF16 = jnp.bfloat16
ROWS = ("chip", "core", "seq")


def norm_rows(values, gain_row):
    inverse = lax.rsqrt(jnp.mean(values * values, axis=1, keepdims=True) + EPSILON)
    normal = values * inverse
    return (normal * gain_row[None, :], normal, inverse)


def norm_back(upstream, normal, inverse, gain_row):
    gain_grad = jnp.sum(upstream * normal, axis=0)
    scaled = upstream * gain_row[None, :]
    return (
        inverse * (scaled - normal * jnp.mean(scaled * normal, axis=1, keepdims=True)),
        gain_grad,
    )


def rope_tables(positions):
    half_size = HEAD // 2
    frequency = jnp.power(THETA, -2.0 * jnp.arange(half_size, dtype=F32) / HEAD)
    angles = positions[:, None] * frequency[None, :]
    cosine = jnp.cos(angles)
    sine = jnp.sin(angles)
    return (
        jnp.concatenate([cosine] * 4, axis=1),
        jnp.concatenate([-sine, sine, -sine, sine], axis=1),
    )


def swap_halves(values):
    lane = lax.broadcasted_iota(jnp.int32, values.shape, 1)
    left = pltpu.roll(values, LANES - HEAD // 2, 1)
    right = pltpu.roll(values, HEAD // 2, 1)
    return jnp.where(lane % HEAD < HEAD // 2, left, right)


def contract_last(left, right):
    return lax.dot_general(left, right, (((1,), (1,)), ((), ())), preferred_element_type=F32)


def params():
    return pltpu.CompilerParams(vmem_limit_bytes=VMEM)


def turned(values):
    return values.astype(F32).T.astype(BF16)


def rows_at(index, count):
    return pl.ds(pl.multiple_of(index * count, count), count)


def project_kernel(spans, half, place_ref, x_ref, gain_ref, wa_ref, wb_ref, cos_ref, sin_ref, h_ref, *outs):
    step = pl.program_id(0)
    hw = wa_ref.shape[1]

    @pl.when(step == 0)
    def _():
        x = x_ref[...].astype(F32)
        inverse = lax.rsqrt(jnp.mean(x * x, axis=1, keepdims=True) + EPSILON)
        h_ref[...] = (x * inverse * gain_ref[...]).astype(BF16)

    def work(w_ref, rotated):
        acc = jnp.dot(h_ref[...], w_ref[...], preferred_element_type=F32)
        if rotated:
            pieces = []
            for c in range(hw // LANES):
                part = acc[:, c * LANES : (c + 1) * LANES]
                pieces.append(part * cos_ref[...] + swap_halves(part) * sin_ref[...])
            acc = jnp.concatenate(pieces, axis=1)
        low = acc.astype(BF16)
        for k in range(spans):

            @pl.when((step % spans) ^ place_ref[0] == k)
            def _(k=k):
                for pair in range(hw // LANES):
                    outs[pair * spans + k][...] = low[:, pair * LANES : (pair + 1) * LANES]

    turning = step < 2 * spans
    pl.when(step < half)(lambda: work(wa_ref, True))
    pl.when((step >= half) & turning)(lambda: work(wb_ref, True))
    pl.when(jnp.logical_not(turning))(lambda: work(wb_ref, False))


def project(spot, x, gain_row, weights, cosine, sine, spans):
    rows, width = x.shape
    hw = width // spans
    half = 3 * spans // 2
    fixed = lambda t, p: (0, 0)
    return pl.pallas_call(
        functools.partial(project_kernel, spans, half),
        grid_spec=pltpu.PrefetchScalarGridSpec(
            num_scalar_prefetch=1,
            grid=(3 * spans,),
            in_specs=[
                pl.BlockSpec((rows, width), fixed),
                pl.BlockSpec((1, width), fixed),
                pl.BlockSpec((width, hw), lambda t, p: (0, jnp.minimum(t, half - 1))),
                pl.BlockSpec((width, hw), lambda t, p: (0, jnp.maximum(t - half, 0))),
                pl.BlockSpec((rows, LANES), fixed),
                pl.BlockSpec((rows, LANES), fixed),
            ],
            out_specs=[pl.BlockSpec((rows, width), fixed)]
            + [pl.BlockSpec((rows, LANES), lambda t, p: (0, t // spans))] * (width // LANES),
        ),
        out_shape=[jax.ShapeDtypeStruct((rows, width), BF16)]
        + [jax.ShapeDtypeStruct((rows, 3 * LANES), BF16)] * (width // LANES),
        compiler_params=params(),
        cost_estimate=pl.CostEstimate(
            flops=17250000000, bytes_accessed=0, transcendentals=0
        ),
        name="project",
    )(spot, x, gain_row, *weights, cosine, sine)


def attend_kernel(spans, place_ref, start_ref, *refs):
    pieces, refs = refs[: 3 * spans], refs[3 * spans :]
    lows, (out_ref, log_ref, q_scr, k_scr, v_scr) = refs[:spans], refs[spans:]
    block = q_scr.shape[0] // spans
    here = place_ref[0]
    relative = pl.program_id(0)
    i = relative ^ here
    lane = lax.broadcasted_iota(jnp.int32, (block, LANES), 1)
    first = lane < HEAD

    @pl.when(relative == 0)
    def _():
        for k in range(spans):
            at = rows_at(here ^ k, block)
            q_scr[k * block : (k + 1) * block, :] = pieces[k][...]
            k_scr[at, :] = pieces[spans + k][...]
            v_scr[:, at] = turned(pieces[2 * spans + k][...])

    q_pair = q_scr[rows_at(relative, block), :] * SCALE
    key = lax.broadcasted_iota(jnp.int32, (block, block), 0)
    query = lax.broadcasted_iota(jnp.int32, (block, block), 1)
    starts = start_ref[:, rows_at(i, block)]
    heads = []
    for head in range(2):
        mine = first if head == 0 else jnp.logical_not(first)
        heads.append(jnp.where(mine, q_pair, jnp.zeros_like(q_pair)))

    def visit(j, carry, diagonal):
        at = rows_at(j, block)
        k = k_scr[at, :]
        seen = key + j * block >= starts
        if diagonal:
            seen = seen & (key <= query)
        result = []
        for head in range(2):
            s = jnp.where(seen, contract_last(k, heads[head]), NEGATIVE)
            lines = slice(head * HEAD, (head + 1) * HEAD)
            new = jnp.max(s, axis=0, keepdims=True)
            if not diagonal:
                top, total, acc = carry[head]
                new = jnp.maximum(top, new)
            p = jnp.exp(s - new)
            added = jnp.sum(p, axis=0, keepdims=True)
            weighed = jnp.dot(v_scr[lines, at], p.astype(BF16), preferred_element_type=F32)
            if not diagonal:
                factor = jnp.exp(top - new)
                added = added + total * factor
                weighed = weighed + acc * factor
            result.append((new, added, weighed))
        return tuple(result)

    carry = visit(i, None, True)
    carry = lax.fori_loop(0, i, lambda j, c: visit(j, c, False), carry)
    parts = []
    for head in range(2):
        top, total, acc = carry[head]
        parts.append(acc / total)
        log_ref[head : head + 1, :] = top + jnp.log(total)
    out = jnp.concatenate(parts, axis=0).T
    out_ref[0] = out
    low = out.astype(BF16)
    for k in range(spans):

        @pl.when(relative == k)
        def _(k=k):
            lows[k][...] = low


def piece_specs(rows, spans):
    return [
        pl.BlockSpec((rows, LANES), functools.partial(lambda part, i, s: (0, part), part))
        for part in range(3)
        for _ in range(spans)
    ]


def attend(spot, qkv, starts):
    spans = len(qkv)
    rows = qkv[0].shape[0]
    group = rows * spans
    return pl.pallas_call(
        functools.partial(attend_kernel, spans),
        grid_spec=pltpu.PrefetchScalarGridSpec(
            num_scalar_prefetch=1,
            grid=(spans,),
            in_specs=[pl.BlockSpec((1, group), lambda i, s: (0, 0))] + piece_specs(rows, spans),
            out_specs=[pl.BlockSpec((rows, LANES), lambda i, s: (0, 0))] * spans
            + [
                pl.BlockSpec((1, rows, LANES), lambda i, s: (i, 0, 0)),
                pl.BlockSpec((8, rows), lambda i, s: (0, i ^ s[0])),
            ],
            scratch_shapes=[
                pltpu.VMEM((group, LANES), BF16),
                pltpu.VMEM((group, LANES), BF16),
                pltpu.VMEM((LANES, group), BF16),
            ],
        ),
        out_shape=[jax.ShapeDtypeStruct((rows, LANES), BF16)] * spans
        + [
            jax.ShapeDtypeStruct((spans, rows, LANES), F32),
            jax.ShapeDtypeStruct((8, group), F32),
        ],
        compiler_params=params(),
        cost_estimate=pl.CostEstimate(
            flops=18400000000, bytes_accessed=0, transcendentals=0
        ),
        name="attend",
    )(spot, starts.reshape(1, group), *(list(qkv) * 3))


def attend_back_kernel(spans, place_ref, start_ref, *refs):
    pieces, refs = refs[: 3 * spans], refs[3 * spans :]
    grads, refs = refs[:spans], refs[spans:]
    (out_ref, log_ref, cos_ref, sin_ref), refs = refs[:4], refs[4:]
    outs, refs = refs[:spans], refs[spans:]
    q_scr, k_scr, v_scr, do_scr, dq_scr, dk_scr, dv_scr, delta_ref, turned_ref = refs
    block = q_scr.shape[0] // spans
    here = place_ref[0]
    j = pl.program_id(0)
    lane = lax.broadcasted_iota(jnp.int32, (block, LANES), 1)
    first = lane < HEAD

    @pl.when(j == 0)
    def _():
        for k in range(spans):
            at = rows_at(here ^ k, block)
            q_scr[at, :] = pieces[k][...]
            k_scr[at, :] = pieces[spans + k][...]
            v_scr[at, :] = pieces[2 * spans + k][...]
            do = grads[k][...]
            do_scr[at, :] = do
            product = (do.astype(F32) * out_ref[k]).T
            delta_ref[0:1, at] = jnp.sum(product[:HEAD], axis=0, keepdims=True)
            delta_ref[1:2, at] = jnp.sum(product[HEAD:], axis=0, keepdims=True)
        turned_ref[...] = jnp.zeros_like(turned_ref)

    now = rows_at(j, block)
    k_pair = k_scr[now, :]
    v_pair = v_scr[now, :]
    k_turned = turned(k_pair)
    key = j * block + lax.broadcasted_iota(jnp.int32, (block, block), 0)
    query = lax.broadcasted_iota(jnp.int32, (block, block), 1)

    def visit(i, carry, diagonal):
        dk, dv = carry
        at = rows_at(i, block)
        q_pair = q_scr[at, :] * SCALE
        do_pair = do_scr[at, :]
        seen = key >= start_ref[:, at]
        if diagonal:
            seen = seen & (key <= query + i * block)
        for head in range(2):
            mine = first if head == 0 else jnp.logical_not(first)
            q = jnp.where(mine, q_pair, jnp.zeros_like(q_pair))
            do = jnp.where(mine, do_pair, jnp.zeros_like(do_pair))
            s = jnp.where(seen, contract_last(k_pair, q), NEGATIVE)
            p = jnp.exp(s - log_ref[head : head + 1, at])
            dp = contract_last(v_pair, do)
            ds = (p * (dp - delta_ref[head : head + 1, at])).astype(BF16)
            dv = dv + jnp.dot(p.astype(BF16), do, preferred_element_type=F32)
            dk = dk + jnp.dot(ds, q, preferred_element_type=F32)
            lines = slice(head * HEAD, (head + 1) * HEAD)
            turned_ref[lines, at] += jnp.dot(k_turned[lines], ds, preferred_element_type=F32)
        return (dk, dv)

    zero = jnp.zeros((block, LANES), F32)
    carry = visit(j, (zero, zero), True)
    dk, dv = lax.fori_loop(j + 1, spans, lambda i, c: visit(i, c, False), carry)

    def turn_back(values, at):
        return values * cos_ref[at, :] + swap_halves(values * sin_ref[at, :])

    dk_scr[now, :] = turn_back(dk, now).astype(BF16)
    dv_scr[now, :] = dv.astype(BF16)

    @pl.when(j == spans - 1)
    def _():
        def finish(i, carry):
            at = rows_at(i, block)
            dq_scr[at, :] = turn_back(turned_ref[:, at].T * SCALE, at).astype(BF16)
            return carry

        lax.fori_loop(0, spans, finish, 0)
        for k in range(spans):
            at = rows_at(here ^ k, block)
            for part, scr in enumerate((dq_scr, dk_scr, dv_scr)):
                outs[k][:, part * LANES : (part + 1) * LANES] = scr[at, :]


def attend_back(spot, pair, qkv, starts, grads, out, logs, cosine, sine):
    spans = len(qkv)
    rows = qkv[0].shape[0]
    group = rows * spans
    whole = lambda j, s: (0, 0)
    low = pltpu.VMEM((group, LANES), BF16)
    return pl.pallas_call(
        functools.partial(attend_back_kernel, spans),
        grid_spec=pltpu.PrefetchScalarGridSpec(
            num_scalar_prefetch=1,
            grid=(spans,),
            in_specs=[pl.BlockSpec((1, group), whole)]
            + piece_specs(rows, spans)
            + [pl.BlockSpec((rows, LANES), lambda j, s: (0, pair))] * spans
            + [
                pl.BlockSpec((spans, rows, LANES), lambda j, s: (0, 0, 0)),
                pl.BlockSpec((8, group), whole),
                pl.BlockSpec((group, LANES), whole),
                pl.BlockSpec((group, LANES), whole),
            ],
            out_specs=[pl.BlockSpec((rows, 3 * LANES), whole)] * spans,
            scratch_shapes=[low] * 7 + [pltpu.VMEM((8, group), F32), pltpu.VMEM((LANES, group), F32)],
        ),
        out_shape=[jax.ShapeDtypeStruct((rows, 3 * LANES), BF16)] * spans,
        compiler_params=params(),
        cost_estimate=pl.CostEstimate(
            flops=27600000000, bytes_accessed=0, transcendentals=0
        ),
        name="attend_back",
    )(spot, starts.reshape(1, group), *(list(qkv) * 3), *grads, out, logs, cosine, sine)


def core_split(values, block, own):
    width = values.shape[1]
    sides = []
    for core in range(2):
        blocks = [values[:, b * block : (b + 1) * block] for b in range(core, width // block, 2)]
        sides.append(jnp.concatenate(blocks, axis=1))
    return (jnp.where(own == 0, sides[0], sides[1]), jnp.where(own == 0, sides[1], sides[0]))


def core_merge(mine, other, block, own):
    sides = (jnp.where(own == 0, mine, other), jnp.where(own == 0, other, mine))
    blocks = mine.shape[1] // block
    return jnp.concatenate(
        [side[:, b * block : (b + 1) * block] for b in range(blocks) for side in sides], axis=1
    )


def middle_kernel(spans, block, place_ref, x_ref, dy_ref, gain_ref, om_ref, oo_ref, *refs):
    heads = x_ref.shape[1] // LANES
    attended, refs = refs[:heads], refs[heads:]
    (gm_ref, um_ref, go_ref, uo_ref, da_ref, db_ref), refs = refs[:6], refs[6:]
    (y_ref, dx_ref, branch_ref, ow_ref, ox_ref, gain_grad_ref), refs = refs[:6], refs[6:]
    (gk_ref, uk_ref, gs_ref, us_ref, ga_ref, gb_ref), refs = refs[:6], refs[6:]
    grads, refs = refs[:spans], refs[spans:]
    hm_scr, ho_scr, kept_scr, sent_scr, x2_scr, y_scr, dm_scr, do_scr, wide_scr = refs
    step, steps = pl.program_id(0), pl.num_programs(0)
    half = x_ref.shape[1] // 2
    here, core = place_ref[0], place_ref[1]

    def pieces_at(pieces):
        for index, piece in enumerate(pieces):
            pair, k = index // spans, index % spans
            yield rows_at((here ^ k) * (heads // spans) + pair, LANES), piece

    hw = x_ref.shape[1] // spans

    def normal():
        x2 = x2_scr[...]
        inverse = lax.rsqrt(jnp.mean(x2 * x2, axis=1, keepdims=True) + EPSILON)
        return (x2 * inverse, inverse)

    @pl.when(step == 0)
    def _():
        for at, piece in pieces_at(attended):
            wide_scr[:, at] = piece[...]
        mine, other = core_split(wide_scr[...], block, core)
        ow_ref[...] = mine
        ox_ref[...] = other
        x2_scr[...] = (
            x_ref[...].astype(F32)
            + jnp.dot(mine, om_ref[...], preferred_element_type=F32)
            + jnp.dot(other, oo_ref[...], preferred_element_type=F32)
        )
        h = (normal()[0] * gain_ref[...]).astype(BF16).astype(F32)
        mine, other = core_split(h, block, core)
        hm_scr[...] = mine.astype(BF16)
        ho_scr[...] = other.astype(BF16)
        kept_scr[...] = mine.T.astype(BF16)
        sent_scr[...] = other.T.astype(BF16)
        y_scr[...] = jnp.zeros_like(y_scr)
        dm_scr[...] = jnp.zeros_like(dm_scr)
        do_scr[...] = jnp.zeros_like(do_scr)

    hm, ho, dy = hm_scr[...], ho_scr[...], dy_ref[...]
    gm, um, go, uo = gm_ref[...], um_ref[...], go_ref[...], uo_ref[...]
    gate = jnp.dot(hm, gm, preferred_element_type=F32) + jnp.dot(ho, go, preferred_element_type=F32)
    up = jnp.dot(hm, um, preferred_element_type=F32) + jnp.dot(ho, uo, preferred_element_type=F32)
    share = jax.nn.sigmoid(gate)
    active = gate * share
    hidden_full = active * up
    hidden = hidden_full.astype(BF16)
    down = jnp.concatenate([da_ref[...], db_ref[...]], axis=1)
    y_scr[...] += jnp.dot(hidden, down, preferred_element_type=F32)
    dhid = contract_last(dy, down)
    dgate = (dhid * up * share * (1.0 + gate * (1.0 - share))).astype(BF16)
    dup = (dhid * active).astype(BF16)
    dm_scr[...] += contract_last(dgate, gm) + contract_last(dup, um)
    do_scr[...] += contract_last(dgate, go) + contract_last(dup, uo)
    kept, sent = kept_scr[...], sent_scr[...]
    gs_ref[...] = jnp.dot(sent, dgate, preferred_element_type=F32).astype(BF16)
    us_ref[...] = jnp.dot(sent, dup, preferred_element_type=F32).astype(BF16)
    gk_ref[...] = jnp.dot(kept, dgate, preferred_element_type=F32).astype(BF16)
    uk_ref[...] = jnp.dot(kept, dup, preferred_element_type=F32).astype(BF16)
    hidden_turned = hidden_full.T.astype(BF16)
    ga_ref[...] = jnp.dot(hidden_turned, dy[:, :half], preferred_element_type=F32).astype(BF16)
    gb_ref[...] = jnp.dot(hidden_turned, dy[:, half:], preferred_element_type=F32).astype(BF16)

    @pl.when(step == steps - 1)
    def _():
        y_ref[...] = (x2_scr[...] + y_scr[...]).astype(BF16)
        norm, inverse = normal()
        dh = core_merge(dm_scr[...], do_scr[...], block, core)
        gain_grad_ref[...] = jnp.sum(dh * norm, axis=0, keepdims=True)
        scaled = dh * gain_ref[...]
        inner = jnp.mean(scaled * norm, axis=1, keepdims=True)
        dx = dy_ref[...].astype(F32) + inverse * (scaled - norm * inner)
        dx_ref[...] = dx
        branch = dx.astype(BF16)
        branch_ref[...] = branch
        mine = contract_last(branch, om_ref[...]).astype(BF16)
        other = contract_last(branch, oo_ref[...]).astype(BF16)
        wide_scr[...] = core_merge(mine, other, block, core)
        for k in range(spans):
            grads[k][...] = wide_scr[:, rows_at(here ^ k, hw)]


def middle(spot, owners, spans, x, dy, gain_row, weight_out, attended, weight_gate, weight_down):
    rows, width = x.shape
    hidden = weight_gate[0].shape[1]
    heads, half, tile = width // LANES, width // 2, 2 * LANES
    tiles = hidden // tile
    fixed = lambda t, s: (0, 0)
    full = pl.BlockSpec((rows, width), fixed)
    side = pl.BlockSpec((rows, half), fixed)
    across = lambda t, s: (0, t)
    along = lambda t, s: (t, 0)
    shape = jax.ShapeDtypeStruct
    return pl.pallas_call(
        functools.partial(middle_kernel, spans, width // owners),
        grid_spec=pltpu.PrefetchScalarGridSpec(
            num_scalar_prefetch=1,
            grid=(tiles,),
            in_specs=[full, full, pl.BlockSpec((1, width), fixed)]
            + [pl.BlockSpec((half, width), fixed)] * 2
            + [pl.BlockSpec((rows, LANES), fixed)] * heads
            + [pl.BlockSpec((half, tile), across)] * 4
            + [pl.BlockSpec((tile, half), along)] * 2,
            out_specs=[full] * 3
            + [side] * 2
            + [pl.BlockSpec((1, width), fixed)]
            + [pl.BlockSpec((half, tile), across)] * 4
            + [pl.BlockSpec((tile, half), along)] * 2
            + [pl.BlockSpec((rows, width // spans), fixed)] * spans,
            scratch_shapes=[
                pltpu.VMEM((rows, half), BF16),
                pltpu.VMEM((rows, half), BF16),
                pltpu.VMEM((half, rows), BF16),
                pltpu.VMEM((half, rows), BF16),
                pltpu.VMEM((rows, width), F32),
                pltpu.VMEM((rows, width), F32),
                pltpu.VMEM((rows, half), F32),
                pltpu.VMEM((rows, half), F32),
                pltpu.VMEM((rows, width), BF16),
            ],
        ),
        out_shape=[
            shape((rows, width), BF16),
            shape((rows, width), F32),
            shape((rows, width), BF16),
            shape((rows, half), BF16),
            shape((rows, half), BF16),
            shape((1, width), F32),
        ]
        + [shape((half, hidden), BF16)] * 4
        + [shape((hidden, half), BF16)] * 2
        + [shape((rows, width // spans), BF16)] * spans,
        compiler_params=params(),
        cost_estimate=pl.CostEstimate(
            flops=55200000000, bytes_accessed=0, transcendentals=0
        ),
        name="middle",
    )(
        spot,
        x,
        dy,
        gain_row,
        *weight_out,
        *attended,
        *weight_gate,
        *weight_down,
    )


def last_kernel(spans, half, block, place_ref, x_ref, dx2_ref, gain_ref, second_ref, h_ref, wa_ref, wb_ref, *refs):
    heads = x_ref.shape[1] // LANES
    pieces, refs = refs[:heads], refs[heads:]
    sa_ref, sb_ref, ka_ref, kb_ref, dx_ref, gk_ref, gs_ref, d_scr, kept_scr, sent_scr, dh_scr = refs
    step = pl.program_id(0)

    @pl.when(step == 0)
    def _():
        kept, sent = core_split(h_ref[...].astype(F32), block, place_ref[1])
        kept_scr[...] = kept.T.astype(BF16)
        sent_scr[...] = sent.T.astype(BF16)
        dh_scr[...] = jnp.zeros_like(dh_scr)

    for k in range(spans):

        @pl.when((step % spans) ^ place_ref[0] == k)
        def _(k=k):
            for pair in range(heads // spans):
                d_scr[:, pair * LANES : (pair + 1) * LANES] = pieces[pair * spans + k][...]

    def work(w_ref, s_ref, k_ref):
        d = d_scr[...]
        s_ref[...] = jnp.dot(sent_scr[...], d, preferred_element_type=F32).astype(BF16)
        k_ref[...] = jnp.dot(kept_scr[...], d, preferred_element_type=F32).astype(BF16)
        dh_scr[...] += contract_last(d, w_ref[...])

    pl.when(step < half)(lambda: work(wa_ref, sa_ref, ka_ref))
    pl.when(step >= half)(lambda: work(wb_ref, sb_ref, kb_ref))

    @pl.when(step == pl.num_programs(0) - 1)
    def _():
        x = x_ref[...].astype(F32)
        inverse = lax.rsqrt(jnp.mean(x * x, axis=1, keepdims=True) + EPSILON)
        norm = x * inverse
        dh = dh_scr[...]
        row = lax.broadcasted_iota(jnp.int32, (LANES, x.shape[1]), 0)
        gains = jnp.where(row == 0, jnp.sum(dh * norm, axis=0, keepdims=True), 0.0)
        gains = jnp.where(row == 1, second_ref[...], gains)
        kept, sent = core_split(gains, block, place_ref[1])
        gk_ref[...] = kept.T.astype(BF16)
        gs_ref[...] = sent.T.astype(BF16)
        scaled = dh * gain_ref[...]
        inner = jnp.mean(scaled * norm, axis=1, keepdims=True)
        dx_ref[...] = (dx2_ref[...] + inverse * (scaled - norm * inner)).astype(BF16)


def last(spot, owners, spans, x, dx2, gain_row, gain_two_grad, normed, weights, pieces):
    rows, width = x.shape
    hw = width // spans
    half = 3 * spans // 2
    low = lambda t, s: (0, jnp.minimum(t, half - 1))
    high = lambda t, s: (0, jnp.maximum(t - half, 0))
    fixed = lambda t, s: (0, 0)
    full = pl.BlockSpec((rows, width), fixed)
    row = pl.BlockSpec((1, width), fixed)
    shape = jax.ShapeDtypeStruct
    return pl.pallas_call(
        functools.partial(last_kernel, spans, half, width // owners),
        grid_spec=pltpu.PrefetchScalarGridSpec(
            num_scalar_prefetch=1,
            grid=(3 * spans,),
            in_specs=[full, full, row, row, full]
            + [pl.BlockSpec((width, hw), low), pl.BlockSpec((width, hw), high)]
            + [pl.BlockSpec((rows, LANES), lambda t, s: (0, t // spans))] * len(pieces),
            out_specs=[
                pl.BlockSpec((width // 2, hw), low),
                pl.BlockSpec((width // 2, hw), high),
                pl.BlockSpec((width // 2, hw), low),
                pl.BlockSpec((width // 2, hw), high),
                full,
                pl.BlockSpec((width // 2, LANES), fixed),
                pl.BlockSpec((width // 2, LANES), fixed),
            ],
            scratch_shapes=[
                pltpu.VMEM((rows, hw), BF16),
                pltpu.VMEM((width // 2, rows), BF16),
                pltpu.VMEM((width // 2, rows), BF16),
                pltpu.VMEM((rows, width), F32),
            ],
        ),
        out_shape=[shape((width // 2, 3 * width // 2), BF16)] * 4
        + [shape((rows, width), BF16)]
        + [shape((width // 2, LANES), BF16)] * 2,
        compiler_params=params(),
        cost_estimate=pl.CostEstimate(
            flops=21850000000, bytes_accessed=0, transcendentals=0
        ),
        name="last",
    )(spot, x, dx2, gain_row, gain_two_grad, normed, *weights, *pieces)


def adamw(weight, gradient, first, second, rate, factor):
    clipped = gradient * factor
    first_new = BETA_FIRST * first + (1.0 - BETA_FIRST) * clipped
    second_new = BETA_SECOND * second + (1.0 - BETA_SECOND) * clipped * clipped
    corrected_first = first_new / (1.0 - BETA_FIRST**STEP)
    corrected_second = second_new / (1.0 - BETA_SECOND**STEP)
    weight_new = weight - rate * (
        corrected_first / (jnp.sqrt(corrected_second) + ADAM_EPSILON) + DECAY * weight
    )
    return (first_new, second_new, weight_new)


def swap(values, axis, step):
    count = lax.axis_size(axis)
    return lax.ppermute(values, axis, [(i, i ^ step) for i in range(count)])


def paired():
    return lax.axis_size("seq") == 4


def group_place():
    if paired():
        return 2 * lax.axis_index("core") + lax.axis_index("seq") % 2
    return lax.axis_index("seq")


def group_swap(values, step):
    if not paired():
        return swap(values, "seq", step)
    spans = lax.axis_size("seq")
    pairs = [
        (c * spans + z, (c ^ (step >> 1)) * spans + (z ^ (step & 1)))
        for c in range(2)
        for z in range(spans)
    ]
    return lax.ppermute(values, ("core", "seq"), pairs)


def regroup(values, *gates):
    if not paired():
        return values
    spans = lax.axis_size("seq")
    pairs = [
        (c * spans + z, (z // 2) * spans + 2 * c + z % 2)
        for c in range(2)
        for z in range(spans)
        if c != z // 2
    ]
    stays = lax.axis_index("core") == lax.axis_index("seq") // 2
    came = after(lax.ppermute(values, ("core", "seq"), pairs), gates)
    return jnp.where(stays, values, came)


def trade(pieces, *gates):
    return [pieces[0], *after([group_swap(pieces[k], k) for k in range(1, len(pieces))], gates)]


def bit_of(axis, step):
    return lax.axis_index(axis) & step


def ordered(own_bit, mine, other, at):
    return jnp.where(own_bit == 0, jnp.stack([mine, other], at), jnp.stack([other, mine], at))


def in_order(pieces, here):
    count = len(pieces)
    bits = count.bit_length() - 1
    stack = jnp.stack(pieces).reshape((2,) * bits + pieces[0].shape)
    for at in range(bits):
        flipped = jnp.flip(stack, axis=at)
        stack = jnp.where((here >> (bits - 1 - at)) & 1 == 1, flipped, stack)
    return stack.reshape((count,) + pieces[0].shape)


def chip_bits():
    count = lax.axis_size("chip")
    bits = [b for b in range(count.bit_length() - 1)]
    return bits, bits[::-1]


def halves_of(values):
    middle = values.shape[-1] // 2
    return (values[..., :middle], values[..., middle:])


def spread(values, axes):
    count = 1
    for axis in axes:
        count *= lax.axis_size(axis)
    copies = jnp.broadcast_to(values[None], (count,) + values.shape)
    return lax.all_to_all(copies, axes, split_axis=0, concat_axis=0, tiled=True)


def gather_line(shard, *gates):
    spans = lax.axis_size("seq")
    pieces = [shard] + [swap(shard, "seq", k) for k in range(1, spans)]
    pieces = after(pieces, gates)
    return in_order(pieces, lax.axis_index("seq")).reshape(-1, shard.shape[1])


def after(values, *tokens):
    return lax.optimization_barrier((values, tokens))[0]


def gather_chips(block, gate=None, came=()):
    parts, orders = halves_of(block), chip_bits()
    for at_step in range(len(orders[0])):
        if gate is not None and at_step == len(orders[0]) - 1:
            parts = after(parts, gate)
        others = [swap(half, "chip", 1 << order[at_step]) for half, order in zip(parts, orders)]
        if at_step < len(came):
            others = after(others, came[at_step])
        parts = [
            ordered(
                bit_of("chip", 1 << order[at_step]),
                half,
                other,
                sum(1 for d in order[:at_step] if d > order[at_step]),
            )
            for half, other, order in zip(parts, others, orders)
        ]
    return [half.reshape(-1, half.shape[-1]) for half in parts]


def core_order(mine, other):
    chips, width = lax.axis_size("chip"), mine.shape[1]
    mine, other = mine.reshape(chips, -1, width), other.reshape(chips, -1, width)
    return ordered(lax.axis_index("core"), mine, other, 1).reshape(-1, width)


def core_sum(kept, sent, *gates):
    came = after([swap(other, "core", 1) for other in sent], gates)
    parts = [
        (mine.astype(F32) + other.astype(F32)).astype(BF16) for mine, other in zip(kept, came)
    ]
    return jnp.concatenate(parts, axis=-1)


def chips_scatter(values):
    return lax.psum_scatter(values, "chip", scatter_dimension=0, tiled=True)


def line_scatter(values):
    return lax.psum_scatter(values, "seq", scatter_dimension=0, tiled=True).astype(F32)


def direct_sum(values, axis, *gates):
    count, here = lax.axis_size(axis), lax.axis_index(axis)
    total = lax.dynamic_index_in_dim(values, here, 0, keepdims=False).astype(F32)
    pieces = [
        swap(lax.dynamic_index_in_dim(values, here ^ k, 0, keepdims=False), axis, k)
        for k in range(1, count)
    ]
    for piece in after(pieces, gates):
        total = total + piece.astype(F32)
    return total


def line_sum(values):
    spans = lax.axis_size("seq")
    return direct_sum(values.reshape(spans, -1, values.shape[-1]), "seq")


def chips_sum(values, *gates):
    chips = lax.axis_size("chip")
    return direct_sum(values.reshape(chips, -1, values.shape[-1]), "chip", *gates).astype(BF16)


def outer(left, right):
    return lax.dot_general(left, right, (((0,), (0,)), ((), ())), preferred_element_type=F32)


def row_parts(gradient):
    width = gradient.shape[1]
    chips = lax.axis_size("chip")
    parts = gradient.reshape(chips, 2, -1, width)
    own = lax.axis_index("core") == 0
    kept = jnp.where(own, parts[:, 0], parts[:, 1]).reshape(-1, width)
    sent = jnp.where(own, parts[:, 1], parts[:, 0]).reshape(-1, width)
    return (kept, sent)


def place(index, values, slots):
    chosen = lax.broadcasted_iota(jnp.int32, (slots, index.shape[0]), 0) == index[None, :]
    return jnp.dot(chosen.astype(BF16), values, preferred_element_type=F32).astype(BF16)


def pick(index, values):
    slots = values.shape[0]
    chosen = lax.broadcasted_iota(jnp.int32, (index.shape[0], slots), 1) == index[:, None]
    return jnp.dot(chosen.astype(BF16), values, preferred_element_type=F32).astype(BF16)


def per_device(
    inputs,
    cotangent,
    target_slot,
    anchor_slot,
    sequence_start,
    attention_in,
    attention_out,
    gate_up,
    feed_down,
    norm_gains,
    first_in,
    first_out,
    first_gate,
    first_down,
    first_gains,
    second_in,
    second_out,
    second_gate,
    second_down,
    second_gains,
):
    owners = lax.axis_size("chip") * lax.axis_size("core")
    spans = lax.axis_size("seq")
    rows, width = inputs.shape
    per_owner = rows // owners
    capacity = per_owner + per_owner // 2
    slots = owners * capacity
    group = rows * spans
    here = group_place()
    device = (lax.axis_index("chip") * 2 + lax.axis_index("core")) * spans + lax.axis_index("seq")
    spot = jnp.stack([here, lax.axis_index("core")]).astype(jnp.int32)

    def exchange(values):
        return lax.all_to_all(values, ("chip", "core"), split_axis=0, concat_axis=0, tiled=True)

    pairs = width // spans // LANES

    def by_pair(pieces):
        return [pieces[p * spans : (p + 1) * spans] for p in range(pairs)]

    def joined(lists):
        return [piece for pieces in lists for piece in pieces]

    columns = norm_gains.shape[1]
    own_gains = jnp.pad(norm_gains.astype(BF16).reshape(1, -1), ((0, 7), (0, width - 2 * columns)))
    placed = jnp.concatenate(
        [
            place(target_slot, inputs, slots).reshape(owners, capacity, width),
            jnp.broadcast_to(own_gains[None], (owners, 8, width)),
        ],
        axis=1,
    )
    arrived = exchange(placed)
    gains_line = arrived[:, capacity, : 2 * columns]
    arrived = arrived[:, :capacity].reshape(slots, width)
    line_in = gather_line(attention_in.astype(BF16), placed)
    picked = pick(anchor_slot, arrived)
    balanced_in = regroup(picked)
    line_gate = gather_line(gate_up.astype(BF16), picked)
    side_in = gather_chips(line_in, gate=picked)
    line_gate_late = after(line_gate, side_in, balanced_in)
    core_in = after(side_in, line_gate)
    own_starts = regroup(sequence_start.reshape(1, rows), side_in)
    straight = jnp.concatenate([attention_out.astype(BF16), feed_down.astype(BF16)], axis=0)
    side_rest = lax.all_gather(after(straight, side_in), ("chip", "seq"), axis=0, tiled=True)
    weight_in = [core_order(half, swap(half, "core", 1)) for half in core_in]
    gains_line = after(gains_line.astype(F32), side_in)
    gain_pieces = [gains_line] + [swap(gains_line, "seq", k) for k in range(1, spans)]
    gain_rows = in_order(gain_pieces, lax.axis_index("seq")).reshape(spans, owners, 2, columns)
    gain_rows = jnp.transpose(gain_rows, (2, 1, 0, 3)).reshape(2, width)

    own_starts = after(own_starts, balanced_in).reshape(rows)
    local = here * rows + jnp.arange(rows, dtype=jnp.int32) - own_starts
    cosine, sine = rope_tables(local.astype(F32))

    normed_one, *cut = project(spot, balanced_in, gain_rows[0:1], weight_in, cosine, sine, spans)
    cuts = by_pair(cut)
    qkv = [trade(cuts[0])]
    pieces = trade([own_starts.reshape(1, rows)] * spans, normed_one)
    starts = in_order(pieces, here).reshape(group)
    late = after(cotangent, normed_one)
    arrived_late = exchange(place(target_slot, late, slots))
    upstream = pick(anchor_slot, arrived_late)
    own_rows = attention_out.shape[0]

    def cut_rest(rest):
        rest = rest.reshape(-1, straight.shape[0], width)
        return [rest[:, :own_rows].reshape(-1, width), rest[:, own_rows:].reshape(-1, width)]

    positions = jnp.arange(group, dtype=jnp.int32) - starts
    cosine_all, sine_all = rope_tables(positions.astype(F32))
    forward = [attend(spot, after(qkv[0], upstream, cosine_all, sine_all), starts)]
    upstream = regroup(upstream)
    side_rest = after(side_rest, forward[0])
    other_rest = swap(side_rest, "core", 1)
    side_rest = cut_rest(side_rest)
    for pieces in cuts[1:]:
        qkv.append(trade(after(pieces, qkv[0]), forward[0]))
        ready = after(qkv[-1], upstream, side_rest)
        forward.append(attend(spot, ready, starts))
    side_gate = gather_chips(line_gate_late, came=(normed_one, forward[-1]))
    other_rest = cut_rest(after(other_rest, forward[-1]))
    weight_out = (side_rest[0], other_rest[0])
    weight_down = halves_of(core_order(side_rest[1], other_rest[1]))
    traded = [trade(out[:spans]) for out in forward]
    side_gate = after(side_gate, traded)
    weight_gate = side_gate + [swap(half, "core", 1) for half in side_gate]
    (
        result_low,
        middle_grad,
        branch_grad,
        attended_mine,
        attended_other,
        gain_two_grad,
        *rest,
    ) = middle(
        spot,
        owners,
        spans,
        balanced_in,
        upstream,
        gain_rows[1:2],
        weight_out,
        joined(traded),
        weight_gate,
        weight_down,
    )
    gate_kept, gate_sent, down_grad, grad_cut = rest[:2], rest[2:4], rest[4:6], rest[6:]
    grad_heads = trade(grad_cut)
    grads = [attend_back(spot, 0, qkv[0], starts, grad_heads, *forward[0][spans:], cosine_all, sine_all)]
    gate_both = core_sum(gate_kept, gate_sent, grads[0])
    down_both = core_sum(*zip(*(row_parts(half) for half in down_grad)), grads[0])
    grad_heads = after(grad_heads, gate_both, down_both)
    down_line = chips_scatter(down_both)
    gate_line = chips_scatter(gate_both)
    grads += [
        attend_back(spot, p, qkv[p], starts, grad_heads, *forward[p][spans:], cosine_all, sine_all)
        for p in range(1, pairs)
    ]
    result_slots = place(anchor_slot, after(regroup(result_low, grads[0]), grads[-1]), slots)
    outputs = exchange(result_slots)
    attended_mine, attended_other, branch_grad = after(
        (attended_mine, attended_other, branch_grad), grads[-1]
    )
    out_kept = outer(attended_mine, branch_grad).astype(BF16)
    out_sent = outer(attended_other, branch_grad).astype(BF16)
    middle_grad = after(middle_grad, result_slots, out_kept, out_sent, down_line)
    sent_a, sent_b, kept_a, kept_b, input_low, gains_kept, gains_sent = last(
        spot,
        owners,
        spans,
        balanced_in,
        middle_grad,
        gain_rows[0:1],
        gain_two_grad,
        normed_one,
        weight_in,
        joined(trade(pieces, grads[-1]) for pieces in grads),
    )
    gate_shard = line_scatter(gate_line)
    down_shard = line_scatter(after(down_line, gate_shard))
    in_both = core_sum(
        [kept_a, kept_b, out_kept, gains_kept], [sent_a, sent_b, out_sent, gains_sent]
    )
    in_both = after(in_both, gate_line)
    in_line = chips_sum(in_both)
    outputs = pick(target_slot, after(outputs, in_both))
    shards = line_sum(in_line)
    in_shard, out_shard = shards[:, : 3 * width], shards[:, 3 * width : 4 * width]
    chosen = jnp.eye(2, LANES, dtype=F32)
    gain_shard = lax.dot_general(
        chosen,
        shards[:, 4 * width :],
        (((1,), (1,)), ((), ())),
        precision=lax.Precision.HIGHEST,
        preferred_element_type=F32,
    )
    returned = exchange(place(anchor_slot, regroup(input_low, in_line), slots))
    input_gradient = pick(target_slot, returned)
    local_total = (
        jnp.sum(in_shard * in_shard)
        + jnp.sum(out_shard * out_shard)
        + jnp.sum(gate_shard * gate_shard)
        + jnp.sum(down_shard * down_shard)
        + jnp.sum(gain_shard * gain_shard)
    )
    total = jnp.sum(spread(jnp.broadcast_to(local_total, (8, LANES)), ROWS).reshape(-1, 8, LANES)[:, 0, 0])
    gradient_norm = jnp.sqrt(total)
    factor = CLIP / jnp.maximum(gradient_norm, CLIP)
    updates = []
    for weight, gradient, first, second, rate in (
        (attention_in, in_shard, first_in, second_in, D ** (-0.5)),
        (attention_out, out_shard, first_out, second_out, 0.5),
        (gate_up, gate_shard, first_gate, second_gate, D ** (-0.5)),
        (feed_down, down_shard, first_down, second_down, 2.0 * FF ** (-0.5)),
        (norm_gains, gain_shard, first_gains, second_gains, 1.5),
    ):
        updates.extend(adamw(weight, gradient, first, second, rate, factor))
    return (outputs, input_gradient, gradient_norm, *updates)


def solution(mesh):
    owners, spans = mesh.shape["dp"], mesh.shape["seq"]
    parts = Mesh(mesh.devices.reshape(owners // 2, 2, spans), ROWS)
    rows = P(ROWS, None)
    columns = P(None, ROWS)
    line = P(ROWS)
    in_specs = (rows, rows, line, line, line) + ((rows,) * 4 + (columns,)) * 3
    out_specs = (rows, rows, P()) + (rows,) * 12 + (columns,) * 3
    return jax.shard_map(
        per_device, mesh=parts, in_specs=in_specs, out_specs=out_specs, check_vma=False
    )
```

```python
import functools

import jax
import jax.numpy as jnp
from jax import lax
from jax.experimental import pallas as pl
from jax.experimental.pallas import tpu as pltpu
from jax.sharding import Mesh
from jax.sharding import PartitionSpec as P

D = 1024
HEAD = 64
FF = 2816
STEP = 10
LANES = 128

EPSILON = 1e-05
THETA = 500000.0
NEGATIVE = -1e30
BETA_FIRST = 0.9
BETA_SECOND = 0.95
ADAM_EPSILON = 1e-08
DECAY = 0.1
CLIP = 1.0
SCALE = 0.125
VMEM = 56 * 1024 * 1024
F32 = jnp.float32
BF16 = jnp.bfloat16
ROWS = ("chip", "core", "seq")


def norm_rows(values, gain_row):
    inverse = lax.rsqrt(jnp.mean(values * values, axis=1, keepdims=True) + EPSILON)
    normal = values * inverse
    return (normal * gain_row[None, :], normal, inverse)


def norm_back(upstream, normal, inverse, gain_row):
    gain_grad = jnp.sum(upstream * normal, axis=0)
    scaled = upstream * gain_row[None, :]
    return (
        inverse * (scaled - normal * jnp.mean(scaled * normal, axis=1, keepdims=True)),
        gain_grad,
    )


def rope_tables(positions):
    half_size = HEAD // 2
    frequency = jnp.power(THETA, -2.0 * jnp.arange(half_size, dtype=F32) / HEAD)
    angles = positions[:, None] * frequency[None, :]
    cosine = jnp.cos(angles)
    sine = jnp.sin(angles)
    return (
        jnp.concatenate([cosine] * 4, axis=1),
        jnp.concatenate([-sine, sine, -sine, sine], axis=1),
    )


def swap_halves(values):
    lane = lax.broadcasted_iota(jnp.int32, values.shape, 1)
    left = pltpu.roll(values, LANES - HEAD // 2, 1)
    right = pltpu.roll(values, HEAD // 2, 1)
    return jnp.where(lane % HEAD < HEAD // 2, left, right)


def contract_last(left, right):
    return lax.dot_general(left, right, (((1,), (1,)), ((), ())), preferred_element_type=F32)


def params():
    return pltpu.CompilerParams(vmem_limit_bytes=VMEM)


def turned(values):
    return values.astype(F32).T.astype(BF16)


def rows_at(index, count):
    return pl.ds(pl.multiple_of(index * count, count), count)


def project_kernel(spans, half, place_ref, x_ref, gain_ref, wa_ref, wb_ref, cos_ref, sin_ref, h_ref, *outs):
    step = pl.program_id(0)
    hw = wa_ref.shape[1] // 2

    @pl.when(step == 0)
    def _():
        x = x_ref[...].astype(F32)
        inverse = lax.rsqrt(jnp.mean(x * x, axis=1, keepdims=True) + EPSILON)
        h_ref[...] = (x * inverse * gain_ref[...]).astype(BF16)

    def work(w_ref, rotated):
        acc = jnp.dot(h_ref[...], w_ref[...], preferred_element_type=F32)
        if rotated:
            pieces = []
            for c in range(2 * hw // LANES):
                part = acc[:, c * LANES : (c + 1) * LANES]
                pieces.append(part * cos_ref[...] + swap_halves(part) * sin_ref[...])
            acc = jnp.concatenate(pieces, axis=1)
        low = acc.astype(BF16)
        for side in range(2):
            for k in range(spans):

                @pl.when(((2 * step + side) % spans) ^ place_ref[0] == k)
                def _(k=k, side=side):
                    for pair in range(hw // LANES):
                        lo = side * hw + pair * LANES
                        outs[pair * spans + k][...] = low[:, lo : lo + LANES]

    turning = step < spans
    pl.when(step < half)(lambda: work(wa_ref, True))
    pl.when((step >= half) & turning)(lambda: work(wb_ref, True))
    pl.when(jnp.logical_not(turning))(lambda: work(wb_ref, False))


def project(spot, x, gain_row, weights, cosine, sine, spans):
    rows, width = x.shape
    hw = width // spans
    half = 3 * spans // 4
    fixed = lambda t, p: (0, 0)
    return pl.pallas_call(
        functools.partial(project_kernel, spans, half),
        grid_spec=pltpu.PrefetchScalarGridSpec(
            num_scalar_prefetch=1,
            grid=(3 * spans // 2,),
            in_specs=[
                pl.BlockSpec((rows, width), fixed),
                pl.BlockSpec((1, width), fixed),
                pl.BlockSpec((width, 2 * hw), lambda t, p: (0, jnp.minimum(t, half - 1))),
                pl.BlockSpec((width, 2 * hw), lambda t, p: (0, jnp.maximum(t - half, 0))),
                pl.BlockSpec((rows, LANES), fixed),
                pl.BlockSpec((rows, LANES), fixed),
            ],
            out_specs=[pl.BlockSpec((rows, width), fixed)]
            + [pl.BlockSpec((rows, LANES), lambda t, p: (0, 2 * t // spans))] * (width // LANES),
        ),
        out_shape=[jax.ShapeDtypeStruct((rows, width), BF16)]
        + [jax.ShapeDtypeStruct((rows, 3 * LANES), BF16)] * (width // LANES),
        compiler_params=params(),
        cost_estimate=pl.CostEstimate(
            flops=17250000000, bytes_accessed=0, transcendentals=0
        ),
        name="project",
    )(spot, x, gain_row, *weights, cosine, sine)


def attend_kernel(spans, place_ref, start_ref, *refs):
    pieces, refs = refs[: 3 * spans], refs[3 * spans :]
    lows, (out_ref, log_ref, q_scr, k_scr, v_scr) = refs[:spans], refs[spans:]
    block = q_scr.shape[0] // spans
    here = place_ref[0]
    relative = pl.program_id(0)
    i = relative ^ here
    lane = lax.broadcasted_iota(jnp.int32, (block, LANES), 1)
    first = lane < HEAD

    @pl.when(relative == 0)
    def _():
        for k in range(spans):
            at = rows_at(here ^ k, block)
            q_scr[k * block : (k + 1) * block, :] = pieces[k][...]
            k_scr[at, :] = pieces[spans + k][...]
            v_scr[:, at] = turned(pieces[2 * spans + k][...])

    q_pair = q_scr[rows_at(relative, block), :] * SCALE
    key = lax.broadcasted_iota(jnp.int32, (block, block), 0)
    query = lax.broadcasted_iota(jnp.int32, (block, block), 1)
    starts = start_ref[:, rows_at(i, block)]
    heads = []
    for head in range(2):
        mine = first if head == 0 else jnp.logical_not(first)
        heads.append(jnp.where(mine, q_pair, jnp.zeros_like(q_pair)))

    def visit(j, carry, diagonal):
        at = rows_at(j, block)
        k = k_scr[at, :]
        seen = key + j * block >= starts
        if diagonal:
            seen = seen & (key <= query)
        result = []
        for head in range(2):
            s = jnp.where(seen, contract_last(k, heads[head]), NEGATIVE)
            lines = slice(head * HEAD, (head + 1) * HEAD)
            new = jnp.max(s, axis=0, keepdims=True)
            if not diagonal:
                top, total, acc = carry[head]
                new = jnp.maximum(top, new)
            p = jnp.exp(s - new)
            added = jnp.sum(p, axis=0, keepdims=True)
            weighed = jnp.dot(v_scr[lines, at], p.astype(BF16), preferred_element_type=F32)
            if not diagonal:
                factor = jnp.exp(top - new)
                added = added + total * factor
                weighed = weighed + acc * factor
            result.append((new, added, weighed))
        return tuple(result)

    carry = visit(i, None, True)
    carry = lax.fori_loop(0, i, lambda j, c: visit(j, c, False), carry)
    parts = []
    for head in range(2):
        top, total, acc = carry[head]
        parts.append(acc / total)
        log_ref[head : head + 1, :] = top + jnp.log(total)
    out = jnp.concatenate(parts, axis=0).T
    out_ref[0] = out
    low = out.astype(BF16)
    for k in range(spans):

        @pl.when(relative == k)
        def _(k=k):
            lows[k][...] = low


def piece_specs(rows, spans):
    return [
        pl.BlockSpec((rows, LANES), functools.partial(lambda part, i, s: (0, part), part))
        for part in range(3)
        for _ in range(spans)
    ]


def attend(spot, qkv, starts):
    spans = len(qkv)
    rows = qkv[0].shape[0]
    group = rows * spans
    return pl.pallas_call(
        functools.partial(attend_kernel, spans),
        grid_spec=pltpu.PrefetchScalarGridSpec(
            num_scalar_prefetch=1,
            grid=(spans,),
            in_specs=[pl.BlockSpec((1, group), lambda i, s: (0, 0))] + piece_specs(rows, spans),
            out_specs=[pl.BlockSpec((rows, LANES), lambda i, s: (0, 0))] * spans
            + [
                pl.BlockSpec((1, rows, LANES), lambda i, s: (i, 0, 0)),
                pl.BlockSpec((8, rows), lambda i, s: (0, i ^ s[0])),
            ],
            scratch_shapes=[
                pltpu.VMEM((group, LANES), BF16),
                pltpu.VMEM((group, LANES), BF16),
                pltpu.VMEM((LANES, group), BF16),
            ],
        ),
        out_shape=[jax.ShapeDtypeStruct((rows, LANES), BF16)] * spans
        + [
            jax.ShapeDtypeStruct((spans, rows, LANES), F32),
            jax.ShapeDtypeStruct((8, group), F32),
        ],
        compiler_params=params(),
        cost_estimate=pl.CostEstimate(
            flops=18400000000, bytes_accessed=0, transcendentals=0
        ),
        name="attend",
    )(spot, starts.reshape(1, group), *(list(qkv) * 3))


def attend_back_kernel(spans, place_ref, start_ref, *refs):
    pieces, refs = refs[: 3 * spans], refs[3 * spans :]
    grads, refs = refs[:spans], refs[spans:]
    (out_ref, log_ref, cos_ref, sin_ref), refs = refs[:4], refs[4:]
    outs, refs = refs[:spans], refs[spans:]
    q_scr, k_scr, v_scr, do_scr, dq_scr, dk_scr, dv_scr, delta_ref, turned_ref = refs
    block = q_scr.shape[0] // spans
    here = place_ref[0]
    j = pl.program_id(0)
    lane = lax.broadcasted_iota(jnp.int32, (block, LANES), 1)
    first = lane < HEAD

    @pl.when(j == 0)
    def _():
        for k in range(spans):
            at = rows_at(here ^ k, block)
            q_scr[at, :] = pieces[k][...]
            k_scr[at, :] = pieces[spans + k][...]
            v_scr[at, :] = pieces[2 * spans + k][...]
            do = grads[k][...]
            do_scr[at, :] = do
            product = (do.astype(F32) * out_ref[k]).T
            delta_ref[0:1, at] = jnp.sum(product[:HEAD], axis=0, keepdims=True)
            delta_ref[1:2, at] = jnp.sum(product[HEAD:], axis=0, keepdims=True)
        turned_ref[...] = jnp.zeros_like(turned_ref)

    now = rows_at(j, block)
    k_pair = k_scr[now, :]
    v_pair = v_scr[now, :]
    k_turned = turned(k_pair)
    key = j * block + lax.broadcasted_iota(jnp.int32, (block, block), 0)
    query = lax.broadcasted_iota(jnp.int32, (block, block), 1)

    def visit(i, carry, diagonal):
        dk, dv = carry
        at = rows_at(i, block)
        q_pair = q_scr[at, :] * SCALE
        do_pair = do_scr[at, :]
        seen = key >= start_ref[:, at]
        if diagonal:
            seen = seen & (key <= query + i * block)
        for head in range(2):
            mine = first if head == 0 else jnp.logical_not(first)
            q = jnp.where(mine, q_pair, jnp.zeros_like(q_pair))
            do = jnp.where(mine, do_pair, jnp.zeros_like(do_pair))
            s = jnp.where(seen, contract_last(k_pair, q), NEGATIVE)
            p = jnp.exp(s - log_ref[head : head + 1, at])
            dp = contract_last(v_pair, do)
            ds = (p * (dp - delta_ref[head : head + 1, at])).astype(BF16)
            dv = dv + jnp.dot(p.astype(BF16), do, preferred_element_type=F32)
            dk = dk + jnp.dot(ds, q, preferred_element_type=F32)
            lines = slice(head * HEAD, (head + 1) * HEAD)
            turned_ref[lines, at] += jnp.dot(k_turned[lines], ds, preferred_element_type=F32)
        return (dk, dv)

    zero = jnp.zeros((block, LANES), F32)
    carry = visit(j, (zero, zero), True)
    dk, dv = lax.fori_loop(j + 1, spans, lambda i, c: visit(i, c, False), carry)

    def turn_back(values, at):
        return values * cos_ref[at, :] + swap_halves(values * sin_ref[at, :])

    dk_scr[now, :] = turn_back(dk, now).astype(BF16)
    dv_scr[now, :] = dv.astype(BF16)

    @pl.when(j == spans - 1)
    def _():
        def finish(i, carry):
            at = rows_at(i, block)
            dq_scr[at, :] = turn_back(turned_ref[:, at].T * SCALE, at).astype(BF16)
            return carry

        lax.fori_loop(0, spans, finish, 0)
        for k in range(spans):
            at = rows_at(here ^ k, block)
            for part, scr in enumerate((dq_scr, dk_scr, dv_scr)):
                outs[k][:, part * LANES : (part + 1) * LANES] = scr[at, :]


def attend_back(spot, pair, qkv, starts, grads, out, logs, cosine, sine):
    spans = len(qkv)
    rows = qkv[0].shape[0]
    group = rows * spans
    whole = lambda j, s: (0, 0)
    low = pltpu.VMEM((group, LANES), BF16)
    return pl.pallas_call(
        functools.partial(attend_back_kernel, spans),
        grid_spec=pltpu.PrefetchScalarGridSpec(
            num_scalar_prefetch=1,
            grid=(spans,),
            in_specs=[pl.BlockSpec((1, group), whole)]
            + piece_specs(rows, spans)
            + [pl.BlockSpec((rows, LANES), lambda j, s: (0, pair))] * spans
            + [
                pl.BlockSpec((spans, rows, LANES), lambda j, s: (0, 0, 0)),
                pl.BlockSpec((8, group), whole),
                pl.BlockSpec((group, LANES), whole),
                pl.BlockSpec((group, LANES), whole),
            ],
            out_specs=[pl.BlockSpec((rows, 3 * LANES), whole)] * spans,
            scratch_shapes=[low] * 7 + [pltpu.VMEM((8, group), F32), pltpu.VMEM((LANES, group), F32)],
        ),
        out_shape=[jax.ShapeDtypeStruct((rows, 3 * LANES), BF16)] * spans,
        compiler_params=params(),
        cost_estimate=pl.CostEstimate(
            flops=27600000000, bytes_accessed=0, transcendentals=0
        ),
        name="attend_back",
    )(spot, starts.reshape(1, group), *(list(qkv) * 3), *grads, out, logs, cosine, sine)


def core_split(values, block, own):
    width = values.shape[1]
    sides = []
    for core in range(2):
        blocks = [values[:, b * block : (b + 1) * block] for b in range(core, width // block, 2)]
        sides.append(jnp.concatenate(blocks, axis=1))
    return (jnp.where(own == 0, sides[0], sides[1]), jnp.where(own == 0, sides[1], sides[0]))


def core_merge(mine, other, block, own):
    sides = (jnp.where(own == 0, mine, other), jnp.where(own == 0, other, mine))
    blocks = mine.shape[1] // block
    return jnp.concatenate(
        [side[:, b * block : (b + 1) * block] for b in range(blocks) for side in sides], axis=1
    )


def middle_kernel(spans, block, place_ref, x_ref, dy_ref, gain_ref, om_ref, oo_ref, *refs):
    heads = x_ref.shape[1] // LANES
    attended, refs = refs[:heads], refs[heads:]
    (gm_ref, um_ref, go_ref, uo_ref, da_ref, db_ref), refs = refs[:6], refs[6:]
    (y_ref, dx_ref, branch_ref, ow_ref, ox_ref, gain_grad_ref), refs = refs[:6], refs[6:]
    (gk_ref, uk_ref, gs_ref, us_ref, ga_ref, gb_ref), refs = refs[:6], refs[6:]
    grads, refs = refs[:spans], refs[spans:]
    hm_scr, ho_scr, kept_scr, sent_scr, x2_scr, y_scr, dm_scr, do_scr, wide_scr = refs
    step, steps = pl.program_id(0), pl.num_programs(0)
    half = x_ref.shape[1] // 2
    here, core = place_ref[0], place_ref[1]

    def pieces_at(pieces):
        for index, piece in enumerate(pieces):
            pair, k = index // spans, index % spans
            yield rows_at((here ^ k) * (heads // spans) + pair, LANES), piece

    hw = x_ref.shape[1] // spans

    def normal():
        x2 = x2_scr[...]
        inverse = lax.rsqrt(jnp.mean(x2 * x2, axis=1, keepdims=True) + EPSILON)
        return (x2 * inverse, inverse)

    @pl.when(step == 0)
    def _():
        for at, piece in pieces_at(attended):
            wide_scr[:, at] = piece[...]
        mine, other = core_split(wide_scr[...], block, core)
        ow_ref[...] = mine
        ox_ref[...] = other
        x2_scr[...] = (
            x_ref[...].astype(F32)
            + jnp.dot(mine, om_ref[...], preferred_element_type=F32)
            + jnp.dot(other, oo_ref[...], preferred_element_type=F32)
        )
        h = (normal()[0] * gain_ref[...]).astype(BF16).astype(F32)
        mine, other = core_split(h, block, core)
        hm_scr[...] = mine.astype(BF16)
        ho_scr[...] = other.astype(BF16)
        kept_scr[...] = mine.T.astype(BF16)
        sent_scr[...] = other.T.astype(BF16)
        y_scr[...] = jnp.zeros_like(y_scr)
        dm_scr[...] = jnp.zeros_like(dm_scr)
        do_scr[...] = jnp.zeros_like(do_scr)

    hm, ho, dy = hm_scr[...], ho_scr[...], dy_ref[...]
    gm, um, go, uo = gm_ref[...], um_ref[...], go_ref[...], uo_ref[...]
    gate = jnp.dot(hm, gm, preferred_element_type=F32) + jnp.dot(ho, go, preferred_element_type=F32)
    up = jnp.dot(hm, um, preferred_element_type=F32) + jnp.dot(ho, uo, preferred_element_type=F32)
    share = jax.nn.sigmoid(gate)
    active = gate * share
    hidden_full = active * up
    hidden = hidden_full.astype(BF16)
    down = jnp.concatenate([da_ref[...], db_ref[...]], axis=1)
    y_scr[...] += jnp.dot(hidden, down, preferred_element_type=F32)
    dhid = contract_last(dy, down)
    dgate = (dhid * up * share * (1.0 + gate * (1.0 - share))).astype(BF16)
    dup = (dhid * active).astype(BF16)
    dm_scr[...] += contract_last(dgate, gm) + contract_last(dup, um)
    do_scr[...] += contract_last(dgate, go) + contract_last(dup, uo)
    kept, sent = kept_scr[...], sent_scr[...]
    gs_ref[...] = jnp.dot(sent, dgate, preferred_element_type=F32).astype(BF16)
    us_ref[...] = jnp.dot(sent, dup, preferred_element_type=F32).astype(BF16)
    gk_ref[...] = jnp.dot(kept, dgate, preferred_element_type=F32).astype(BF16)
    uk_ref[...] = jnp.dot(kept, dup, preferred_element_type=F32).astype(BF16)
    hidden_turned = hidden_full.T.astype(BF16)
    ga_ref[...] = jnp.dot(hidden_turned, dy[:, :half], preferred_element_type=F32).astype(BF16)
    gb_ref[...] = jnp.dot(hidden_turned, dy[:, half:], preferred_element_type=F32).astype(BF16)

    @pl.when(step == steps - 1)
    def _():
        y_ref[...] = (x2_scr[...] + y_scr[...]).astype(BF16)
        norm, inverse = normal()
        dh = core_merge(dm_scr[...], do_scr[...], block, core)
        gain_grad_ref[...] = jnp.sum(dh * norm, axis=0, keepdims=True)
        scaled = dh * gain_ref[...]
        inner = jnp.mean(scaled * norm, axis=1, keepdims=True)
        dx = dy_ref[...].astype(F32) + inverse * (scaled - norm * inner)
        dx_ref[...] = dx
        branch = dx.astype(BF16)
        branch_ref[...] = branch
        mine = contract_last(branch, om_ref[...]).astype(BF16)
        other = contract_last(branch, oo_ref[...]).astype(BF16)
        wide_scr[...] = core_merge(mine, other, block, core)
        for k in range(spans):
            grads[k][...] = wide_scr[:, rows_at(here ^ k, hw)]


def middle(spot, owners, spans, x, dy, gain_row, weight_out, attended, weight_gate, weight_down):
    rows, width = x.shape
    hidden = weight_gate[0].shape[1]
    heads, half, tile = width // LANES, width // 2, 2 * LANES
    tiles = hidden // tile
    fixed = lambda t, s: (0, 0)
    full = pl.BlockSpec((rows, width), fixed)
    side = pl.BlockSpec((rows, half), fixed)
    across = lambda t, s: (0, t)
    along = lambda t, s: (t, 0)
    shape = jax.ShapeDtypeStruct
    return pl.pallas_call(
        functools.partial(middle_kernel, spans, width // owners),
        grid_spec=pltpu.PrefetchScalarGridSpec(
            num_scalar_prefetch=1,
            grid=(tiles,),
            in_specs=[full, full, pl.BlockSpec((1, width), fixed)]
            + [pl.BlockSpec((half, width), fixed)] * 2
            + [pl.BlockSpec((rows, LANES), fixed)] * heads
            + [pl.BlockSpec((half, tile), across)] * 4
            + [pl.BlockSpec((tile, half), along)] * 2,
            out_specs=[full] * 3
            + [side] * 2
            + [pl.BlockSpec((1, width), fixed)]
            + [pl.BlockSpec((half, tile), across)] * 4
            + [pl.BlockSpec((tile, half), along)] * 2
            + [pl.BlockSpec((rows, width // spans), fixed)] * spans,
            scratch_shapes=[
                pltpu.VMEM((rows, half), BF16),
                pltpu.VMEM((rows, half), BF16),
                pltpu.VMEM((half, rows), BF16),
                pltpu.VMEM((half, rows), BF16),
                pltpu.VMEM((rows, width), F32),
                pltpu.VMEM((rows, width), F32),
                pltpu.VMEM((rows, half), F32),
                pltpu.VMEM((rows, half), F32),
                pltpu.VMEM((rows, width), BF16),
            ],
        ),
        out_shape=[
            shape((rows, width), BF16),
            shape((rows, width), F32),
            shape((rows, width), BF16),
            shape((rows, half), BF16),
            shape((rows, half), BF16),
            shape((1, width), F32),
        ]
        + [shape((half, hidden), BF16)] * 4
        + [shape((hidden, half), BF16)] * 2
        + [shape((rows, width // spans), BF16)] * spans,
        compiler_params=params(),
        cost_estimate=pl.CostEstimate(
            flops=55200000000, bytes_accessed=0, transcendentals=0
        ),
        name="middle",
    )(
        spot,
        x,
        dy,
        gain_row,
        *weight_out,
        *attended,
        *weight_gate,
        *weight_down,
    )


def last_kernel(spans, half, block, place_ref, x_ref, dx2_ref, gain_ref, second_ref, h_ref, wa_ref, wb_ref, *refs):
    heads = x_ref.shape[1] // LANES
    pieces, refs = refs[:heads], refs[heads:]
    sa_ref, sb_ref, ka_ref, kb_ref, dx_ref, gk_ref, gs_ref, d_scr, kept_scr, sent_scr, dh_scr = refs
    step = pl.program_id(0)

    @pl.when(step == 0)
    def _():
        kept, sent = core_split(h_ref[...].astype(F32), block, place_ref[1])
        kept_scr[...] = kept.T.astype(BF16)
        sent_scr[...] = sent.T.astype(BF16)
        dh_scr[...] = jnp.zeros_like(dh_scr)

    for side in range(2):
        for k in range(spans):

            @pl.when(((2 * step + side) % spans) ^ place_ref[0] == k)
            def _(k=k, side=side):
                for pair in range(heads // spans):
                    lo = side * (heads // spans) * LANES + pair * LANES
                    d_scr[:, lo : lo + LANES] = pieces[pair * spans + k][...]

    def work(w_ref, s_ref, k_ref):
        d = d_scr[...]
        s_ref[...] = jnp.dot(sent_scr[...], d, preferred_element_type=F32).astype(BF16)
        k_ref[...] = jnp.dot(kept_scr[...], d, preferred_element_type=F32).astype(BF16)
        dh_scr[...] += contract_last(d, w_ref[...])

    pl.when(step < half)(lambda: work(wa_ref, sa_ref, ka_ref))
    pl.when(step >= half)(lambda: work(wb_ref, sb_ref, kb_ref))

    @pl.when(step == pl.num_programs(0) - 1)
    def _():
        x = x_ref[...].astype(F32)
        inverse = lax.rsqrt(jnp.mean(x * x, axis=1, keepdims=True) + EPSILON)
        norm = x * inverse
        dh = dh_scr[...]
        row = lax.broadcasted_iota(jnp.int32, (LANES, x.shape[1]), 0)
        gains = jnp.where(row == 0, jnp.sum(dh * norm, axis=0, keepdims=True), 0.0)
        gains = jnp.where(row == 1, second_ref[...], gains)
        kept, sent = core_split(gains, block, place_ref[1])
        gk_ref[...] = kept.T.astype(BF16)
        gs_ref[...] = sent.T.astype(BF16)
        scaled = dh * gain_ref[...]
        inner = jnp.mean(scaled * norm, axis=1, keepdims=True)
        dx_ref[...] = (dx2_ref[...] + inverse * (scaled - norm * inner)).astype(BF16)


def last(spot, owners, spans, x, dx2, gain_row, gain_two_grad, normed, weights, pieces):
    rows, width = x.shape
    hw = 2 * width // spans
    half = 3 * spans // 4
    low = lambda t, s: (0, jnp.minimum(t, half - 1))
    high = lambda t, s: (0, jnp.maximum(t - half, 0))
    fixed = lambda t, s: (0, 0)
    full = pl.BlockSpec((rows, width), fixed)
    row = pl.BlockSpec((1, width), fixed)
    shape = jax.ShapeDtypeStruct
    return pl.pallas_call(
        functools.partial(last_kernel, spans, half, width // owners),
        grid_spec=pltpu.PrefetchScalarGridSpec(
            num_scalar_prefetch=1,
            grid=(3 * spans // 2,),
            in_specs=[full, full, row, row, full]
            + [pl.BlockSpec((width, hw), low), pl.BlockSpec((width, hw), high)]
            + [pl.BlockSpec((rows, LANES), lambda t, s: (0, 2 * t // spans))] * len(pieces),
            out_specs=[
                pl.BlockSpec((width // 2, hw), low),
                pl.BlockSpec((width // 2, hw), high),
                pl.BlockSpec((width // 2, hw), low),
                pl.BlockSpec((width // 2, hw), high),
                full,
                pl.BlockSpec((width // 2, LANES), fixed),
                pl.BlockSpec((width // 2, LANES), fixed),
            ],
            scratch_shapes=[
                pltpu.VMEM((rows, hw), BF16),
                pltpu.VMEM((width // 2, rows), BF16),
                pltpu.VMEM((width // 2, rows), BF16),
                pltpu.VMEM((rows, width), F32),
            ],
        ),
        out_shape=[shape((width // 2, 3 * width // 2), BF16)] * 4
        + [shape((rows, width), BF16)]
        + [shape((width // 2, LANES), BF16)] * 2,
        compiler_params=params(),
        cost_estimate=pl.CostEstimate(
            flops=21850000000, bytes_accessed=0, transcendentals=0
        ),
        name="last",
    )(spot, x, dx2, gain_row, gain_two_grad, normed, *weights, *pieces)


def adamw(weight, gradient, first, second, rate, factor):
    clipped = gradient * factor
    first_new = BETA_FIRST * first + (1.0 - BETA_FIRST) * clipped
    second_new = BETA_SECOND * second + (1.0 - BETA_SECOND) * clipped * clipped
    corrected_first = first_new / (1.0 - BETA_FIRST**STEP)
    corrected_second = second_new / (1.0 - BETA_SECOND**STEP)
    weight_new = weight - rate * (
        corrected_first / (jnp.sqrt(corrected_second) + ADAM_EPSILON) + DECAY * weight
    )
    return (first_new, second_new, weight_new)


def swap(values, axis, step):
    count = lax.axis_size(axis)
    return lax.ppermute(values, axis, [(i, i ^ step) for i in range(count)])


def paired():
    return lax.axis_size("seq") == 4


def group_place():
    if paired():
        return 2 * lax.axis_index("core") + lax.axis_index("seq") % 2
    return lax.axis_index("seq")


def group_swap(values, step):
    if not paired():
        return swap(values, "seq", step)
    spans = lax.axis_size("seq")
    pairs = [
        (c * spans + z, (c ^ (step >> 1)) * spans + (z ^ (step & 1)))
        for c in range(2)
        for z in range(spans)
    ]
    return lax.ppermute(values, ("core", "seq"), pairs)


def regroup(values, *gates):
    if not paired():
        return values
    spans = lax.axis_size("seq")
    pairs = [
        (c * spans + z, (z // 2) * spans + 2 * c + z % 2)
        for c in range(2)
        for z in range(spans)
        if c != z // 2
    ]
    stays = lax.axis_index("core") == lax.axis_index("seq") // 2
    came = after(lax.ppermute(values, ("core", "seq"), pairs), gates)
    return jnp.where(stays, values, came)


def trade(pieces, *gates):
    return [pieces[0], *after([group_swap(pieces[k], k) for k in range(1, len(pieces))], gates)]


def bit_of(axis, step):
    return lax.axis_index(axis) & step


def ordered(own_bit, mine, other, at):
    return jnp.where(own_bit == 0, jnp.stack([mine, other], at), jnp.stack([other, mine], at))


def in_order(pieces, here):
    count = len(pieces)
    bits = count.bit_length() - 1
    stack = jnp.stack(pieces).reshape((2,) * bits + pieces[0].shape)
    for at in range(bits):
        flipped = jnp.flip(stack, axis=at)
        stack = jnp.where((here >> (bits - 1 - at)) & 1 == 1, flipped, stack)
    return stack.reshape((count,) + pieces[0].shape)


def chip_bits():
    count = lax.axis_size("chip")
    bits = [b for b in range(count.bit_length() - 1)]
    return bits, bits[::-1]


def halves_of(values):
    middle = values.shape[-1] // 2
    return (values[..., :middle], values[..., middle:])


def spread(values, axes):
    count = 1
    for axis in axes:
        count *= lax.axis_size(axis)
    copies = jnp.broadcast_to(values[None], (count,) + values.shape)
    return lax.all_to_all(copies, axes, split_axis=0, concat_axis=0, tiled=True)


def gather_line(shard, *gates):
    spans = lax.axis_size("seq")
    pieces = [shard] + [swap(shard, "seq", k) for k in range(1, spans)]
    pieces = after(pieces, gates)
    return in_order(pieces, lax.axis_index("seq")).reshape(-1, shard.shape[1])


def after(values, *tokens):
    return lax.optimization_barrier((values, tokens))[0]


def gather_chips(block, gate=None, came=()):
    parts, orders = halves_of(block), chip_bits()
    for at_step in range(len(orders[0])):
        if gate is not None and at_step == len(orders[0]) - 1:
            parts = after(parts, gate)
        others = [swap(half, "chip", 1 << order[at_step]) for half, order in zip(parts, orders)]
        if at_step < len(came):
            others = after(others, came[at_step])
        parts = [
            ordered(
                bit_of("chip", 1 << order[at_step]),
                half,
                other,
                sum(1 for d in order[:at_step] if d > order[at_step]),
            )
            for half, other, order in zip(parts, others, orders)
        ]
    return [half.reshape(-1, half.shape[-1]) for half in parts]


def core_order(mine, other):
    chips, width = lax.axis_size("chip"), mine.shape[1]
    mine, other = mine.reshape(chips, -1, width), other.reshape(chips, -1, width)
    return ordered(lax.axis_index("core"), mine, other, 1).reshape(-1, width)


def core_sum(kept, sent, *gates):
    came = after([swap(other, "core", 1) for other in sent], gates)
    parts = [
        (mine.astype(F32) + other.astype(F32)).astype(BF16) for mine, other in zip(kept, came)
    ]
    return jnp.concatenate(parts, axis=-1)


def chips_scatter(values):
    return lax.psum_scatter(values, "chip", scatter_dimension=0, tiled=True)


def line_scatter(values):
    return lax.psum_scatter(values, "seq", scatter_dimension=0, tiled=True).astype(F32)


def direct_sum(values, axis, *gates):
    count, here = lax.axis_size(axis), lax.axis_index(axis)
    total = lax.dynamic_index_in_dim(values, here, 0, keepdims=False).astype(F32)
    pieces = [
        swap(lax.dynamic_index_in_dim(values, here ^ k, 0, keepdims=False), axis, k)
        for k in range(1, count)
    ]
    for piece in after(pieces, gates):
        total = total + piece.astype(F32)
    return total


def line_sum(values):
    spans = lax.axis_size("seq")
    return direct_sum(values.reshape(spans, -1, values.shape[-1]), "seq")


def chips_sum(values, *gates):
    chips = lax.axis_size("chip")
    return direct_sum(values.reshape(chips, -1, values.shape[-1]), "chip", *gates).astype(BF16)


def outer(left, right):
    return lax.dot_general(left, right, (((0,), (0,)), ((), ())), preferred_element_type=F32)


def row_parts(gradient):
    width = gradient.shape[1]
    chips = lax.axis_size("chip")
    parts = gradient.reshape(chips, 2, -1, width)
    own = lax.axis_index("core") == 0
    kept = jnp.where(own, parts[:, 0], parts[:, 1]).reshape(-1, width)
    sent = jnp.where(own, parts[:, 1], parts[:, 0]).reshape(-1, width)
    return (kept, sent)


def place(index, values, slots):
    chosen = lax.broadcasted_iota(jnp.int32, (slots, index.shape[0]), 0) == index[None, :]
    return jnp.dot(chosen.astype(BF16), values, preferred_element_type=F32).astype(BF16)


def pick(index, values):
    slots = values.shape[0]
    chosen = lax.broadcasted_iota(jnp.int32, (index.shape[0], slots), 1) == index[:, None]
    return jnp.dot(chosen.astype(BF16), values, preferred_element_type=F32).astype(BF16)


def per_device(
    inputs,
    cotangent,
    target_slot,
    anchor_slot,
    sequence_start,
    attention_in,
    attention_out,
    gate_up,
    feed_down,
    norm_gains,
    first_in,
    first_out,
    first_gate,
    first_down,
    first_gains,
    second_in,
    second_out,
    second_gate,
    second_down,
    second_gains,
):
    owners = lax.axis_size("chip") * lax.axis_size("core")
    spans = lax.axis_size("seq")
    rows, width = inputs.shape
    per_owner = rows // owners
    capacity = per_owner + per_owner // 2
    slots = owners * capacity
    group = rows * spans
    here = group_place()
    device = (lax.axis_index("chip") * 2 + lax.axis_index("core")) * spans + lax.axis_index("seq")
    spot = jnp.stack([here, lax.axis_index("core")]).astype(jnp.int32)

    def exchange(values):
        return lax.all_to_all(values, ("chip", "core"), split_axis=0, concat_axis=0, tiled=True)

    pairs = width // spans // LANES

    def by_pair(pieces):
        return [pieces[p * spans : (p + 1) * spans] for p in range(pairs)]

    def joined(lists):
        return [piece for pieces in lists for piece in pieces]

    columns = norm_gains.shape[1]
    own_gains = jnp.pad(norm_gains.astype(BF16).reshape(1, -1), ((0, 7), (0, width - 2 * columns)))
    placed = jnp.concatenate(
        [
            place(target_slot, inputs, slots).reshape(owners, capacity, width),
            jnp.broadcast_to(own_gains[None], (owners, 8, width)),
        ],
        axis=1,
    )
    arrived = exchange(placed)
    gains_line = arrived[:, capacity, : 2 * columns]
    arrived = arrived[:, :capacity].reshape(slots, width)
    line_in = gather_line(attention_in.astype(BF16), placed)
    picked = pick(anchor_slot, arrived)
    balanced_in = regroup(picked)
    line_gate = gather_line(gate_up.astype(BF16), picked)
    side_in = gather_chips(line_in, gate=picked)
    line_gate_late = after(line_gate, side_in, balanced_in)
    core_in = after(side_in, line_gate)
    own_starts = regroup(sequence_start.reshape(1, rows), side_in)
    straight = jnp.concatenate([attention_out.astype(BF16), feed_down.astype(BF16)], axis=0)
    side_rest = lax.all_gather(after(straight, side_in), ("chip", "seq"), axis=0, tiled=True)
    weight_in = [core_order(half, swap(half, "core", 1)) for half in core_in]
    gains_line = after(gains_line.astype(F32), side_in)
    gain_pieces = [gains_line] + [swap(gains_line, "seq", k) for k in range(1, spans)]
    gain_rows = in_order(gain_pieces, lax.axis_index("seq")).reshape(spans, owners, 2, columns)
    gain_rows = jnp.transpose(gain_rows, (2, 1, 0, 3)).reshape(2, width)

    own_starts = after(own_starts, balanced_in).reshape(rows)
    local = here * rows + jnp.arange(rows, dtype=jnp.int32) - own_starts
    cosine, sine = rope_tables(local.astype(F32))

    normed_one, *cut = project(spot, balanced_in, gain_rows[0:1], weight_in, cosine, sine, spans)
    cuts = by_pair(cut)
    qkv = [trade(cuts[0])]
    pieces = trade([own_starts.reshape(1, rows)] * spans, normed_one)
    starts = in_order(pieces, here).reshape(group)
    late = after(cotangent, normed_one)
    arrived_late = exchange(place(target_slot, late, slots))
    upstream = pick(anchor_slot, arrived_late)
    own_rows = attention_out.shape[0]

    def cut_rest(rest):
        rest = rest.reshape(-1, straight.shape[0], width)
        return [rest[:, :own_rows].reshape(-1, width), rest[:, own_rows:].reshape(-1, width)]

    positions = jnp.arange(group, dtype=jnp.int32) - starts
    cosine_all, sine_all = rope_tables(positions.astype(F32))
    forward = [attend(spot, after(qkv[0], upstream, cosine_all, sine_all), starts)]
    upstream = regroup(upstream)
    side_rest = after(side_rest, forward[0])
    other_rest = swap(side_rest, "core", 1)
    side_rest = cut_rest(side_rest)
    for pieces in cuts[1:]:
        qkv.append(trade(after(pieces, qkv[0]), forward[0]))
        ready = after(qkv[-1], upstream, side_rest)
        forward.append(attend(spot, ready, starts))
    side_gate = gather_chips(line_gate_late, came=(normed_one, forward[-1]))
    other_rest = cut_rest(after(other_rest, forward[-1]))
    weight_out = (side_rest[0], other_rest[0])
    weight_down = halves_of(core_order(side_rest[1], other_rest[1]))
    traded = [trade(out[:spans]) for out in forward]
    side_gate = after(side_gate, traded)
    weight_gate = side_gate + [swap(half, "core", 1) for half in side_gate]
    (
        result_low,
        middle_grad,
        branch_grad,
        attended_mine,
        attended_other,
        gain_two_grad,
        *rest,
    ) = middle(
        spot,
        owners,
        spans,
        balanced_in,
        upstream,
        gain_rows[1:2],
        weight_out,
        joined(traded),
        weight_gate,
        weight_down,
    )
    gate_kept, gate_sent, down_grad, grad_cut = rest[:2], rest[2:4], rest[4:6], rest[6:]
    grad_heads = trade(grad_cut)
    grads = [attend_back(spot, 0, qkv[0], starts, grad_heads, *forward[0][spans:], cosine_all, sine_all)]
    gate_both = core_sum(gate_kept, gate_sent, grads[0])
    down_both = core_sum(*zip(*(row_parts(half) for half in down_grad)), grads[0])
    grad_heads = after(grad_heads, gate_both, down_both)
    down_line = chips_scatter(down_both)
    gate_line = chips_scatter(gate_both)
    grads += [
        attend_back(spot, p, qkv[p], starts, grad_heads, *forward[p][spans:], cosine_all, sine_all)
        for p in range(1, pairs)
    ]
    result_slots = place(anchor_slot, after(regroup(result_low, grads[0]), grads[-1]), slots)
    outputs = exchange(result_slots)
    attended_mine, attended_other, branch_grad = after(
        (attended_mine, attended_other, branch_grad), grads[-1]
    )
    out_kept = outer(attended_mine, branch_grad).astype(BF16)
    out_sent = outer(attended_other, branch_grad).astype(BF16)
    middle_grad = after(middle_grad, result_slots, out_kept, out_sent, down_line)
    sent_a, sent_b, kept_a, kept_b, input_low, gains_kept, gains_sent = last(
        spot,
        owners,
        spans,
        balanced_in,
        middle_grad,
        gain_rows[0:1],
        gain_two_grad,
        normed_one,
        weight_in,
        joined(trade(pieces, grads[-1]) for pieces in grads),
    )
    gate_shard = line_scatter(gate_line)
    down_shard = line_scatter(after(down_line, gate_shard))
    in_both = core_sum(
        [kept_a, kept_b, out_kept, gains_kept], [sent_a, sent_b, out_sent, gains_sent]
    )
    in_both = after(in_both, gate_line)
    in_line = chips_sum(in_both)
    outputs = pick(target_slot, after(outputs, in_both))
    shards = line_sum(in_line)
    in_shard, out_shard = shards[:, : 3 * width], shards[:, 3 * width : 4 * width]
    chosen = jnp.eye(2, LANES, dtype=F32)
    gain_shard = lax.dot_general(
        chosen,
        shards[:, 4 * width :],
        (((1,), (1,)), ((), ())),
        precision=lax.Precision.HIGHEST,
        preferred_element_type=F32,
    )
    returned = exchange(place(anchor_slot, regroup(input_low, in_line), slots))
    input_gradient = pick(target_slot, returned)
    local_total = (
        jnp.sum(in_shard * in_shard)
        + jnp.sum(out_shard * out_shard)
        + jnp.sum(gate_shard * gate_shard)
        + jnp.sum(down_shard * down_shard)
        + jnp.sum(gain_shard * gain_shard)
    )
    total = jnp.sum(spread(jnp.broadcast_to(local_total, (8, LANES)), ROWS).reshape(-1, 8, LANES)[:, 0, 0])
    gradient_norm = jnp.sqrt(total)
    factor = CLIP / jnp.maximum(gradient_norm, CLIP)
    updates = []
    for weight, gradient, first, second, rate in (
        (attention_in, in_shard, first_in, second_in, D ** (-0.5)),
        (attention_out, out_shard, first_out, second_out, 0.5),
        (gate_up, gate_shard, first_gate, second_gate, D ** (-0.5)),
        (feed_down, down_shard, first_down, second_down, 2.0 * FF ** (-0.5)),
        (norm_gains, gain_shard, first_gains, second_gains, 1.5),
    ):
        updates.extend(adamw(weight, gradient, first, second, rate, factor))
    return (outputs, input_gradient, gradient_norm, *updates)


def solution(mesh):
    owners, spans = mesh.shape["dp"], mesh.shape["seq"]
    parts = Mesh(mesh.devices.reshape(owners // 2, 2, spans), ROWS)
    rows = P(ROWS, None)
    columns = P(None, ROWS)
    line = P(ROWS)
    in_specs = (rows, rows, line, line, line) + ((rows,) * 4 + (columns,)) * 3
    out_specs = (rows, rows, P()) + (rows,) * 12 + (columns,) * 3
    return jax.shard_map(
        per_device, mesh=parts, in_specs=in_specs, out_specs=out_specs, check_vma=False
    )
```
